32 devices in a mesh: group: 8 (over z, core), blk: 4 (over y, x).
Axes of the slice: x: 2, y: 2, z: 4, core: 2. Of those that a mesh axis runs over, the one named last changes fastest.
Arguments:
- hamiltonian: bfloat16 [512, 6, 64, 256], P(('group', 'blk')), may hold values from -0.15625 to 0.15625
- block_columns: int32 [512, 6, 4], P(('group', 'blk')), may hold values from 0 to 15, as said below
- potential: float32 [32768], P(('group', 'blk')), may hold values from -1 to 1
- trial_slab: float32 [32768, 128], P(('group', 'blk')), may hold values from -40 to 40
Outputs:
- ortho_slab: float32 [32768, 128], P(('group', 'blk'))
- upper_factor: float32 [128, 128], replicated
The draws below stay inside these ranges and needn't reach their ends.
Inputs may be any that keep to these rules, and one draw needn't show every extreme that they name: `block_columns`: for each row block and each source, the 4 entries are distinct.
All inputs are finite; a program needn't handle non-finite values.
Results may differ from the reference program's by a relative error of at most 0.0021.
Values may be sent and summed in bfloat16 or wider, within the bound.
No kernel may reach another device: no remote copies, remote signals or barrier semaphores. Data moves between devices by JAX's collectives and lax.ppermute only.
A program may use at most 64 MiB of HBM per device.

```python
import math
import jax
import jax.numpy as jnp
from jax import lax

BS = 64
STATES = 128
NPD = 4
RB = 16
CYCLE = 4
GROUPS = 8
NSRC = 6
ROWB = 512
ROWS = 32768


def draw_block_columns(key, part):
    scores = jax.random.randint(key, (ROWB, NSRC, RB), 0, 1048576) * RB + jnp.arange(RB, dtype=jnp.int32)
    values, picked = lax.top_k(scores, NPD)
    return picked.astype(jnp.int32)


def draw_trial_slab(key, part):
    key_base, key_rows, key_cols = jax.random.split(jax.random.fold_in(key, 7), 3)
    row_scale = jnp.exp(jax.random.uniform(key_rows, (ROWB, 1, 1), jnp.float32, 0.0, math.log(10.0)))
    col_scale = jnp.exp(jax.random.uniform(key_cols, (1, 1, STATES), jnp.float32, 0.0, math.log(10.0)))
    base = jax.random.truncated_normal(key_base, -4.0, 4.0, (ROWB, BS, STATES), jnp.float32)
    return (0.1 * base * row_scale * col_scale).reshape(ROWS, STATES)


def steps_of(key, shape, shards, least, high):
    factor_of = 1.0
    for dim, blocks in shards:
        heights = jax.random.uniform(jax.random.fold_in(jax.random.fold_in(key, 6), dim), (blocks,), jnp.float32, least / len(shards), high / len(shards))
        factor_of = factor_of * jnp.repeat(jnp.exp(heights), shape[dim] // blocks).reshape((-1,) + (1,) * (len(shape) - 1 - dim))
    return factor_of


def scatter_about(stream_key, extent, deviation, bound, pieces=(), kind=jnp.bfloat16):
    array = deviation * jax.random.normal(stream_key, extent, jnp.float32)
    if pieces:
        array = array * steps_of(stream_key, extent, pieces, -0.22, 0.18)
    return jnp.clip(array, -bound, bound).astype(kind)


def setup_inputs(seed: int = 0) -> dict:
    splits = jax.random.split(jax.random.key(seed), 5)
    return {
        "hamiltonian": scatter_about(splits[0], (ROWB, NSRC, BS, NPD * BS), (NSRC * NPD * BS) ** -0.5, 0.15625, ((0, 32),)),
        "block_columns": draw_block_columns(jax.random.fold_in(splits[4], 71), 0),
        "potential": jnp.clip(jax.random.uniform(splits[2], (ROWS,), jnp.float32, -1.0, 1.0) * steps_of(splits[2], (ROWS,), ((0, 32),), -0.4, 0.0), -1.0, 1.0),
        "trial_slab": draw_trial_slab(jax.random.fold_in(splits[4], 71), 0),
    }


def pattern_index(block_columns):
    rows_index = jnp.arange(ROWB, dtype=jnp.int32)
    group_index = rows_index // (RB * CYCLE)
    inner_index = rows_index // RB % CYCLE
    own_base = (group_index[:, None] * CYCLE + jnp.arange(CYCLE, dtype=jnp.int32)[None, :]) * RB
    own_cols = own_base[:, :, None] + block_columns[:, :CYCLE, :]
    below_base = ((group_index - 1) * CYCLE + inner_index) * RB
    above_base = ((group_index + 1) * CYCLE + inner_index) * RB
    below_cols = jnp.where((group_index >= 1)[:, None], below_base[:, None] + block_columns[:, CYCLE, :], ROWB)
    above_cols = jnp.where((group_index < GROUPS - 1)[:, None], above_base[:, None] + block_columns[:, CYCLE + 1, :], ROWB)
    every = jnp.concatenate([own_cols, below_cols[:, None, :], above_cols[:, None, :]], axis=1)
    return every.astype(jnp.int32)

def coupled(hamiltonian, column_index, rounded):
    blocks = rounded.reshape(ROWB, BS, STATES)
    padded = jnp.concatenate([blocks, jnp.zeros((1, BS, STATES), jnp.bfloat16)], axis=0)
    ham_spans = hamiltonian.reshape(ROWB // RB, RB, NSRC, BS, NPD * BS)
    col_spans = column_index.reshape(ROWB // RB, RB, NSRC * NPD)

    def one_span(pair):
        ham_part, col_part = pair
        picked = padded[col_part].reshape(RB, NSRC, NPD * BS, STATES).astype(jnp.float32)
        return jnp.einsum('rsik,rskn->rin', ham_part.astype(jnp.float32), picked, precision=lax.Precision.HIGHEST)
    result = lax.map(one_span, (ham_spans, col_spans))
    return result.reshape(ROWS, STATES)

def reference(hamiltonian, block_columns, potential, trial_slab):
    column_index = pattern_index(block_columns)
    weights = potential[:, None]
    start_round = trial_slab.astype(jnp.bfloat16)
    filtered_once = 0.5 * (coupled(hamiltonian, column_index, start_round) + weights * trial_slab)
    once_round = filtered_once.astype(jnp.bfloat16)
    filtered = coupled(hamiltonian, column_index, once_round) + weights * filtered_once - trial_slab
    gram = jnp.dot(filtered.T, filtered, precision=lax.Precision.HIGHEST) / ROWS
    lower = jnp.linalg.cholesky(gram)
    ortho_slab = lax.linalg.triangular_solve(lower, filtered, left_side=False, lower=True, transpose_a=True)
    return (ortho_slab, jnp.transpose(lower))
```

```python
import functools

import jax
import jax.numpy as jnp
from jax import lax
from jax.experimental import pallas as pl
from jax.experimental.pallas import tpu as pltpu
from jax.sharding import PartitionSpec as P

precise = lax.Precision.HIGHEST
LANES = 128
SUB = 8
VMEM_LIMIT = 40 * 1024 * 1024
vmem = pl.BlockSpec(memory_space=pltpu.VMEM)
smem = pl.BlockSpec(memory_space=pltpu.SMEM)


def pair_exchange(value, offset):
    count = lax.axis_size("group")
    route = []
    for low in range(offset, count - 1, 2):
        route += [(low, low + 1), (low + 1, low)]
    return lax.ppermute(value, "group", route)


def potential_columns(potential_ref):
    return jnp.transpose(potential_ref[...])


def couple_row(place_ref, columns_ref, hamiltonian_ref, pieces, row, total):
    sources, per_source = hamiltonian_ref.shape[1], hamiltonian_ref.shape[3] // hamiltonian_ref.shape[2]
    for source, block_of in pieces:
        first = (row * sources + source) * per_source
        picked = jnp.concatenate(
            [block_of(columns_ref[first + slot]) for slot in range(per_source)], axis=0
        )
        product = jnp.dot(
            hamiltonian_ref[row, source], picked, preferred_element_type=jnp.float32
        )
        total = product if total is None else total + product
    return total


def all_pieces(place_ref, gathered_ref, inner_ref, outer_ref):
    cycle_size = gathered_ref.shape[0]
    odd = place_ref[0]
    pieces = [
        (source, functools.partial(lambda source, block: gathered_ref[source, block], source))
        for source in range(cycle_size)
    ]
    pieces.append((cycle_size + 1 - odd, lambda block: inner_ref[block]))
    pieces.append((cycle_size + odd, lambda block: outer_ref[block]))
    return pieces


def first_kernel(
    place_ref, columns_ref, hamiltonian_ref, gathered_ref, inner_ref, outer_ref,
    potential_ref, trial_ref, once_ref, round_ref,
):
    shard_blocks, _, block_size, _ = hamiltonian_ref.shape
    weights = potential_columns(potential_ref)
    pieces = all_pieces(place_ref, gathered_ref, inner_ref, outer_ref)
    per_column = LANES // block_size
    for row in range(shard_blocks):
        column, part = divmod(row, per_column)
        weight = weights[part * block_size : (part + 1) * block_size, column : column + 1]
        rows = pl.ds(row * block_size, block_size)
        total = couple_row(place_ref, columns_ref, hamiltonian_ref, pieces, row, None)
        once = 0.5 * (total + weight * trial_ref[rows, :])
        once_ref[rows, :] = once
        round_ref[row] = once.astype(jnp.bfloat16)


def second_kernel(
    place_ref, columns_ref, hamiltonian_ref, gathered_ref, inner_ref, outer_ref,
    potential_ref, trial_ref, once_ref, filtered_ref, gram_ref,
):
    shard_blocks, _, block_size, _ = hamiltonian_ref.shape
    weights = potential_columns(potential_ref)
    pieces = all_pieces(place_ref, gathered_ref, inner_ref, outer_ref)
    per_column = LANES // block_size
    for row in range(shard_blocks):
        column, part = divmod(row, per_column)
        weight = weights[part * block_size : (part + 1) * block_size, column : column + 1]
        rows = pl.ds(row * block_size, block_size)
        total = couple_row(place_ref, columns_ref, hamiltonian_ref, pieces, row, None)
        filtered_ref[rows, :] = total + weight * once_ref[rows, :] - trial_ref[rows, :]
    flat = filtered_ref[...]
    gram_ref[...] = lax.dot_general(
        flat, flat, (((0,), (0,)), ((), ())), precision=precise,
        preferred_element_type=jnp.float32,
    )


def factor_kernel(rows_total, gram_ref, filtered_ref, ortho_ref, upper_ref, inverse_ref):
    size = gram_ref.shape[0]
    panels = size // SUB
    shape = (SUB, size)
    row_index = lax.broadcasted_iota(jnp.int32, shape, 0)
    lane_index = lax.broadcasted_iota(jnp.int32, shape, 1)

    def along_lanes(panel, lane):
        return jnp.broadcast_to(panel[:, lane : lane + 1], shape)

    def along_rows(panel, row):
        return jnp.broadcast_to(panel[row : row + 1, :], shape)

    matrix = [gram_ref[pl.ds(k * SUB, SUB), :] * (1.0 / rows_total) for k in range(panels)]
    inverse = [
        jnp.where(lane_index == row_index + k * SUB, 1.0, 0.0).astype(jnp.float32)
        for k in range(panels)
    ]
    for k in range(panels):
        block = [along_lanes(matrix[k], k * SUB + c) for c in range(SUB)]
        below = {
            p: [along_lanes(matrix[p], k * SUB + c) for c in range(SUB)]
            for p in range(k + 1, panels)
        }
        pivots = jnp.ones(shape, jnp.float32)
        for j in range(SUB):
            pivot = along_rows(block[j], j)
            reciprocal = 1.0 / pivot
            pivots = jnp.where(row_index == j, pivot, pivots)
            lower_part = jnp.where(row_index > j, block[j], 0.0)
            row = along_rows(matrix[k], j) * reciprocal
            inverse_row = along_rows(inverse[k], j) * reciprocal
            for c in range(j + 1, SUB):
                factor = along_rows(block[c], j) * reciprocal
                block[c] = block[c] - block[j] * factor
                for p in below:
                    below[p][c] = below[p][c] - below[p][j] * factor
            matrix[k] = matrix[k] - lower_part * row
            inverse[k] = inverse[k] - lower_part * inverse_row
            for p in below:
                matrix[p] = matrix[p] - below[p][j] * row
                inverse[p] = inverse[p] - below[p][j] * inverse_row
        scale = lax.rsqrt(pivots)
        upper = jnp.where(lane_index >= row_index + k * SUB, matrix[k] * scale, 0.0)
        upper_ref[pl.ds(k * SUB, SUB), :] = upper
        inverse_ref[pl.ds(k * SUB, SUB), :] = inverse[k] * scale
    ortho_ref[...] = lax.dot_general(
        filtered_ref[...], inverse_ref[...], (((1,), (1,)), ((), ())), precision=precise,
        preferred_element_type=jnp.float32,
    )


def call(kernel, out_shape, in_specs, scratch=()):
    return pl.pallas_call(
        kernel,
        out_shape=out_shape,
        in_specs=in_specs,
        out_specs=jax.tree.map(lambda _: vmem, out_shape),
        scratch_shapes=list(scratch),
        compiler_params=pltpu.CompilerParams(vmem_limit_bytes=VMEM_LIMIT),
    )


def on_device(hamiltonian, block_columns, potential, trial_slab):
    shard_blocks, _, block_size, _ = hamiltonian.shape
    flat_rows, states = trial_slab.shape
    columns = block_columns.reshape(-1)
    weights = potential.reshape(-1, LANES)
    rows_total = flat_rows * lax.axis_size("group") * lax.axis_size("blk")
    place = (lax.axis_index("group") % 2).reshape(1).astype(jnp.int32)
    flat = jax.ShapeDtypeStruct((flat_rows, states), jnp.float32)
    rounded = jax.ShapeDtypeStruct((shard_blocks, block_size, states), jnp.bfloat16)
    square = jax.ShapeDtypeStruct((states, states), jnp.float32)

    def exchanged(value):
        return lax.all_gather(value, "blk"), pair_exchange(value, 0), pair_exchange(value, 1)

    start = trial_slab.reshape(shard_blocks, block_size, states).astype(jnp.bfloat16)
    once, once_round = call(first_kernel, (flat, rounded), [smem, smem] + [vmem] * 6)(
        place, columns, hamiltonian, *exchanged(start), weights, trial_slab
    )
    filtered, gram = call(second_kernel, (flat, square), [smem, smem] + [vmem] * 7)(
        place, columns, hamiltonian, *exchanged(once_round), weights, trial_slab, once
    )
    gram = lax.psum(gram, ("group", "blk"))
    return call(
        functools.partial(factor_kernel, rows_total),
        (flat, square),
        [vmem, vmem],
        [pltpu.VMEM((states, states), jnp.float32)],
    )(gram, filtered)


def solution(mesh):
    placed = (
        P(("group", "blk"), None, None, None),
        P(("group", "blk"), None, None),
        P(("group", "blk")),
        P(("group", "blk"), None),
    )
    return jax.shard_map(
        on_device,
        mesh=mesh,
        in_specs=placed,
        out_specs=(P(("group", "blk"), None), P()),
        check_vma=False,
    )
```

```python
import functools

import jax
import jax.numpy as jnp
from jax import lax
from jax.experimental import pallas as pl
from jax.experimental.pallas import tpu as pltpu
from jax.sharding import PartitionSpec as P

precise = lax.Precision.HIGHEST
LANES = 128
SUB = 8
VMEM_LIMIT = 40 * 1024 * 1024
vmem = pl.BlockSpec(memory_space=pltpu.VMEM)
smem = pl.BlockSpec(memory_space=pltpu.SMEM)


def pair_exchange(value, offset):
    count = lax.axis_size("group")
    route = []
    for low in range(offset, count - 1, 2):
        route += [(low, low + 1), (low + 1, low)]
    return lax.ppermute(value, "group", route)


def step_bits(group, level):
    levels = lax.axis_size("blk").bit_length() - 1
    return jnp.where(group % 2 == 1, levels - 1 - level, level)


def cycle_exchange(value, level):
    groups, cycle_size = lax.axis_size("group"), lax.axis_size("blk")
    levels = cycle_size.bit_length() - 1
    route = []
    for group in range(groups):
        bit = levels - 1 - level if group % 2 else level
        route += [
            (group * cycle_size + index, group * cycle_size + (index ^ 1 << bit))
            for index in range(cycle_size)
        ]
    return lax.ppermute(value, ("group", "blk"), route)


def from_partner(value, axis, bit):
    count = lax.axis_size(axis)
    return lax.ppermute(value, axis, [(index, index ^ 1 << bit) for index in range(count)])


def summed(value):
    for axis in ("group", "blk"):
        for bit in range(lax.axis_size(axis).bit_length() - 1):
            value = value + from_partner(value, axis, bit)
    return value


def potential_columns(potential_ref):
    return jnp.transpose(potential_ref[...])


def couple_row(sources_ref, columns_ref, hamiltonian_ref, pieces, row):
    sources, per_source = hamiltonian_ref.shape[1], hamiltonian_ref.shape[3] // hamiltonian_ref.shape[2]
    total = None
    for index, piece_ref in enumerate(pieces):
        source = sources_ref[index]
        first = (row * sources + source) * per_source
        picked = jnp.concatenate(
            [piece_ref[columns_ref[first + slot]] for slot in range(per_source)], axis=0
        )
        product = jnp.dot(
            hamiltonian_ref[row, source], picked, preferred_element_type=jnp.float32
        )
        total = product if total is None else total + product
    return total


def first_kernel(count, sources_ref, columns_ref, hamiltonian_ref, potential_ref, trial_ref, *refs):
    pieces, (once_ref, round_ref) = refs[:count], refs[count:]
    shard_blocks, _, block_size, _ = hamiltonian_ref.shape
    weights = potential_columns(potential_ref)
    per_column = LANES // block_size
    for row in range(shard_blocks):
        column, part = divmod(row, per_column)
        weight = weights[part * block_size : (part + 1) * block_size, column : column + 1]
        rows = pl.ds(row * block_size, block_size)
        total = couple_row(sources_ref, columns_ref, hamiltonian_ref, pieces, row)
        once = 0.5 * (total + weight * trial_ref[rows, :])
        once_ref[rows, :] = once
        round_ref[row] = once.astype(jnp.bfloat16)


def second_kernel(
    count, sources_ref, columns_ref, hamiltonian_ref, potential_ref, trial_ref, once_ref, *refs
):
    pieces, (filtered_ref, gram_ref) = refs[:count], refs[count:]
    shard_blocks, _, block_size, _ = hamiltonian_ref.shape
    weights = potential_columns(potential_ref)
    per_column = LANES // block_size
    for row in range(shard_blocks):
        column, part = divmod(row, per_column)
        weight = weights[part * block_size : (part + 1) * block_size, column : column + 1]
        rows = pl.ds(row * block_size, block_size)
        total = couple_row(sources_ref, columns_ref, hamiltonian_ref, pieces, row)
        filtered_ref[rows, :] = total + weight * once_ref[rows, :] - trial_ref[rows, :]
    flat = filtered_ref[...]
    gram_ref[...] = lax.dot_general(
        flat, flat, (((0,), (0,)), ((), ())), precision=precise,
        preferred_element_type=jnp.float32,
    )


def factor_kernel(rows_total, gram_ref, filtered_ref, ortho_ref, upper_ref, inverse_ref):
    size = gram_ref.shape[0]
    panels = size // SUB
    shape = (SUB, size)
    row_index = lax.broadcasted_iota(jnp.int32, shape, 0)
    lane_index = lax.broadcasted_iota(jnp.int32, shape, 1)

    def along_lanes(panel, lane):
        return jnp.broadcast_to(panel[:, lane : lane + 1], shape)

    def along_rows(panel, row):
        return jnp.broadcast_to(panel[row : row + 1, :], shape)

    matrix = [gram_ref[pl.ds(k * SUB, SUB), :] * (1.0 / rows_total) for k in range(panels)]
    inverse = [
        jnp.where(lane_index == row_index + k * SUB, 1.0, 0.0).astype(jnp.float32)
        for k in range(panels)
    ]
    for k in range(panels):
        block = [along_lanes(matrix[k], k * SUB + c) for c in range(SUB)]
        below = {
            p: [along_lanes(matrix[p], k * SUB + c) for c in range(SUB)]
            for p in range(k + 1, panels)
        }
        pivots = jnp.ones(shape, jnp.float32)
        for j in range(SUB):
            pivot = along_rows(block[j], j)
            reciprocal = 1.0 / pivot
            pivots = jnp.where(row_index == j, pivot, pivots)
            lower_part = jnp.where(row_index > j, block[j], 0.0)
            row = along_rows(matrix[k], j) * reciprocal
            inverse_row = along_rows(inverse[k], j) * reciprocal
            for c in range(j + 1, SUB):
                factor = along_rows(block[c], j) * reciprocal
                block[c] = block[c] - block[j] * factor
                for p in below:
                    below[p][c] = below[p][c] - below[p][j] * factor
            matrix[k] = matrix[k] - lower_part * row
            inverse[k] = inverse[k] - lower_part * inverse_row
            for p in below:
                matrix[p] = matrix[p] - below[p][j] * row
                inverse[p] = inverse[p] - below[p][j] * inverse_row
        scale = lax.rsqrt(pivots)
        upper = jnp.where(lane_index >= row_index + k * SUB, matrix[k] * scale, 0.0)
        upper_ref[pl.ds(k * SUB, SUB), :] = upper
        inverse_ref[pl.ds(k * SUB, SUB), :] = inverse[k] * scale
    ortho_ref[...] = lax.dot_general(
        filtered_ref[...], inverse_ref[...], (((1,), (1,)), ((), ())), precision=precise,
        preferred_element_type=jnp.float32,
    )


def call(kernel, out_shape, in_specs, scratch=()):
    return pl.pallas_call(
        kernel,
        out_shape=out_shape,
        in_specs=in_specs,
        out_specs=jax.tree.map(lambda _: vmem, out_shape),
        scratch_shapes=list(scratch),
        compiler_params=pltpu.CompilerParams(vmem_limit_bytes=VMEM_LIMIT),
    )


def on_device(hamiltonian, block_columns, potential, trial_slab):
    shard_blocks, _, block_size, _ = hamiltonian.shape
    flat_rows, states = trial_slab.shape
    columns = block_columns.reshape(-1)
    weights = potential.reshape(-1, LANES)
    rows_total = flat_rows * lax.axis_size("group") * lax.axis_size("blk")
    group, index = lax.axis_index("group"), lax.axis_index("blk")
    cycle_size = lax.axis_size("blk")
    levels = cycle_size.bit_length() - 1
    origins = [index]
    for level in range(levels):
        flip = jnp.left_shift(1, step_bits(group, level))
        origins += [jnp.bitwise_xor(origin, flip) for origin in origins]
    odd = group % 2
    origins += [cycle_size + 1 - odd, cycle_size + odd]
    sources = jnp.stack(origins).astype(jnp.int32)
    flat = jax.ShapeDtypeStruct((flat_rows, states), jnp.float32)
    rounded = jax.ShapeDtypeStruct((shard_blocks, block_size, states), jnp.bfloat16)
    square = jax.ShapeDtypeStruct((states, states), jnp.float32)

    def exchanged(value):
        pieces = [value]
        for level in range(levels):
            pieces += [cycle_exchange(piece, level) for piece in pieces]
        return pieces + [pair_exchange(value, 0), pair_exchange(value, 1)]

    count = cycle_size + 2
    start = trial_slab.reshape(shard_blocks, block_size, states).astype(jnp.bfloat16)
    once, once_round = call(
        functools.partial(first_kernel, count), (flat, rounded), [smem] * 2 + [vmem] * (3 + count)
    )(sources, columns, hamiltonian, weights, trial_slab, *exchanged(start))
    filtered, gram = call(
        functools.partial(second_kernel, count), (flat, square), [smem] * 2 + [vmem] * (4 + count)
    )(sources, columns, hamiltonian, weights, trial_slab, once, *exchanged(once_round))
    gram = summed(gram)
    return call(
        functools.partial(factor_kernel, rows_total),
        (flat, square),
        [vmem, vmem],
        [pltpu.VMEM((states, states), jnp.float32)],
    )(gram, filtered)


def solution(mesh):
    placed = (
        P(("group", "blk"), None, None, None),
        P(("group", "blk"), None, None),
        P(("group", "blk")),
        P(("group", "blk"), None),
    )
    return jax.shard_map(
        on_device,
        mesh=mesh,
        in_specs=placed,
        out_specs=(P(("group", "blk"), None), P()),
        check_vma=False,
    )
```

```python
import functools

import jax
import jax.numpy as jnp
from jax import lax
from jax.experimental import pallas as pl
from jax.experimental.pallas import tpu as pltpu
from jax.sharding import PartitionSpec as P

precise = lax.Precision.HIGHEST
LANES = 128
SUB = 8
VMEM_LIMIT = 40 * 1024 * 1024
vmem = pl.BlockSpec(memory_space=pltpu.VMEM)
smem = pl.BlockSpec(memory_space=pltpu.SMEM)


def pair_exchange(value, offset):
    count = lax.axis_size("group")
    route = []
    for low in range(offset, count - 1, 2):
        route += [(low, low + 1), (low + 1, low)]
    return lax.ppermute(value, "group", route)


def step_bits(group, level):
    levels = lax.axis_size("blk").bit_length() - 1
    return jnp.where(group % 2 == 1, levels - 1 - level, level)


def cycle_exchange(value, level):
    groups, cycle_size = lax.axis_size("group"), lax.axis_size("blk")
    levels = cycle_size.bit_length() - 1
    route = []
    for group in range(groups):
        bit = levels - 1 - level if group % 2 else level
        route += [
            (group * cycle_size + index, group * cycle_size + (index ^ 1 << bit))
            for index in range(cycle_size)
        ]
    return lax.ppermute(value, ("group", "blk"), route)


def potential_columns(potential_ref):
    return jnp.transpose(potential_ref[...])


def couple_row(sources_ref, columns_ref, hamiltonian_ref, pieces, row):
    sources, per_source = hamiltonian_ref.shape[1], hamiltonian_ref.shape[3] // hamiltonian_ref.shape[2]
    total = None
    for index, piece_ref in pieces:
        source = sources_ref[index]
        first = (row * sources + source) * per_source
        picked = jnp.concatenate(
            [piece_ref[columns_ref[first + slot]] for slot in range(per_source)], axis=0
        )
        product = jnp.dot(
            hamiltonian_ref[row, source], picked, preferred_element_type=jnp.float32
        )
        total = product if total is None else total + product
    return total


def own_kernel(
    sources_ref, columns_ref, hamiltonian_ref, own_ref, potential_ref, scaled_ref, *refs
):
    less, partial_ref = refs[:-1], refs[-1]
    shard_blocks, _, block_size, _ = hamiltonian_ref.shape
    weights = potential_columns(potential_ref)
    per_column = LANES // block_size
    for row in range(shard_blocks):
        column, part = divmod(row, per_column)
        weight = weights[part * block_size : (part + 1) * block_size, column : column + 1]
        rows = pl.ds(row * block_size, block_size)
        total = weight * scaled_ref[rows, :]
        for less_ref in less:
            total = total - less_ref[rows, :]
        partial_ref[rows, :] = total + couple_row(
            sources_ref, columns_ref, hamiltonian_ref, [(0, own_ref)], row
        )


def middle_kernel(numbers, sources_ref, columns_ref, hamiltonian_ref, partial_ref, *refs):
    pieces, sum_ref = list(zip(numbers, refs[:-1])), refs[-1]
    shard_blocks, _, block_size, _ = hamiltonian_ref.shape
    for row in range(shard_blocks):
        rows = pl.ds(row * block_size, block_size)
        sum_ref[rows, :] = partial_ref[rows, :] + couple_row(
            sources_ref, columns_ref, hamiltonian_ref, pieces, row
        )


def first_kernel(
    number, sources_ref, columns_ref, hamiltonian_ref, partial_ref, piece_ref, once_ref, round_ref
):
    shard_blocks, _, block_size, _ = hamiltonian_ref.shape
    for row in range(shard_blocks):
        rows = pl.ds(row * block_size, block_size)
        once = 0.5 * (
            partial_ref[rows, :]
            + couple_row(sources_ref, columns_ref, hamiltonian_ref, [(number, piece_ref)], row)
        )
        once_ref[rows, :] = once
        round_ref[row] = once.astype(jnp.bfloat16)


def second_kernel(
    number, sources_ref, columns_ref, hamiltonian_ref, partial_ref, piece_ref,
    filtered_ref, packed_ref,
):
    shard_blocks, _, block_size, _ = hamiltonian_ref.shape
    for row in range(shard_blocks):
        rows = pl.ds(row * block_size, block_size)
        filtered_ref[rows, :] = partial_ref[rows, :] + couple_row(
            sources_ref, columns_ref, hamiltonian_ref, [(number, piece_ref)], row
        )
    flat = filtered_ref[...]
    gram = lax.dot_general(
        flat, flat, (((0,), (0,)), ((), ())), precision=precise,
        preferred_element_type=jnp.float32,
    )
    pack(gram, packed_ref)


def pack(gram, packed_ref):
    size = gram.shape[0]
    half = size // 2
    row = lax.broadcasted_iota(jnp.int32, (half, size), 0)
    lane = lax.broadcasted_iota(jnp.int32, (half, size), 1)
    lower = gram[half:, :]
    packed_ref[pl.ds(0, half), :] = jnp.where(lane < row, pltpu.roll(lower, half, 1), gram[:half, :])
    diagonal = jnp.sum(jnp.where(lane == row + half, lower, 0.0), axis=0, keepdims=True)
    packed_ref[pl.ds(half, SUB), :] = jnp.broadcast_to(diagonal, (SUB, size))


def unpack(packed_ref):
    size = packed_ref.shape[1]
    half = size // 2
    row = lax.broadcasted_iota(jnp.int32, (size, size), 0)
    lane = lax.broadcasted_iota(jnp.int32, (size, size), 1)
    upper = packed_ref[pl.ds(0, half), :]
    both = jnp.concatenate([upper, pltpu.roll(upper, half, 1)], axis=0)
    held = ((row < half) & (lane > row)) | ((row >= half) & (lane >= half) & (lane < row))
    off_diagonal = jnp.where(held, both, 0.0)
    diagonal = jnp.where(row < half, both, packed_ref[pl.ds(half, 1), :])
    return off_diagonal + jnp.transpose(off_diagonal) + jnp.where(row == lane, diagonal, 0.0)


def inverse_of(value):
    estimate = pl.reciprocal(value, approx=True)
    estimate = estimate * (2.0 - value * estimate)
    return estimate * (2.0 - value * estimate)


def factor_kernel(rows_total, packed_ref, filtered_ref, ortho_ref, upper_ref, inverse_ref):
    size = packed_ref.shape[1]
    panels = size // SUB
    shape = (SUB, size)
    row_index = lax.broadcasted_iota(jnp.int32, shape, 0)
    lane_index = lax.broadcasted_iota(jnp.int32, shape, 1)

    def along_lanes(panel, first):
        return [jnp.broadcast_to(panel[:, first + c : first + c + 1], shape) for c in range(SUB)]

    def along_rows(panel, row):
        return jnp.broadcast_to(panel[row : row + 1, :], shape)

    gram = unpack(packed_ref) * (1.0 / rows_total)
    matrix = [gram[k * SUB : (k + 1) * SUB, :] for k in range(panels)]
    inverse = [
        jnp.where(lane_index == row_index + k * SUB, 1.0, 0.0).astype(jnp.float32)
        for k in range(panels)
    ]
    block = along_lanes(matrix[0], 0)
    for k in range(panels):
        below = {p: along_lanes(matrix[p], k * SUB) for p in range(k + 1, panels)}
        following = along_lanes(matrix[k + 1], (k + 1) * SUB) if k + 1 < panels else None
        pivots = jnp.ones(shape, jnp.float32)
        for j in range(SUB):
            pivot = along_rows(block[j], j)
            reciprocal = inverse_of(pivot)
            pivots = jnp.where(row_index == j, pivot, pivots)
            factors = {c: along_rows(block[c], j) * reciprocal for c in range(j + 1, SUB)}
            for c in factors:
                block[c] = block[c] - block[j] * factors[c]
            if following is not None:
                column = below[k + 1][j]
                for c in factors:
                    below[k + 1][c] = below[k + 1][c] - column * factors[c]
                scaled = column * reciprocal
                for c in range(SUB):
                    following[c] = following[c] - column * along_rows(scaled, c)
            lower_part = jnp.where(row_index > j, block[j], 0.0)
            row = along_rows(matrix[k], j) * reciprocal
            inverse_row = along_rows(inverse[k], j) * reciprocal
            matrix[k] = matrix[k] - lower_part * row
            inverse[k] = inverse[k] - lower_part * inverse_row
            for p in below:
                if p > k + 1:
                    for c in factors:
                        below[p][c] = below[p][c] - below[p][j] * factors[c]
                matrix[p] = matrix[p] - below[p][j] * row
                inverse[p] = inverse[p] - below[p][j] * inverse_row
        block = following
        scale = lax.rsqrt(pivots)
        upper = jnp.where(lane_index >= row_index + k * SUB, matrix[k] * scale, 0.0)
        upper_ref[pl.ds(k * SUB, SUB), :] = upper
        inverse_ref[pl.ds(k * SUB, SUB), :] = inverse[k] * scale
    ortho_ref[...] = lax.dot_general(
        filtered_ref[...], inverse_ref[...], (((1,), (1,)), ((), ())), precision=precise,
        preferred_element_type=jnp.float32,
    )


def call(kernel, out_shape, in_specs, scratch=()):
    return pl.pallas_call(
        kernel,
        out_shape=out_shape,
        in_specs=in_specs,
        out_specs=jax.tree.map(lambda _: vmem, out_shape),
        scratch_shapes=list(scratch),
        compiler_params=pltpu.CompilerParams(vmem_limit_bytes=VMEM_LIMIT),
    )


def on_device(hamiltonian, block_columns, potential, trial_slab):
    shard_blocks, _, block_size, _ = hamiltonian.shape
    flat_rows, states = trial_slab.shape
    columns = block_columns.reshape(-1)
    weights = potential.reshape(-1, LANES)
    rows_total = flat_rows * lax.axis_size("group") * lax.axis_size("blk")
    group, index = lax.axis_index("group"), lax.axis_index("blk")
    cycle_size = lax.axis_size("blk")
    levels = cycle_size.bit_length() - 1
    origins = [index]
    for level in range(levels):
        flip = jnp.left_shift(1, step_bits(group, level))
        origins += [jnp.bitwise_xor(origin, flip) for origin in origins]
    odd = group % 2
    origins += [cycle_size + 1 - odd, cycle_size + odd]
    sources = jnp.stack(origins).astype(jnp.int32)
    last = cycle_size - 1
    middle = list(range(1, last)) + [cycle_size + 1, cycle_size]
    flat = jax.ShapeDtypeStruct((flat_rows, states), jnp.float32)
    rounded = jax.ShapeDtypeStruct((shard_blocks, block_size, states), jnp.bfloat16)
    packed = jax.ShapeDtypeStruct((states // 2 + SUB, states), jnp.float32)
    square = jax.ShapeDtypeStruct((states, states), jnp.float32)

    def exchanged(value):
        pairs = [pair_exchange(value, 0), pair_exchange(value, 1)]
        pieces = [value]
        for level in range(levels):
            pieces += [cycle_exchange(piece, level) for piece in pieces]
        return pieces + pairs

    def most(pieces, *terms):
        own = call(own_kernel, flat, [smem] * 2 + [vmem] * (3 + len(terms)))(
            sources, columns, hamiltonian, pieces[0], weights, *terms
        )
        return call(
            functools.partial(middle_kernel, middle), flat,
            [smem] * 2 + [vmem] * (2 + len(middle)),
        )(sources, columns, hamiltonian, own, *[pieces[number] for number in middle])

    pieces = exchanged(trial_slab.reshape(rounded.shape).astype(jnp.bfloat16))
    partial = most(pieces, trial_slab)
    once, once_round = call(
        functools.partial(first_kernel, last), (flat, rounded), [smem] * 2 + [vmem] * 3
    )(sources, columns, hamiltonian, partial, pieces[last])
    pieces = exchanged(once_round)
    partial = most(pieces, once, trial_slab)
    filtered, gram = call(
        functools.partial(second_kernel, last), (flat, packed), [smem] * 2 + [vmem] * 3
    )(sources, columns, hamiltonian, partial, pieces[last])
    gram = lax.psum(gram, ("group", "blk"))
    return call(
        functools.partial(factor_kernel, rows_total),
        (flat, square),
        [vmem, vmem],
        [pltpu.VMEM((states, states), jnp.float32)],
    )(gram, filtered)


def solution(mesh):
    placed = (
        P(("group", "blk"), None, None, None),
        P(("group", "blk"), None, None),
        P(("group", "blk")),
        P(("group", "blk"), None),
    )
    return jax.shard_map(
        on_device,
        mesh=mesh,
        in_specs=placed,
        out_specs=(P(("group", "blk"), None), P()),
        check_vma=False,
    )
```

```python
import functools

import jax
import jax.numpy as jnp
from jax import lax
from jax.experimental import pallas as pl
from jax.experimental.pallas import tpu as pltpu
from jax.sharding import PartitionSpec as P

precise = lax.Precision.HIGHEST
LANES = 128
SUB = 8
VMEM_LIMIT = 40 * 1024 * 1024
vmem = pl.BlockSpec(memory_space=pltpu.VMEM)
smem = pl.BlockSpec(memory_space=pltpu.SMEM)


def pair_exchange(value, offset):
    count = lax.axis_size("group")
    route = []
    for low in range(offset, count - 1, 2):
        route += [(low, low + 1), (low + 1, low)]
    return lax.ppermute(value, "group", route)


def step_bits(group, level):
    levels = lax.axis_size("blk").bit_length() - 1
    return jnp.where(group % 2 == 1, levels - 1 - level, level)


def cycle_exchange(value, level):
    groups, cycle_size = lax.axis_size("group"), lax.axis_size("blk")
    levels = cycle_size.bit_length() - 1
    route = []
    for group in range(groups):
        bit = levels - 1 - level if group % 2 else level
        route += [
            (group * cycle_size + index, group * cycle_size + (index ^ 1 << bit))
            for index in range(cycle_size)
        ]
    return lax.ppermute(value, ("group", "blk"), route)


def summed(value):
    axes = ("group", "blk")
    devices = lax.axis_size("group") * lax.axis_size("blk")
    shape = value.shape
    value = value.reshape((devices, -1) + ((shape[-1],) if shape[0] == devices else ()))
    part = jnp.sum(lax.all_to_all(value, axes, 0, 0), axis=0)
    shared = lax.all_to_all(jnp.broadcast_to(part, value.shape), axes, 0, 0)
    return shared.reshape(-1, shape[-1])


def potential_columns(potential_ref):
    return jnp.transpose(potential_ref[...])


def couple_row(sources_ref, columns_ref, hamiltonian_ref, pieces, row):
    sources, per_source = hamiltonian_ref.shape[1], hamiltonian_ref.shape[3] // hamiltonian_ref.shape[2]
    total = None
    for index, piece_ref in pieces:
        source = sources_ref[index]
        first = (row * sources + source) * per_source
        picked = jnp.concatenate(
            [piece_ref[columns_ref[first + slot]] for slot in range(per_source)], axis=0
        )
        product = jnp.dot(
            hamiltonian_ref[row, source], picked, preferred_element_type=jnp.float32
        )
        total = product if total is None else total + product
    return total


def own_kernel(
    sources_ref, columns_ref, hamiltonian_ref, own_ref, potential_ref, scaled_ref, *refs
):
    less, partial_ref = refs[:-1], refs[-1]
    shard_blocks, _, block_size, _ = hamiltonian_ref.shape
    weights = potential_columns(potential_ref)
    per_column = LANES // block_size
    for row in range(shard_blocks):
        column, part = divmod(row, per_column)
        weight = weights[part * block_size : (part + 1) * block_size, column : column + 1]
        rows = pl.ds(row * block_size, block_size)
        total = weight * scaled_ref[rows, :]
        for less_ref in less:
            total = total - less_ref[rows, :]
        partial_ref[rows, :] = total + couple_row(
            sources_ref, columns_ref, hamiltonian_ref, [(0, own_ref)], row
        )


def middle_kernel(numbers, sources_ref, columns_ref, hamiltonian_ref, partial_ref, *refs):
    pieces, sum_ref = list(zip(numbers, refs[:-1])), refs[-1]
    shard_blocks, _, block_size, _ = hamiltonian_ref.shape
    for row in range(shard_blocks):
        rows = pl.ds(row * block_size, block_size)
        sum_ref[rows, :] = partial_ref[rows, :] + couple_row(
            sources_ref, columns_ref, hamiltonian_ref, pieces, row
        )


def first_kernel(
    number, sources_ref, columns_ref, hamiltonian_ref, partial_ref, piece_ref, once_ref, round_ref
):
    shard_blocks, _, block_size, _ = hamiltonian_ref.shape
    for row in range(shard_blocks):
        rows = pl.ds(row * block_size, block_size)
        once = 0.5 * (
            partial_ref[rows, :]
            + couple_row(sources_ref, columns_ref, hamiltonian_ref, [(number, piece_ref)], row)
        )
        once_ref[rows, :] = once
        round_ref[row] = once.astype(jnp.bfloat16)


def second_kernel(
    number, sources_ref, columns_ref, hamiltonian_ref, partial_ref, piece_ref,
    filtered_ref, gram_ref,
):
    shard_blocks, _, block_size, _ = hamiltonian_ref.shape
    for row in range(shard_blocks):
        rows = pl.ds(row * block_size, block_size)
        filtered_ref[rows, :] = partial_ref[rows, :] + couple_row(
            sources_ref, columns_ref, hamiltonian_ref, [(number, piece_ref)], row
        )
    flat = filtered_ref[...]
    gram = lax.dot_general(
        flat, flat, (((0,), (0,)), ((), ())), precision=precise,
        preferred_element_type=jnp.float32,
    )
    per_part = gram_ref.shape[1]
    for part in range(gram_ref.shape[0]):
        gram_ref[part] = gram[part * per_part : (part + 1) * per_part, :]


def inverse_of(value):
    estimate = pl.reciprocal(value, approx=True)
    estimate = estimate * (2.0 - value * estimate)
    return estimate * (2.0 - value * estimate)


def factor_kernel(rows_total, gram_ref, filtered_ref, ortho_ref, upper_ref, inverse_ref):
    size = gram_ref.shape[1]
    panels = size // SUB
    shape = (SUB, size)
    row_index = lax.broadcasted_iota(jnp.int32, shape, 0)
    lane_index = lax.broadcasted_iota(jnp.int32, shape, 1)

    def along_lanes(panel, first):
        return [jnp.broadcast_to(panel[:, first + c : first + c + 1], shape) for c in range(SUB)]

    def along_rows(panel, row):
        return jnp.broadcast_to(panel[row : row + 1, :], shape)

    matrix = [gram_ref[pl.ds(k * SUB, SUB), :] * (1.0 / rows_total) for k in range(panels)]
    inverse = [
        jnp.where(lane_index == row_index + k * SUB, 1.0, 0.0).astype(jnp.float32)
        for k in range(panels)
    ]
    block = along_lanes(matrix[0], 0)
    for k in range(panels):
        below = {p: along_lanes(matrix[p], k * SUB) for p in range(k + 1, panels)}
        following = along_lanes(matrix[k + 1], (k + 1) * SUB) if k + 1 < panels else None
        pivots = jnp.ones(shape, jnp.float32)
        for j in range(SUB):
            pivot = along_rows(block[j], j)
            reciprocal = inverse_of(pivot)
            pivots = jnp.where(row_index == j, pivot, pivots)
            factors = {c: along_rows(block[c], j) * reciprocal for c in range(j + 1, SUB)}
            for c in factors:
                block[c] = block[c] - block[j] * factors[c]
            if following is not None:
                column = below[k + 1][j]
                for c in factors:
                    below[k + 1][c] = below[k + 1][c] - column * factors[c]
                scaled = column * reciprocal
                for c in range(SUB):
                    following[c] = following[c] - column * along_rows(scaled, c)
            lower_part = jnp.where(row_index > j, block[j], 0.0)
            row = along_rows(matrix[k], j) * reciprocal
            inverse_row = along_rows(inverse[k], j) * reciprocal
            matrix[k] = matrix[k] - lower_part * row
            inverse[k] = inverse[k] - lower_part * inverse_row
            for p in below:
                if p > k + 1:
                    for c in factors:
                        below[p][c] = below[p][c] - below[p][j] * factors[c]
                matrix[p] = matrix[p] - below[p][j] * row
                inverse[p] = inverse[p] - below[p][j] * inverse_row
        block = following
        scale = lax.rsqrt(pivots)
        upper = jnp.where(lane_index >= row_index + k * SUB, matrix[k] * scale, 0.0)
        upper_ref[pl.ds(k * SUB, SUB), :] = upper
        inverse_ref[pl.ds(k * SUB, SUB), :] = inverse[k] * scale
    ortho_ref[...] = lax.dot_general(
        filtered_ref[...], inverse_ref[...], (((1,), (1,)), ((), ())), precision=precise,
        preferred_element_type=jnp.float32,
    )


def call(kernel, out_shape, in_specs, scratch=()):
    return pl.pallas_call(
        kernel,
        out_shape=out_shape,
        in_specs=in_specs,
        out_specs=jax.tree.map(lambda _: vmem, out_shape),
        scratch_shapes=list(scratch),
        compiler_params=pltpu.CompilerParams(vmem_limit_bytes=VMEM_LIMIT),
    )


def on_device(hamiltonian, block_columns, potential, trial_slab):
    shard_blocks, _, block_size, _ = hamiltonian.shape
    flat_rows, states = trial_slab.shape
    columns = block_columns.reshape(-1)
    weights = potential.reshape(-1, LANES)
    rows_total = flat_rows * lax.axis_size("group") * lax.axis_size("blk")
    group, index = lax.axis_index("group"), lax.axis_index("blk")
    cycle_size = lax.axis_size("blk")
    levels = cycle_size.bit_length() - 1
    origins = [index]
    for level in range(levels):
        flip = jnp.left_shift(1, step_bits(group, level))
        origins += [jnp.bitwise_xor(origin, flip) for origin in origins]
    odd = group % 2
    origins += [cycle_size + 1 - odd, cycle_size + odd]
    sources = jnp.stack(origins).astype(jnp.int32)
    last = cycle_size - 1
    middle = list(range(1, last)) + [cycle_size + 1, cycle_size]
    flat = jax.ShapeDtypeStruct((flat_rows, states), jnp.float32)
    rounded = jax.ShapeDtypeStruct((shard_blocks, block_size, states), jnp.bfloat16)
    devices = lax.axis_size("group") * cycle_size
    parts = min(devices, states)
    parted = jax.ShapeDtypeStruct((parts, states // parts, states), jnp.float32)
    square = jax.ShapeDtypeStruct((states, states), jnp.float32)

    def exchanged(value):
        pairs = [pair_exchange(value, 0), pair_exchange(value, 1)]
        pieces = [value]
        for level in range(levels):
            pieces += [cycle_exchange(piece, level) for piece in pieces]
        return pieces + pairs

    def most(pieces, *terms):
        own = call(own_kernel, flat, [smem] * 2 + [vmem] * (3 + len(terms)))(
            sources, columns, hamiltonian, pieces[0], weights, *terms
        )
        return call(
            functools.partial(middle_kernel, middle), flat,
            [smem] * 2 + [vmem] * (2 + len(middle)),
        )(sources, columns, hamiltonian, own, *[pieces[number] for number in middle])

    pieces = exchanged(trial_slab.reshape(rounded.shape).astype(jnp.bfloat16))
    partial = most(pieces, trial_slab)
    once, once_round = call(
        functools.partial(first_kernel, last), (flat, rounded), [smem] * 2 + [vmem] * 3
    )(sources, columns, hamiltonian, partial, pieces[last])
    pieces = exchanged(once_round)
    partial = most(pieces, once, trial_slab)
    filtered, gram = call(
        functools.partial(second_kernel, last), (flat, parted), [smem] * 2 + [vmem] * 3
    )(sources, columns, hamiltonian, partial, pieces[last])
    gram = summed(gram)
    return call(
        functools.partial(factor_kernel, rows_total),
        (flat, square),
        [vmem, vmem],
        [pltpu.VMEM((states, states), jnp.float32)],
    )(gram, filtered)


def solution(mesh):
    placed = (
        P(("group", "blk"), None, None, None),
        P(("group", "blk"), None, None),
        P(("group", "blk")),
        P(("group", "blk"), None),
    )
    return jax.shard_map(
        on_device,
        mesh=mesh,
        in_specs=placed,
        out_specs=(P(("group", "blk"), None), P()),
        check_vma=False,
    )
```

```python
import functools

import jax
import jax.numpy as jnp
from jax import lax
from jax.experimental import pallas as pl
from jax.experimental.pallas import tpu as pltpu
from jax.sharding import PartitionSpec as P

precise = lax.Precision.HIGHEST
LANES = 128
SUB = 8
VMEM_LIMIT = 40 * 1024 * 1024
vmem = pl.BlockSpec(memory_space=pltpu.VMEM)
smem = pl.BlockSpec(memory_space=pltpu.SMEM)


def pair_exchange(value, offset):
    count = lax.axis_size("group")
    route = []
    for low in range(offset, count - 1, 2):
        route += [(low, low + 1), (low + 1, low)]
    return lax.ppermute(value, "group", route)


def step_bits(group, level):
    levels = lax.axis_size("blk").bit_length() - 1
    return jnp.where(group % 2 == 1, levels - 1 - level, level)


def cycle_exchange(value, level):
    groups, cycle_size = lax.axis_size("group"), lax.axis_size("blk")
    levels = cycle_size.bit_length() - 1
    route = []
    for group in range(groups):
        bit = levels - 1 - level if group % 2 else level
        route += [
            (group * cycle_size + index, group * cycle_size + (index ^ 1 << bit))
            for index in range(cycle_size)
        ]
    return lax.ppermute(value, ("group", "blk"), route)


def handed_out(value, axis):
    copies = jnp.broadcast_to(value, (lax.axis_size(axis),) + value.shape)
    return lax.all_to_all(copies, axis, 0, 0)


def summed(value):
    part = jnp.sum(lax.all_to_all(value, "blk", 0, 0), axis=0)
    part = jnp.sum(handed_out(part, "group"), axis=0)
    return handed_out(part, "blk").reshape(-1, value.shape[-1])


def potential_columns(potential_ref):
    return jnp.transpose(potential_ref[...])


def couple_row(sources_ref, columns_ref, hamiltonian_ref, pieces, row):
    sources, per_source = hamiltonian_ref.shape[1], hamiltonian_ref.shape[3] // hamiltonian_ref.shape[2]
    total = None
    for index, piece_ref in pieces:
        source = sources_ref[index]
        first = (row * sources + source) * per_source
        picked = jnp.concatenate(
            [piece_ref[columns_ref[first + slot]] for slot in range(per_source)], axis=0
        )
        product = jnp.dot(
            hamiltonian_ref[row, source], picked, preferred_element_type=jnp.float32
        )
        total = product if total is None else total + product
    return total


def own_kernel(
    sources_ref, columns_ref, hamiltonian_ref, own_ref, potential_ref, scaled_ref, *refs
):
    less, partial_ref = refs[:-1], refs[-1]
    shard_blocks, _, block_size, _ = hamiltonian_ref.shape
    weights = potential_columns(potential_ref)
    per_column = LANES // block_size
    for row in range(shard_blocks):
        column, part = divmod(row, per_column)
        weight = weights[part * block_size : (part + 1) * block_size, column : column + 1]
        rows = pl.ds(row * block_size, block_size)
        total = weight * scaled_ref[rows, :]
        for less_ref in less:
            total = total - less_ref[rows, :]
        partial_ref[rows, :] = total + couple_row(
            sources_ref, columns_ref, hamiltonian_ref, [(0, own_ref)], row
        )


def middle_kernel(numbers, sources_ref, columns_ref, hamiltonian_ref, partial_ref, *refs):
    pieces, sum_ref = list(zip(numbers, refs[:-1])), refs[-1]
    shard_blocks, _, block_size, _ = hamiltonian_ref.shape
    for row in range(shard_blocks):
        rows = pl.ds(row * block_size, block_size)
        sum_ref[rows, :] = partial_ref[rows, :] + couple_row(
            sources_ref, columns_ref, hamiltonian_ref, pieces, row
        )


def first_kernel(
    number, sources_ref, columns_ref, hamiltonian_ref, partial_ref, piece_ref, once_ref, round_ref
):
    shard_blocks, _, block_size, _ = hamiltonian_ref.shape
    for row in range(shard_blocks):
        rows = pl.ds(row * block_size, block_size)
        once = 0.5 * (
            partial_ref[rows, :]
            + couple_row(sources_ref, columns_ref, hamiltonian_ref, [(number, piece_ref)], row)
        )
        once_ref[rows, :] = once
        round_ref[row] = once.astype(jnp.bfloat16)


def second_kernel(
    number, sources_ref, columns_ref, hamiltonian_ref, partial_ref, piece_ref,
    filtered_ref, gram_ref,
):
    shard_blocks, _, block_size, _ = hamiltonian_ref.shape
    for row in range(shard_blocks):
        rows = pl.ds(row * block_size, block_size)
        filtered_ref[rows, :] = partial_ref[rows, :] + couple_row(
            sources_ref, columns_ref, hamiltonian_ref, [(number, piece_ref)], row
        )
    flat = filtered_ref[...]
    gram = lax.dot_general(
        flat, flat, (((0,), (0,)), ((), ())), precision=precise,
        preferred_element_type=jnp.float32,
    )
    per_part = gram_ref.shape[1]
    for part in range(gram_ref.shape[0]):
        gram_ref[part] = gram[part * per_part : (part + 1) * per_part, :]


def inverse_of(value):
    estimate = pl.reciprocal(value, approx=True)
    estimate = estimate * (2.0 - value * estimate)
    return estimate * (2.0 - value * estimate)


def factor_kernel(rows_total, gram_ref, filtered_ref, ortho_ref, upper_ref, inverse_ref):
    size = gram_ref.shape[1]
    panels = size // SUB
    shape = (SUB, size)
    row_index = lax.broadcasted_iota(jnp.int32, shape, 0)
    lane_index = lax.broadcasted_iota(jnp.int32, shape, 1)

    def along_lanes(panel, first):
        return [jnp.broadcast_to(panel[:, first + c : first + c + 1], shape) for c in range(SUB)]

    def along_rows(panel, row):
        return jnp.broadcast_to(panel[row : row + 1, :], shape)

    matrix = [gram_ref[pl.ds(k * SUB, SUB), :] * (1.0 / rows_total) for k in range(panels)]
    inverse = [
        jnp.where(lane_index == row_index + k * SUB, 1.0, 0.0).astype(jnp.float32)
        for k in range(panels)
    ]
    block = along_lanes(matrix[0], 0)
    for k in range(panels):
        below = {p: along_lanes(matrix[p], k * SUB) for p in range(k + 1, panels)}
        following = along_lanes(matrix[k + 1], (k + 1) * SUB) if k + 1 < panels else None
        pivots = jnp.ones(shape, jnp.float32)
        for j in range(SUB):
            pivot = along_rows(block[j], j)
            reciprocal = inverse_of(pivot)
            pivots = jnp.where(row_index == j, pivot, pivots)
            factors = {c: along_rows(block[c], j) * reciprocal for c in range(j + 1, SUB)}
            for c in factors:
                block[c] = block[c] - block[j] * factors[c]
            if following is not None:
                column = below[k + 1][j]
                for c in factors:
                    below[k + 1][c] = below[k + 1][c] - column * factors[c]
                scaled = column * reciprocal
                for c in range(SUB):
                    following[c] = following[c] - column * along_rows(scaled, c)
            lower_part = jnp.where(row_index > j, block[j], 0.0)
            row = along_rows(matrix[k], j) * reciprocal
            inverse_row = along_rows(inverse[k], j) * reciprocal
            matrix[k] = matrix[k] - lower_part * row
            inverse[k] = inverse[k] - lower_part * inverse_row
            for p in below:
                if p > k + 1:
                    for c in factors:
                        below[p][c] = below[p][c] - below[p][j] * factors[c]
                matrix[p] = matrix[p] - below[p][j] * row
                inverse[p] = inverse[p] - below[p][j] * inverse_row
        block = following
        scale = lax.rsqrt(pivots)
        upper = jnp.where(lane_index >= row_index + k * SUB, matrix[k] * scale, 0.0)
        upper_ref[pl.ds(k * SUB, SUB), :] = upper
        inverse_ref[pl.ds(k * SUB, SUB), :] = inverse[k] * scale
    ortho_ref[...] = lax.dot_general(
        filtered_ref[...], inverse_ref[...], (((1,), (1,)), ((), ())), precision=precise,
        preferred_element_type=jnp.float32,
    )


def call(kernel, out_shape, in_specs, scratch=()):
    return pl.pallas_call(
        kernel,
        out_shape=out_shape,
        in_specs=in_specs,
        out_specs=jax.tree.map(lambda _: vmem, out_shape),
        scratch_shapes=list(scratch),
        compiler_params=pltpu.CompilerParams(vmem_limit_bytes=VMEM_LIMIT),
    )


def on_device(hamiltonian, block_columns, potential, trial_slab):
    shard_blocks, _, block_size, _ = hamiltonian.shape
    flat_rows, states = trial_slab.shape
    columns = block_columns.reshape(-1)
    weights = potential.reshape(-1, LANES)
    rows_total = flat_rows * lax.axis_size("group") * lax.axis_size("blk")
    group, index = lax.axis_index("group"), lax.axis_index("blk")
    cycle_size = lax.axis_size("blk")
    levels = cycle_size.bit_length() - 1
    origins = [index]
    for level in range(levels):
        flip = jnp.left_shift(1, step_bits(group, level))
        origins += [jnp.bitwise_xor(origin, flip) for origin in origins]
    odd = group % 2
    origins += [cycle_size + 1 - odd, cycle_size + odd]
    sources = jnp.stack(origins).astype(jnp.int32)
    last = cycle_size - 1
    middle = list(range(1, last)) + [cycle_size + 1, cycle_size]
    flat = jax.ShapeDtypeStruct((flat_rows, states), jnp.float32)
    rounded = jax.ShapeDtypeStruct((shard_blocks, block_size, states), jnp.bfloat16)
    parted = jax.ShapeDtypeStruct((cycle_size, states // cycle_size, states), jnp.float32)
    square = jax.ShapeDtypeStruct((states, states), jnp.float32)

    def exchanged(value):
        pairs = [pair_exchange(value, 0), pair_exchange(value, 1)]
        pieces = [value]
        for level in range(levels):
            pieces += [cycle_exchange(piece, level) for piece in pieces]
        return pieces + pairs

    def most(pieces, *terms):
        own = call(own_kernel, flat, [smem] * 2 + [vmem] * (3 + len(terms)))(
            sources, columns, hamiltonian, pieces[0], weights, *terms
        )
        return call(
            functools.partial(middle_kernel, middle), flat,
            [smem] * 2 + [vmem] * (2 + len(middle)),
        )(sources, columns, hamiltonian, own, *[pieces[number] for number in middle])

    pieces = exchanged(trial_slab.reshape(rounded.shape).astype(jnp.bfloat16))
    partial = most(pieces, trial_slab)
    once, once_round = call(
        functools.partial(first_kernel, last), (flat, rounded), [smem] * 2 + [vmem] * 3
    )(sources, columns, hamiltonian, partial, pieces[last])
    pieces = exchanged(once_round)
    partial = most(pieces, once, trial_slab)
    filtered, gram = call(
        functools.partial(second_kernel, last), (flat, parted), [smem] * 2 + [vmem] * 3
    )(sources, columns, hamiltonian, partial, pieces[last])
    gram = summed(gram)
    return call(
        functools.partial(factor_kernel, rows_total),
        (flat, square),
        [vmem, vmem],
        [pltpu.VMEM((states, states), jnp.float32)],
    )(gram, filtered)


def solution(mesh):
    placed = (
        P(("group", "blk"), None, None, None),
        P(("group", "blk"), None, None),
        P(("group", "blk")),
        P(("group", "blk"), None),
    )
    return jax.shard_map(
        on_device,
        mesh=mesh,
        in_specs=placed,
        out_specs=(P(("group", "blk"), None), P()),
        check_vma=False,
    )
```

```python
import functools

import jax
import jax.numpy as jnp
from jax import lax
from jax.experimental import pallas as pl
from jax.experimental.pallas import tpu as pltpu
from jax.sharding import PartitionSpec as P

precise = lax.Precision.HIGHEST
LANES = 128
SUB = 8
VMEM_LIMIT = 40 * 1024 * 1024
vmem = pl.BlockSpec(memory_space=pltpu.VMEM)
hbm = pl.BlockSpec(memory_space=pl.ANY)
smem = pl.BlockSpec(memory_space=pltpu.SMEM)


def pair_exchange(value, offset):
    count = lax.axis_size("group")
    route = []
    for low in range(offset, count - 1, 2):
        route += [(low, low + 1), (low + 1, low)]
    return lax.ppermute(value, "group", route)


def step_bits(group, level):
    levels = lax.axis_size("blk").bit_length() - 1
    return jnp.where(group % 2 == 1, levels - 1 - level, level)


def cycle_exchange(value, level):
    groups, cycle_size = lax.axis_size("group"), lax.axis_size("blk")
    levels = cycle_size.bit_length() - 1
    route = []
    for group in range(groups):
        bit = levels - 1 - level if group % 2 else level
        route += [
            (group * cycle_size + index, group * cycle_size + (index ^ 1 << bit))
            for index in range(cycle_size)
        ]
    return lax.ppermute(value, ("group", "blk"), route)


def on_odd_cores(value, axis, flip):
    groups, cycle_size = lax.axis_size("group"), lax.axis_size("blk")
    route = []
    for group in range(1, groups, 2):
        for index in range(cycle_size):
            if axis == "group":
                partner = (group ^ 2 * flip) * cycle_size + index
            else:
                partner = group * cycle_size + (index ^ flip)
            route.append((group * cycle_size + index, partner))
    return lax.ppermute(value, ("group", "blk"), route)


def summed(value):
    groups = lax.axis_size("group")
    odd = lax.axis_index("group") % 2 == 1
    up = [(group, group + 1) for group in range(0, groups - 1, 2)]
    down = [(target, source) for source, target in up]
    value = jnp.where(odd, value + lax.ppermute(value, "group", up), 0.0)
    for axis, count in (("group", groups // 2), ("blk", lax.axis_size("blk"))):
        step = 1
        while step < count:
            flips = [step, 2 * step, 3 * step] if 2 * step < count else [step]
            others = [on_odd_cores(value, axis, flip) for flip in flips]
            value = value + others[0]
            if len(others) == 3:
                value = value + (others[1] + others[2])
            step *= len(flips) + 1
    return value + lax.ppermute(value, "group", down)


def potential_columns(potential_ref):
    return jnp.transpose(potential_ref[...])


def couple_row(sources_ref, columns_ref, hamiltonian_ref, pieces, row):
    sources, per_source = hamiltonian_ref.shape[1], hamiltonian_ref.shape[3] // hamiltonian_ref.shape[2]
    total = None
    for index, piece_ref in pieces:
        source = sources_ref[index]
        first = (row * sources + source) * per_source
        picked = jnp.concatenate(
            [piece_ref[columns_ref[first + slot]] for slot in range(per_source)], axis=0
        )
        product = jnp.dot(
            hamiltonian_ref[row, source], picked, preferred_element_type=jnp.float32
        )
        total = product if total is None else total + product
    return total


def own_kernel(
    sources_ref, columns_ref, hamiltonian_ref, own_ref, potential_ref, scaled_ref, *refs
):
    less, partial_ref = refs[:-1], refs[-1]
    shard_blocks, _, block_size, _ = hamiltonian_ref.shape
    weights = potential_columns(potential_ref)
    per_column = LANES // block_size
    for row in range(shard_blocks):
        column, part = divmod(row, per_column)
        weight = weights[part * block_size : (part + 1) * block_size, column : column + 1]
        rows = pl.ds(row * block_size, block_size)
        total = weight * scaled_ref[rows, :]
        for less_ref in less:
            total = total - less_ref[rows, :]
        partial_ref[rows, :] = total + couple_row(
            sources_ref, columns_ref, hamiltonian_ref, [(0, own_ref)], row
        )


def middle_kernel(numbers, sources_ref, columns_ref, hamiltonian_ref, partial_ref, *refs):
    pieces, sum_ref = list(zip(numbers, refs[:-1])), refs[-1]
    shard_blocks, _, block_size, _ = hamiltonian_ref.shape
    for row in range(shard_blocks):
        rows = pl.ds(row * block_size, block_size)
        sum_ref[rows, :] = partial_ref[rows, :] + couple_row(
            sources_ref, columns_ref, hamiltonian_ref, pieces, row
        )


def first_kernel(
    number, sources_ref, columns_ref, hamiltonian_ref, partial_ref, piece_ref, once_ref, round_ref
):
    shard_blocks, _, block_size, _ = hamiltonian_ref.shape
    for row in range(shard_blocks):
        rows = pl.ds(row * block_size, block_size)
        once = 0.5 * (
            partial_ref[rows, :]
            + couple_row(sources_ref, columns_ref, hamiltonian_ref, [(number, piece_ref)], row)
        )
        once_ref[rows, :] = once
        round_ref[row] = once.astype(jnp.bfloat16)


def second_kernel(
    number, sources_ref, columns_ref, hamiltonian_ref, partial_ref, piece_ref,
    filtered_ref, packed_ref,
):
    shard_blocks, _, block_size, _ = hamiltonian_ref.shape
    for row in range(shard_blocks):
        rows = pl.ds(row * block_size, block_size)
        filtered_ref[rows, :] = partial_ref[rows, :] + couple_row(
            sources_ref, columns_ref, hamiltonian_ref, [(number, piece_ref)], row
        )
    flat = filtered_ref[...]
    gram = lax.dot_general(
        flat, flat, (((0,), (0,)), ((), ())), precision=precise,
        preferred_element_type=jnp.float32,
    )
    pack(gram, packed_ref)


def pack(gram, packed_ref):
    size = gram.shape[0]
    half = size // 2
    row = lax.broadcasted_iota(jnp.int32, (half, size), 0)
    lane = lax.broadcasted_iota(jnp.int32, (half, size), 1)
    lower = gram[half:, :]
    packed_ref[pl.ds(0, half), :] = jnp.where(lane < row, pltpu.roll(lower, half, 1), gram[:half, :])
    diagonal = jnp.sum(jnp.where(lane == row + half, lower, 0.0), axis=0, keepdims=True)
    packed_ref[pl.ds(half, SUB), :] = jnp.broadcast_to(diagonal, (SUB, size))


def unpack(packed_ref):
    size = packed_ref.shape[1]
    half = size // 2
    row = lax.broadcasted_iota(jnp.int32, (size, size), 0)
    lane = lax.broadcasted_iota(jnp.int32, (size, size), 1)
    upper = packed_ref[pl.ds(0, half), :]
    both = jnp.concatenate([upper, pltpu.roll(upper, half, 1)], axis=0)
    held = ((row < half) & (lane > row)) | ((row >= half) & (lane >= half) & (lane < row))
    off_diagonal = jnp.where(held, both, 0.0)
    diagonal = jnp.where(row < half, both, packed_ref[pl.ds(half, 1), :])
    return off_diagonal + jnp.transpose(off_diagonal) + jnp.where(row == lane, diagonal, 0.0)


def inverse_of(value):
    estimate = pl.reciprocal(value, approx=True)
    estimate = estimate * (2.0 - value * estimate)
    return estimate * (2.0 - value * estimate)


def factor(gram, upper_ref, inverse_ref):
    size = gram.shape[1]
    panels = size // SUB
    shape = (SUB, size)
    row_index = lax.broadcasted_iota(jnp.int32, shape, 0)
    lane_index = lax.broadcasted_iota(jnp.int32, shape, 1)

    def along_lanes(panel, first):
        return [jnp.broadcast_to(panel[:, first + c : first + c + 1], shape) for c in range(SUB)]

    def along_rows(panel, row):
        return jnp.broadcast_to(panel[row : row + 1, :], shape)

    held = [gram[k * SUB : (k + 1) * SUB, :] for k in range(panels)]
    block = along_lanes(held[0], 0)
    for k in range(panels):
        first = k * SUB
        below = {p: along_lanes(held[p], first) for p in range(k + 1, panels)}
        after = list(below[k + 1]) if k + 1 < panels else None
        following = along_lanes(held[k + 1], first + SUB) if k + 1 < panels else None
        right = jnp.where(lane_index >= first, held[k], 0.0)
        left = jnp.where(
            lane_index < first, held[k], jnp.where(lane_index == row_index + first, 1.0, 0.0)
        )
        pivots = jnp.ones(shape, jnp.float32)
        reciprocals = jnp.ones(shape, jnp.float32)
        for j in range(0, SUB, 2):
            a, b, c = along_rows(block[j], j), along_rows(block[j], j + 1), along_rows(block[j + 1], j + 1)
            determinant = a * c - b * b
            over = inverse_of(determinant)
            over_a = inverse_of(a)
            shift = b * over_a
            pivots = jnp.where(row_index == j, a, pivots)
            pivots = jnp.where(row_index == j + 1, determinant * over_a, pivots)
            reciprocals = jnp.where(row_index == j, over_a, reciprocals)
            reciprocals = jnp.where(row_index == j + 1, a * over, reciprocals)
            x, y = block[j], block[j + 1]
            one = jnp.where(row_index > j + 1, (x * c - y * b) * over, jnp.where(row_index == j + 1, shift, 0.0))
            two = jnp.where(row_index > j + 1, (y * a - x * b) * over, 0.0)
            upper = {n: (along_rows(block[n], j), along_rows(block[n], j + 1)) for n in range(j + 2, SUB)}
            for n in upper:
                block[n] = block[n] - one * upper[n][0] - two * upper[n][1]
            if following is not None:
                x, y = after[j], after[j + 1]
                next_one, next_two = (x * c - y * b) * over, (y * a - x * b) * over
                for n in range(SUB):
                    following[n] = following[n] - next_one * along_rows(x, n) - next_two * along_rows(y, n)
                for n in upper:
                    after[n] = after[n] - next_one * upper[n][0] - next_two * upper[n][1]
            right = right - one * along_rows(right, j) - two * along_rows(right, j + 1)
            left = left - one * along_rows(left, j) - two * along_rows(left, j + 1)
        scale = lax.rsqrt(pivots)
        upper_ref[pl.ds(first, SUB), :] = jnp.where(lane_index >= row_index + first, right * scale, 0.0)
        inverse_ref[pl.ds(first, SUB), :] = left * scale
        if k + 1 < panels:
            reduced = jnp.where(lane_index >= first + SUB, right, left) * reciprocals
            for n in range(SUB - 1, 0, -1):
                column = jnp.where(row_index < n, block[n] * reciprocals, 0.0)
                reduced = reduced - column * along_rows(reduced, n)
            rows = [along_rows(reduced, n) for n in range(SUB)]
            inside = (lane_index >= first) & (lane_index < first + SUB)
            for p in below:
                total = jnp.where(inside, 0.0, held[p])
                for n in range(SUB):
                    total = total - below[p][n] * rows[n]
                held[p] = total
        block = following


def two_parts(value):
    high = value.astype(jnp.bfloat16)
    return high, (value - high.astype(jnp.float32)).astype(jnp.bfloat16)


def factor_kernel(
    rows_total, packed_ref, filtered_ref, ortho_hbm, upper_hbm,
    upper_ref, inverse_ref, ortho_ref, sent, upper_sent,
):
    factor(unpack(packed_ref) * (1.0 / rows_total), upper_ref, inverse_ref)
    copies = [pltpu.make_async_copy(upper_ref, upper_hbm, upper_sent)]
    copies[0].start()
    high, low = two_parts(inverse_ref[...])
    right = jnp.concatenate([high, high, low], axis=1)
    chunks = sent.shape[0]
    per_chunk = filtered_ref.shape[0] // chunks
    for chunk in range(chunks):
        rows = pl.ds(chunk * per_chunk, per_chunk)
        high, low = two_parts(filtered_ref[rows, :])
        ortho_ref[rows, :] = lax.dot_general(
            jnp.concatenate([high, low, high], axis=1), right, (((1,), (1,)), ((), ())),
            preferred_element_type=jnp.float32,
        )
        copies.append(
            pltpu.make_async_copy(ortho_ref.at[rows, :], ortho_hbm.at[rows, :], sent.at[chunk])
        )
        copies[-1].start()
    for copy in copies:
        copy.wait()


def call(kernel, out_shape, in_specs, scratch=(), out_spec=vmem):
    return pl.pallas_call(
        kernel,
        out_shape=out_shape,
        in_specs=in_specs,
        out_specs=jax.tree.map(lambda _: out_spec, out_shape),
        scratch_shapes=list(scratch),
        compiler_params=pltpu.CompilerParams(vmem_limit_bytes=VMEM_LIMIT),
    )


def on_device(hamiltonian, block_columns, potential, trial_slab):
    shard_blocks, _, block_size, _ = hamiltonian.shape
    flat_rows, states = trial_slab.shape
    columns = block_columns.reshape(-1)
    weights = potential.reshape(-1, LANES)
    rows_total = flat_rows * lax.axis_size("group") * lax.axis_size("blk")
    group, index = lax.axis_index("group"), lax.axis_index("blk")
    cycle_size = lax.axis_size("blk")
    levels = cycle_size.bit_length() - 1
    origins = [index]
    for level in range(levels):
        flip = jnp.left_shift(1, step_bits(group, level))
        origins += [jnp.bitwise_xor(origin, flip) for origin in origins]
    odd = group % 2
    origins += [cycle_size + 1 - odd, cycle_size + odd]
    sources = jnp.stack(origins).astype(jnp.int32)
    last = cycle_size - 1
    middle = list(range(1, last)) + [cycle_size + 1, cycle_size]
    flat = jax.ShapeDtypeStruct((flat_rows, states), jnp.float32)
    rounded = jax.ShapeDtypeStruct((shard_blocks, block_size, states), jnp.bfloat16)
    packed = jax.ShapeDtypeStruct((states // 2 + SUB, states), jnp.float32)
    square = jax.ShapeDtypeStruct((states, states), jnp.float32)

    def exchanged(value):
        pairs = [pair_exchange(value, 0), pair_exchange(value, 1)]
        pieces = [value]
        for level in range(levels):
            pieces += [cycle_exchange(piece, level) for piece in pieces]
        return pieces + pairs

    def most(pieces, *terms):
        own = call(own_kernel, flat, [smem] * 2 + [vmem] * (3 + len(terms)))(
            sources, columns, hamiltonian, pieces[0], weights, *terms
        )
        return call(
            functools.partial(middle_kernel, middle), flat,
            [smem] * 2 + [vmem] * (2 + len(middle)),
        )(sources, columns, hamiltonian, own, *[pieces[number] for number in middle])

    pieces = exchanged(trial_slab.reshape(rounded.shape).astype(jnp.bfloat16))
    partial = most(pieces, trial_slab)
    once, once_round = call(
        functools.partial(first_kernel, last), (flat, rounded), [smem] * 2 + [vmem] * 3
    )(sources, columns, hamiltonian, partial, pieces[last])
    pieces = exchanged(once_round)
    partial = most(pieces, once, trial_slab)
    filtered, gram = call(
        functools.partial(second_kernel, last), (flat, packed), [smem] * 2 + [vmem] * 3
    )(sources, columns, hamiltonian, partial, pieces[last])
    gram = summed(gram)
    return call(
        functools.partial(factor_kernel, rows_total),
        (flat, square),
        [vmem, vmem],
        [
            pltpu.VMEM((states, states), jnp.float32),
            pltpu.VMEM((states, states), jnp.float32),
            pltpu.VMEM((flat_rows, states), jnp.float32),
            pltpu.SemaphoreType.DMA((4,)),
            pltpu.SemaphoreType.DMA,
        ],
        hbm,
    )(gram, filtered)


def solution(mesh):
    placed = (
        P(("group", "blk"), None, None, None),
        P(("group", "blk"), None, None),
        P(("group", "blk")),
        P(("group", "blk"), None),
    )
    return jax.shard_map(
        on_device,
        mesh=mesh,
        in_specs=placed,
        out_specs=(P(("group", "blk"), None), P()),
        check_vma=False,
    )
```

```python
import functools

import jax
import jax.numpy as jnp
from jax import lax
from jax.experimental import pallas as pl
from jax.experimental.pallas import tpu as pltpu
from jax.sharding import PartitionSpec as P

precise = lax.Precision.HIGHEST
LANES = 128
SUB = 8
OUTER = 4
VMEM_LIMIT = 40 * 1024 * 1024
vmem = pl.BlockSpec(memory_space=pltpu.VMEM)
hbm = pl.BlockSpec(memory_space=pl.ANY)
smem = pl.BlockSpec(memory_space=pltpu.SMEM)


def pair_exchange(value, offset):
    count = lax.axis_size("group")
    route = {group: group for group in range(count)}
    for low in range(offset, count - 1, 2):
        route[low], route[low + 1] = low + 1, low
    return lax.ppermute(value, "group", list(route.items()))


def step_bits(group, level):
    levels = lax.axis_size("blk").bit_length() - 1
    return jnp.where(group % 2 == 1, levels - 1 - level, level)


def cycle_exchange(value, level):
    groups, cycle_size = lax.axis_size("group"), lax.axis_size("blk")
    levels = cycle_size.bit_length() - 1
    route = []
    for group in range(groups):
        bit = levels - 1 - level if group % 2 else level
        route += [
            (group * cycle_size + index, group * cycle_size + (index ^ 1 << bit))
            for index in range(cycle_size)
        ]
    return lax.ppermute(value, ("group", "blk"), route)


def on_odd_cores(value, axis, flip):
    groups, cycle_size = lax.axis_size("group"), lax.axis_size("blk")
    route = []
    for group in range(groups):
        for index in range(cycle_size):
            partner = (group, index)
            if group % 2 == 1:
                partner = (group ^ 2 * flip, index) if axis == "group" else (group, index ^ flip)
            route.append((group * cycle_size + index, partner[0] * cycle_size + partner[1]))
    return lax.ppermute(value, ("group", "blk"), route)


def summed(value):
    groups = lax.axis_size("group")
    value = value + pair_exchange(value, 0)
    for axis, count in (("group", groups // 2), ("blk", lax.axis_size("blk"))):
        step = 1
        while step < count:
            flips = [step, 2 * step, 3 * step] if 2 * step < count else [step]
            others = [on_odd_cores(value, axis, flip) for flip in flips]
            value = value + others[0]
            if len(others) == 3:
                value = value + (others[1] + others[2])
            step *= len(flips) + 1
    return jnp.where(lax.axis_index("group") % 2 == 1, value, pair_exchange(value, 0))


def potential_columns(potential_ref):
    return jnp.transpose(potential_ref[...])


def couple_row(sources_ref, columns_ref, hamiltonian_ref, pieces, row):
    sources, per_source = hamiltonian_ref.shape[1], hamiltonian_ref.shape[3] // hamiltonian_ref.shape[2]
    total = None
    for index, piece_ref in pieces:
        source = sources_ref[index]
        first = (row * sources + source) * per_source
        picked = jnp.concatenate(
            [piece_ref[columns_ref[first + slot]] for slot in range(per_source)], axis=0
        )
        product = jnp.dot(
            hamiltonian_ref[row, source], picked, preferred_element_type=jnp.float32
        )
        if index == sources - 1:
            absent = sources_ref[sources] == index
            product = jnp.where(absent, 0.0, product)
        total = product if total is None else total + product
    return total


def own_kernel(
    sources_ref, columns_ref, hamiltonian_ref, own_ref, potential_ref, scaled_ref, *refs
):
    less, partial_ref = refs[:-1], refs[-1]
    shard_blocks, _, block_size, _ = hamiltonian_ref.shape
    weights = potential_columns(potential_ref)
    per_column = LANES // block_size
    for row in range(shard_blocks):
        column, part = divmod(row, per_column)
        weight = weights[part * block_size : (part + 1) * block_size, column : column + 1]
        rows = pl.ds(row * block_size, block_size)
        total = weight * scaled_ref[rows, :]
        for less_ref in less:
            total = total - less_ref[rows, :]
        partial_ref[rows, :] = total + couple_row(
            sources_ref, columns_ref, hamiltonian_ref, [(0, own_ref)], row
        )


def middle_kernel(numbers, sources_ref, columns_ref, hamiltonian_ref, partial_ref, *refs):
    pieces, sum_ref = list(zip(numbers, refs[:-1])), refs[-1]
    shard_blocks, _, block_size, _ = hamiltonian_ref.shape
    for row in range(shard_blocks):
        rows = pl.ds(row * block_size, block_size)
        sum_ref[rows, :] = partial_ref[rows, :] + couple_row(
            sources_ref, columns_ref, hamiltonian_ref, pieces, row
        )


def first_kernel(
    number, sources_ref, columns_ref, hamiltonian_ref, partial_ref, piece_ref, once_ref, round_ref
):
    shard_blocks, _, block_size, _ = hamiltonian_ref.shape
    for row in range(shard_blocks):
        rows = pl.ds(row * block_size, block_size)
        once = 0.5 * (
            partial_ref[rows, :]
            + couple_row(sources_ref, columns_ref, hamiltonian_ref, [(number, piece_ref)], row)
        )
        once_ref[rows, :] = once
        round_ref[row] = once.astype(jnp.bfloat16)


def second_kernel(
    number, sources_ref, columns_ref, hamiltonian_ref, partial_ref, piece_ref,
    filtered_ref, packed_ref,
):
    shard_blocks, _, block_size, _ = hamiltonian_ref.shape
    for row in range(shard_blocks):
        rows = pl.ds(row * block_size, block_size)
        filtered_ref[rows, :] = partial_ref[rows, :] + couple_row(
            sources_ref, columns_ref, hamiltonian_ref, [(number, piece_ref)], row
        )
    flat = filtered_ref[...]
    gram = lax.dot_general(
        flat, flat, (((0,), (0,)), ((), ())), precision=precise,
        preferred_element_type=jnp.float32,
    )
    pack(gram, packed_ref)


def pack(gram, packed_ref):
    size = gram.shape[0]
    half = size // 2
    row = lax.broadcasted_iota(jnp.int32, (half, size), 0)
    lane = lax.broadcasted_iota(jnp.int32, (half, size), 1)
    lower = gram[half:, :]
    packed_ref[pl.ds(0, half), :] = jnp.where(lane < row, pltpu.roll(lower, half, 1), gram[:half, :])
    diagonal = jnp.sum(jnp.where(lane == row + half, lower, 0.0), axis=0, keepdims=True)
    packed_ref[pl.ds(half, SUB), :] = jnp.broadcast_to(diagonal, (SUB, size))


def unpack(packed_ref):
    size = packed_ref.shape[1]
    half = size // 2
    row = lax.broadcasted_iota(jnp.int32, (size, size), 0)
    lane = lax.broadcasted_iota(jnp.int32, (size, size), 1)
    upper = packed_ref[pl.ds(0, half), :]
    both = jnp.concatenate([upper, pltpu.roll(upper, half, 1)], axis=0)
    held = ((row < half) & (lane > row)) | ((row >= half) & (lane >= half) & (lane < row))
    off_diagonal = jnp.where(held, both, 0.0)
    diagonal = jnp.where(row < half, both, packed_ref[pl.ds(half, 1), :])
    return off_diagonal + jnp.transpose(off_diagonal) + jnp.where(row == lane, diagonal, 0.0)


def inverse_of(value):
    estimate = pl.reciprocal(value, approx=True)
    estimate = estimate * (2.0 - value * estimate)
    return estimate * (2.0 - value * estimate)


def factor(gram, upper_ref, inverse_ref):
    size = gram.shape[1]
    panels = size // SUB
    shape = (SUB, size)
    row_index = lax.broadcasted_iota(jnp.int32, shape, 0)
    lane_index = lax.broadcasted_iota(jnp.int32, shape, 1)

    def along_lanes(panel, first):
        return [jnp.broadcast_to(panel[:, first + c : first + c + 1], shape) for c in range(SUB)]

    def along_rows(panel, row):
        return jnp.broadcast_to(panel[row : row + 1, :], shape)

    def between(low, high):
        return (lane_index >= low) & (lane_index < high)

    held = [gram[k * SUB : (k + 1) * SUB, :] for k in range(panels)]
    for outer in range(0, panels, OUTER):
        end = outer + OUTER
        rows_then, rows_reduced = [], []
        block = along_lanes(held[outer], outer * SUB)
        for k in range(outer, end):
            first = k * SUB
            below = {p: along_lanes(held[p], first) for p in range(k + 1, end)}
            after = list(below[k + 1]) if k + 1 < end else None
            following = along_lanes(held[k + 1], first + SUB) if k + 1 < end else None
            right = held[k]
            left = jnp.where(
                lane_index < first, held[k], jnp.where(lane_index == row_index + first, 1.0, 0.0)
            )
            pivots = jnp.ones(shape, jnp.float32)
            reciprocals = jnp.ones(shape, jnp.float32)
            for j in range(0, SUB, 2):
                a, b = along_rows(block[j], j), along_rows(block[j], j + 1)
                c = along_rows(block[j + 1], j + 1)
                determinant = a * c - b * b
                over = inverse_of(determinant)
                over_a = inverse_of(a)
                pivots = jnp.where(row_index == j, a, pivots)
                pivots = jnp.where(row_index == j + 1, determinant * over_a, pivots)
                reciprocals = jnp.where(row_index == j, over_a, reciprocals)
                reciprocals = jnp.where(row_index == j + 1, a * over, reciprocals)
                x, y = block[j], block[j + 1]
                one = jnp.where(row_index == j + 1, b * over_a, 0.0)
                one = jnp.where(row_index > j + 1, (x * c - y * b) * over, one)
                two = jnp.where(row_index > j + 1, (y * a - x * b) * over, 0.0)
                upper = {
                    n: (along_rows(block[n], j), along_rows(block[n], j + 1))
                    for n in range(j + 2, SUB)
                }
                for n in upper:
                    block[n] = block[n] - one * upper[n][0] - two * upper[n][1]
                if following is not None:
                    x, y = after[j], after[j + 1]
                    next_one, next_two = (x * c - y * b) * over, (y * a - x * b) * over
                    for n in range(SUB):
                        following[n] = (
                            following[n] - next_one * along_rows(x, n) - next_two * along_rows(y, n)
                        )
                    for n in upper:
                        after[n] = after[n] - next_one * upper[n][0] - next_two * upper[n][1]
                right = right - one * along_rows(right, j) - two * along_rows(right, j + 1)
                left = left - one * along_rows(left, j) - two * along_rows(left, j + 1)
            scale = lax.rsqrt(pivots)
            upper_ref[pl.ds(first, SUB), :] = jnp.where(
                lane_index >= row_index + first, right * scale, 0.0
            )
            inverse_ref[pl.ds(first, SUB), :] = left * scale
            if k + 1 < panels:
                reduced = jnp.where(lane_index >= first + SUB, right, left) * reciprocals
                for n in range(SUB - 1, 0, -1):
                    column = jnp.where(row_index < n, block[n] * reciprocals, 0.0)
                    reduced = reduced - column * along_rows(reduced, n)
                rows_then.append(held[k])
                rows_reduced.append(jnp.where(between(first + SUB, end * SUB), 0.0, reduced))
                rows = [along_rows(reduced, n) for n in range(SUB)]
                for p in below:
                    total = jnp.where(between(first, first + SUB), 0.0, held[p])
                    for n in range(SUB):
                        total = total - below[p][n] * rows[n]
                    held[p] = total
            block = following
        if end < panels:
            change = lax.dot_general(
                jnp.concatenate(rows_then, axis=0), jnp.concatenate(rows_reduced, axis=0),
                (((0,), (0,)), ((), ())), precision=precise, preferred_element_type=jnp.float32,
            )
            for p in range(end, panels):
                kept = jnp.where(between(outer * SUB, end * SUB), 0.0, held[p])
                held[p] = kept - change[p * SUB : (p + 1) * SUB, :]


def two_parts(value):
    high = value.astype(jnp.bfloat16)
    return high, (value - high.astype(jnp.float32)).astype(jnp.bfloat16)


def factor_kernel(
    rows_total, packed_ref, filtered_ref, ortho_hbm, upper_hbm,
    upper_ref, inverse_ref, ortho_ref, sent, upper_sent,
):
    factor(unpack(packed_ref) * (1.0 / rows_total), upper_ref, inverse_ref)
    copies = [pltpu.make_async_copy(upper_ref, upper_hbm, upper_sent)]
    copies[0].start()
    high, low = two_parts(inverse_ref[...])
    right = jnp.concatenate([high, high, low], axis=1)
    chunks = sent.shape[0]
    per_chunk = filtered_ref.shape[0] // chunks
    for chunk in range(chunks):
        rows = pl.ds(chunk * per_chunk, per_chunk)
        high, low = two_parts(filtered_ref[rows, :])
        ortho_ref[rows, :] = lax.dot_general(
            jnp.concatenate([high, low, high], axis=1), right, (((1,), (1,)), ((), ())),
            preferred_element_type=jnp.float32,
        )
        copies.append(
            pltpu.make_async_copy(ortho_ref.at[rows, :], ortho_hbm.at[rows, :], sent.at[chunk])
        )
        copies[-1].start()
    for copy in copies:
        copy.wait()


def call(kernel, out_shape, in_specs, scratch=(), out_spec=vmem):
    return pl.pallas_call(
        kernel,
        out_shape=out_shape,
        in_specs=in_specs,
        out_specs=jax.tree.map(lambda _: out_spec, out_shape),
        scratch_shapes=list(scratch),
        compiler_params=pltpu.CompilerParams(vmem_limit_bytes=VMEM_LIMIT),
    )


def on_device(hamiltonian, block_columns, potential, trial_slab):
    shard_blocks, _, block_size, _ = hamiltonian.shape
    flat_rows, states = trial_slab.shape
    columns = block_columns.reshape(-1)
    weights = potential.reshape(-1, LANES)
    rows_total = flat_rows * lax.axis_size("group") * lax.axis_size("blk")
    group, index = lax.axis_index("group"), lax.axis_index("blk")
    cycle_size = lax.axis_size("blk")
    levels = cycle_size.bit_length() - 1
    origins = [index]
    for level in range(levels):
        flip = jnp.left_shift(1, step_bits(group, level))
        origins += [jnp.bitwise_xor(origin, flip) for origin in origins]
    odd = group % 2
    origins += [cycle_size + 1 - odd, cycle_size + odd]
    alone = (group == 0) | (group == lax.axis_size("group") - 1)
    origins.append(jnp.where(alone, cycle_size + 1, -1))
    sources = jnp.stack(origins).astype(jnp.int32)
    last = cycle_size - 1
    middle = list(range(1, last)) + [cycle_size + 1, cycle_size]
    flat = jax.ShapeDtypeStruct((flat_rows, states), jnp.float32)
    rounded = jax.ShapeDtypeStruct((shard_blocks, block_size, states), jnp.bfloat16)
    packed = jax.ShapeDtypeStruct((states // 2 + SUB, states), jnp.float32)
    square = jax.ShapeDtypeStruct((states, states), jnp.float32)

    def exchanged(value):
        pairs = [pair_exchange(value, 0), pair_exchange(value, 1)]
        pieces = [value]
        for level in range(levels):
            pieces += [cycle_exchange(piece, level) for piece in pieces]
        return pieces + pairs

    def most(pieces, *terms):
        own = call(own_kernel, flat, [smem] * 2 + [vmem] * (3 + len(terms)))(
            sources, columns, hamiltonian, pieces[0], weights, *terms
        )
        return call(
            functools.partial(middle_kernel, middle), flat,
            [smem] * 2 + [vmem] * (2 + len(middle)),
        )(sources, columns, hamiltonian, own, *[pieces[number] for number in middle])

    pieces = exchanged(trial_slab.reshape(rounded.shape).astype(jnp.bfloat16))
    partial = most(pieces, trial_slab)
    once, once_round = call(
        functools.partial(first_kernel, last), (flat, rounded), [smem] * 2 + [vmem] * 3
    )(sources, columns, hamiltonian, partial, pieces[last])
    pieces = exchanged(once_round)
    partial = most(pieces, once, trial_slab)
    filtered, gram = call(
        functools.partial(second_kernel, last), (flat, packed), [smem] * 2 + [vmem] * 3
    )(sources, columns, hamiltonian, partial, pieces[last])
    gram = summed(gram)
    return call(
        functools.partial(factor_kernel, rows_total),
        (flat, square),
        [vmem, vmem],
        [
            pltpu.VMEM((states, states), jnp.float32),
            pltpu.VMEM((states, states), jnp.float32),
            pltpu.VMEM((flat_rows, states), jnp.float32),
            pltpu.SemaphoreType.DMA((4,)),
            pltpu.SemaphoreType.DMA,
        ],
        hbm,
    )(gram, filtered)


def solution(mesh):
    placed = (
        P(("group", "blk"), None, None, None),
        P(("group", "blk"), None, None),
        P(("group", "blk")),
        P(("group", "blk"), None),
    )
    return jax.shard_map(
        on_device,
        mesh=mesh,
        in_specs=placed,
        out_specs=(P(("group", "blk"), None), P()),
        check_vma=False,
    )
```

```python
import functools

import jax
import jax.numpy as jnp
from jax import lax
from jax.experimental import pallas as pl
from jax.experimental.pallas import tpu as pltpu
from jax.sharding import PartitionSpec as P

precise = lax.Precision.HIGHEST
LANES = 128
SUB = 8
OUTER = 4
VMEM_LIMIT = 40 * 1024 * 1024
vmem = pl.BlockSpec(memory_space=pltpu.VMEM)
hbm = pl.BlockSpec(memory_space=pl.ANY)
smem = pl.BlockSpec(memory_space=pltpu.SMEM)


def pair_exchange(value, offset):
    count = lax.axis_size("group")
    route = []
    for low in range(offset, count + offset, 2):
        first, second = low % count, (low + 1) % count
        route += [(first, second), (second, first)]
    return lax.ppermute(value, "group", route)


def step_bits(group, level):
    levels = lax.axis_size("blk").bit_length() - 1
    return jnp.where(group % 2 == 1, levels - 1 - level, level)


def cycle_exchange(value, level):
    groups, cycle_size = lax.axis_size("group"), lax.axis_size("blk")
    levels = cycle_size.bit_length() - 1
    route = []
    for group in range(groups):
        bit = levels - 1 - level if group % 2 else level
        route += [
            (group * cycle_size + index, group * cycle_size + (index ^ 1 << bit))
            for index in range(cycle_size)
        ]
    return lax.ppermute(value, ("group", "blk"), route)


def from_partner(value, axis, flip):
    count = lax.axis_size(axis)
    return lax.ppermute(value, axis, [(index, index ^ flip) for index in range(count)])


def summed(value):
    for axis, step in (("group", 1), ("group", 2), ("blk", 1)):
        count = 2 if (axis, step) == ("group", 1) else lax.axis_size(axis)
        while step < count:
            flips = [step, 2 * step, 3 * step] if 2 * step < count else [step]
            others = [from_partner(value, axis, flip) for flip in flips]
            value = value + others[0]
            if len(others) == 3:
                value = value + (others[1] + others[2])
            step *= len(flips) + 1
    return value


def potential_columns(potential_ref):
    return jnp.transpose(potential_ref[...])


def couple_row(sources_ref, columns_ref, hamiltonian_ref, pieces, row):
    sources, per_source = hamiltonian_ref.shape[1], hamiltonian_ref.shape[3] // hamiltonian_ref.shape[2]
    total = None
    for index, piece_ref in pieces:
        source = sources_ref[index]
        first = (row * sources + source) * per_source
        picked = jnp.concatenate(
            [piece_ref[columns_ref[first + slot]] for slot in range(per_source)], axis=0
        )
        product = jnp.dot(
            hamiltonian_ref[row, source], picked, preferred_element_type=jnp.float32
        )
        if index == sources - 1:
            absent = sources_ref[sources] == index
            product = jnp.where(absent, 0.0, product)
        total = product if total is None else total + product
    return total


def own_kernel(sources_ref, columns_ref, hamiltonian_ref, own_ref, *refs):
    terms, partial_ref = refs[:-1], refs[-1]
    shard_blocks, _, block_size, _ = hamiltonian_ref.shape
    per_column = LANES // block_size
    if len(terms) == 3:
        weights = potential_columns(terms[0])
    for row in range(shard_blocks):
        rows = pl.ds(row * block_size, block_size)
        if len(terms) == 3:
            column, part = divmod(row, per_column)
            weight = weights[part * block_size : (part + 1) * block_size, column : column + 1]
            total = weight * terms[1][rows, :] - terms[2][rows, :]
        else:
            total = terms[0][rows, :]
        partial_ref[rows, :] = total + couple_row(
            sources_ref, columns_ref, hamiltonian_ref, [(0, own_ref)], row
        )


def middle_kernel(numbers, sources_ref, columns_ref, hamiltonian_ref, partial_ref, *refs):
    pieces, sum_ref = list(zip(numbers, refs[:-1])), refs[-1]
    shard_blocks, _, block_size, _ = hamiltonian_ref.shape
    for row in range(shard_blocks):
        rows = pl.ds(row * block_size, block_size)
        sum_ref[rows, :] = partial_ref[rows, :] + couple_row(
            sources_ref, columns_ref, hamiltonian_ref, pieces, row
        )


def first_kernel(
    number, sources_ref, columns_ref, hamiltonian_ref, partial_ref, piece_ref, once_ref, round_ref
):
    shard_blocks, _, block_size, _ = hamiltonian_ref.shape
    for row in range(shard_blocks):
        rows = pl.ds(row * block_size, block_size)
        once = 0.5 * (
            partial_ref[rows, :]
            + couple_row(sources_ref, columns_ref, hamiltonian_ref, [(number, piece_ref)], row)
        )
        once_ref[rows, :] = once
        round_ref[row] = once.astype(jnp.bfloat16)


def second_kernel(
    number, sources_ref, columns_ref, hamiltonian_ref, partial_ref, piece_ref,
    filtered_ref, packed_ref,
):
    shard_blocks, _, block_size, _ = hamiltonian_ref.shape
    for row in range(shard_blocks):
        rows = pl.ds(row * block_size, block_size)
        filtered_ref[rows, :] = partial_ref[rows, :] + couple_row(
            sources_ref, columns_ref, hamiltonian_ref, [(number, piece_ref)], row
        )
    flat = filtered_ref[...]
    gram = lax.dot_general(
        flat, flat, (((0,), (0,)), ((), ())), precision=precise,
        preferred_element_type=jnp.float32,
    )
    pack(gram, packed_ref)


def pack(gram, packed_ref):
    size = gram.shape[0]
    half = size // 2
    row = lax.broadcasted_iota(jnp.int32, (half, size), 0)
    lane = lax.broadcasted_iota(jnp.int32, (half, size), 1)
    lower = gram[half:, :]
    packed_ref[pl.ds(0, half), :] = jnp.where(lane < row, pltpu.roll(lower, half, 1), gram[:half, :])
    diagonal = jnp.sum(jnp.where(lane == row + half, lower, 0.0), axis=0, keepdims=True)
    packed_ref[pl.ds(half, SUB), :] = jnp.broadcast_to(diagonal, (SUB, size))


def unpack(packed_ref):
    size = packed_ref.shape[1]
    half = size // 2
    row = lax.broadcasted_iota(jnp.int32, (size, size), 0)
    lane = lax.broadcasted_iota(jnp.int32, (size, size), 1)
    upper = packed_ref[pl.ds(0, half), :]
    both = jnp.concatenate([upper, pltpu.roll(upper, half, 1)], axis=0)
    held = ((row < half) & (lane > row)) | ((row >= half) & (lane >= half) & (lane < row))
    off_diagonal = jnp.where(held, both, 0.0)
    diagonal = jnp.where(row < half, both, packed_ref[pl.ds(half, 1), :])
    return off_diagonal + jnp.transpose(off_diagonal) + jnp.where(row == lane, diagonal, 0.0)


def inverse_of(value):
    estimate = pl.reciprocal(value, approx=True)
    estimate = estimate * (2.0 - value * estimate)
    return estimate * (2.0 - value * estimate)


def factor(gram, upper_ref, inverse_ref):
    size = gram.shape[1]
    panels = size // SUB
    shape = (SUB, size)
    row_index = lax.broadcasted_iota(jnp.int32, shape, 0)
    lane_index = lax.broadcasted_iota(jnp.int32, shape, 1)

    def along_lanes(panel, first):
        return [jnp.broadcast_to(panel[:, first + c : first + c + 1], shape) for c in range(SUB)]

    def along_rows(panel, row):
        return jnp.broadcast_to(panel[row : row + 1, :], shape)

    def between(low, high):
        return (lane_index >= low) & (lane_index < high)

    held = [gram[k * SUB : (k + 1) * SUB, :] for k in range(panels)]
    for outer in range(0, panels, OUTER):
        end = outer + OUTER
        rows_then, rows_reduced = [], []
        block = along_lanes(held[outer], outer * SUB)
        for k in range(outer, end):
            first = k * SUB
            below = {p: along_lanes(held[p], first) for p in range(k + 1, end)}
            after = list(below[k + 1]) if k + 1 < end else None
            following = along_lanes(held[k + 1], first + SUB) if k + 1 < end else None
            right = held[k]
            left = jnp.where(
                lane_index < first, held[k], jnp.where(lane_index == row_index + first, 1.0, 0.0)
            )
            pivots = jnp.ones(shape, jnp.float32)
            reciprocals = jnp.ones(shape, jnp.float32)
            for j in range(0, SUB, 2):
                a, b = along_rows(block[j], j), along_rows(block[j], j + 1)
                c = along_rows(block[j + 1], j + 1)
                determinant = a * c - b * b
                over = inverse_of(determinant)
                over_a = inverse_of(a)
                pivots = jnp.where(row_index == j, a, pivots)
                pivots = jnp.where(row_index == j + 1, determinant * over_a, pivots)
                reciprocals = jnp.where(row_index == j, over_a, reciprocals)
                reciprocals = jnp.where(row_index == j + 1, a * over, reciprocals)
                x, y = block[j], block[j + 1]
                one = jnp.where(row_index == j + 1, b * over_a, 0.0)
                one = jnp.where(row_index > j + 1, (x * c - y * b) * over, one)
                two = jnp.where(row_index > j + 1, (y * a - x * b) * over, 0.0)
                upper = {
                    n: (along_rows(block[n], j), along_rows(block[n], j + 1))
                    for n in range(j + 2, SUB)
                }
                for n in upper:
                    block[n] = block[n] - one * upper[n][0] - two * upper[n][1]
                if following is not None:
                    x, y = after[j], after[j + 1]
                    next_one, next_two = (x * c - y * b) * over, (y * a - x * b) * over
                    for n in range(SUB):
                        following[n] = (
                            following[n] - next_one * along_rows(x, n) - next_two * along_rows(y, n)
                        )
                    for n in upper:
                        after[n] = after[n] - next_one * upper[n][0] - next_two * upper[n][1]
                right = right - one * along_rows(right, j) - two * along_rows(right, j + 1)
                left = left - one * along_rows(left, j) - two * along_rows(left, j + 1)
            scale = lax.rsqrt(pivots)
            upper_ref[pl.ds(first, SUB), :] = jnp.where(
                lane_index >= row_index + first, right * scale, 0.0
            )
            inverse_ref[pl.ds(first, SUB), :] = left * scale
            if k + 1 < panels:
                reduced = jnp.where(lane_index >= first + SUB, right, left) * reciprocals
                for n in range(SUB - 1, 0, -1):
                    column = jnp.where(row_index < n, block[n] * reciprocals, 0.0)
                    reduced = reduced - column * along_rows(reduced, n)
                rows_then.append(held[k])
                rows_reduced.append(jnp.where(between(first + SUB, end * SUB), 0.0, reduced))
                rows = [along_rows(reduced, n) for n in range(SUB)]
                for p in below:
                    total = jnp.where(between(first, first + SUB), 0.0, held[p])
                    for n in range(SUB):
                        total = total - below[p][n] * rows[n]
                    held[p] = total
            block = following
        if end < panels:
            change = lax.dot_general(
                jnp.concatenate(rows_then, axis=0), jnp.concatenate(rows_reduced, axis=0),
                (((0,), (0,)), ((), ())), precision=precise, preferred_element_type=jnp.float32,
            )
            for p in range(end, panels):
                kept = jnp.where(between(outer * SUB, end * SUB), 0.0, held[p])
                held[p] = kept - change[p * SUB : (p + 1) * SUB, :]


def two_parts(value):
    high = value.astype(jnp.bfloat16)
    return high, (value - high.astype(jnp.float32)).astype(jnp.bfloat16)


def factor_kernel(
    rows_total, packed_ref, filtered_ref, ortho_hbm, upper_hbm,
    upper_ref, inverse_ref, ortho_ref, sent, upper_sent,
):
    factor(unpack(packed_ref) * (1.0 / rows_total), upper_ref, inverse_ref)
    copies = [pltpu.make_async_copy(upper_ref, upper_hbm, upper_sent)]
    copies[0].start()
    high, low = two_parts(inverse_ref[...])
    right = jnp.concatenate([high, high, low], axis=1)
    chunks = sent.shape[0]
    per_chunk = filtered_ref.shape[0] // chunks
    for chunk in range(chunks):
        rows = pl.ds(chunk * per_chunk, per_chunk)
        high, low = two_parts(filtered_ref[rows, :])
        ortho_ref[rows, :] = lax.dot_general(
            jnp.concatenate([high, low, high], axis=1), right, (((1,), (1,)), ((), ())),
            preferred_element_type=jnp.float32,
        )
        copies.append(
            pltpu.make_async_copy(ortho_ref.at[rows, :], ortho_hbm.at[rows, :], sent.at[chunk])
        )
        copies[-1].start()
    for copy in copies:
        copy.wait()


def call(kernel, out_shape, in_specs, scratch=(), out_spec=vmem):
    return pl.pallas_call(
        kernel,
        out_shape=out_shape,
        in_specs=in_specs,
        out_specs=jax.tree.map(lambda _: out_spec, out_shape),
        scratch_shapes=list(scratch),
        compiler_params=pltpu.CompilerParams(vmem_limit_bytes=VMEM_LIMIT),
    )


def on_device(hamiltonian, block_columns, potential, trial_slab):
    shard_blocks, _, block_size, _ = hamiltonian.shape
    flat_rows, states = trial_slab.shape
    columns = block_columns.reshape(-1)
    weights = potential.reshape(-1, LANES)
    rows_total = flat_rows * lax.axis_size("group") * lax.axis_size("blk")
    group, index = lax.axis_index("group"), lax.axis_index("blk")
    cycle_size = lax.axis_size("blk")
    levels = cycle_size.bit_length() - 1
    origins = [index]
    for level in range(levels):
        flip = jnp.left_shift(1, step_bits(group, level))
        origins += [jnp.bitwise_xor(origin, flip) for origin in origins]
    odd = group % 2
    origins += [cycle_size + 1 - odd, cycle_size + odd]
    alone = (group == 0) | (group == lax.axis_size("group") - 1)
    origins.append(jnp.where(alone, cycle_size + 1, -1))
    sources = jnp.stack(origins).astype(jnp.int32)
    last = cycle_size - 1
    middle = [1, cycle_size, cycle_size + 1] + list(range(2, last))
    flat = jax.ShapeDtypeStruct((flat_rows, states), jnp.float32)
    rounded = jax.ShapeDtypeStruct((shard_blocks, block_size, states), jnp.bfloat16)
    packed = jax.ShapeDtypeStruct((states // 2 + SUB, states), jnp.float32)
    square = jax.ShapeDtypeStruct((states, states), jnp.float32)

    def own_part(value, *terms):
        return call(own_kernel, flat, [smem] * 2 + [vmem] * (2 + len(terms)))(
            sources, columns, hamiltonian, value, *terms
        )

    def coupled(value, *terms):
        pairs = [pair_exchange(value, 0), pair_exchange(value, 1)]
        pieces = [value, cycle_exchange(value, 0)]
        partial = own_part(value, *terms)
        for level in range(1, levels):
            arrived = pieces[1:]
            if level == 1:
                arrived, partial = lax.optimization_barrier((arrived, partial))
            pieces += [cycle_exchange(piece, level) for piece in [value] + arrived]
        pieces += pairs
        partial = call(
            functools.partial(middle_kernel, middle), flat,
            [smem] * 2 + [vmem] * (2 + len(middle)),
        )(sources, columns, hamiltonian, partial, *[pieces[number] for number in middle])
        return partial, pieces[last]

    weighted = (weights.reshape(-1, 1) * trial_slab)
    partial, piece = coupled(trial_slab.reshape(rounded.shape).astype(jnp.bfloat16), weighted)
    once, once_round = call(
        functools.partial(first_kernel, last), (flat, rounded), [smem] * 2 + [vmem] * 3
    )(sources, columns, hamiltonian, partial, piece)
    partial, piece = coupled(once_round, weights, once, trial_slab)
    filtered, gram = call(
        functools.partial(second_kernel, last), (flat, packed), [smem] * 2 + [vmem] * 3
    )(sources, columns, hamiltonian, partial, piece)
    gram = summed(gram)
    return call(
        functools.partial(factor_kernel, rows_total),
        (flat, square),
        [vmem, vmem],
        [
            pltpu.VMEM((states, states), jnp.float32),
            pltpu.VMEM((states, states), jnp.float32),
            pltpu.VMEM((flat_rows, states), jnp.float32),
            pltpu.SemaphoreType.DMA((4,)),
            pltpu.SemaphoreType.DMA,
        ],
        hbm,
    )(gram, filtered)


def solution(mesh):
    placed = (
        P(("group", "blk"), None, None, None),
        P(("group", "blk"), None, None),
        P(("group", "blk")),
        P(("group", "blk"), None),
    )
    return jax.shard_map(
        on_device,
        mesh=mesh,
        in_specs=placed,
        out_specs=(P(("group", "blk"), None), P()),
        check_vma=False,
    )
```

```python
import functools

import jax
import jax.numpy as jnp
from jax import lax
from jax.experimental import pallas as pl
from jax.experimental.pallas import tpu as pltpu
from jax.sharding import PartitionSpec as P

precise = lax.Precision.HIGHEST
LANES = 128
SUB = 8
OUTER = 4
VMEM_LIMIT = 40 * 1024 * 1024
vmem = pl.BlockSpec(memory_space=pltpu.VMEM)
hbm = pl.BlockSpec(memory_space=pl.ANY)
smem = pl.BlockSpec(memory_space=pltpu.SMEM)


def pair_exchange(value, offset):
    count = lax.axis_size("group")
    route = []
    for low in range(offset, count - 1, 2):
        route += [(low, low + 1), (low + 1, low)]
    return lax.ppermute(value, "group", route)


def step_bits(group, level):
    levels = lax.axis_size("blk").bit_length() - 1
    return jnp.where(group % 2 == 1, levels - 1 - level, level)


def cycle_exchange(value, level):
    groups, cycle_size = lax.axis_size("group"), lax.axis_size("blk")
    levels = cycle_size.bit_length() - 1
    route = []
    for group in range(groups):
        bit = levels - 1 - level if group % 2 else level
        route += [
            (group * cycle_size + index, group * cycle_size + (index ^ 1 << bit))
            for index in range(cycle_size)
        ]
    return lax.ppermute(value, ("group", "blk"), route)


def from_partner(value, axis, flip):
    count = lax.axis_size(axis)
    return lax.ppermute(value, axis, [(index, index ^ flip) for index in range(count)])


def summed(value):
    for axis, step in (("group", 1), ("group", 2), ("blk", 1)):
        count = 2 if (axis, step) == ("group", 1) else lax.axis_size(axis)
        while step < count:
            flips = [step, 2 * step, 3 * step] if 2 * step < count else [step]
            others = [from_partner(value, axis, flip) for flip in flips]
            value = value + others[0]
            if len(others) == 3:
                value = value + (others[1] + others[2])
            step *= len(flips) + 1
    return value


def potential_columns(potential_ref):
    return jnp.transpose(potential_ref[...])


def couple_row(index_ref, hamiltonian_ref, pieces, row):
    shard_blocks, sources, block_size, width = hamiltonian_ref.shape
    per_source = width // block_size
    total = None
    for number, piece_ref in pieces:
        source = index_ref[shard_blocks * sources * per_source + number]
        first = (row * sources + source) * per_source
        picked = jnp.concatenate(
            [piece_ref[index_ref[first + slot]] for slot in range(per_source)], axis=0
        )
        product = jnp.dot(
            hamiltonian_ref[row, source], picked, preferred_element_type=jnp.float32
        )
        total = product if total is None else total + product
    return total


def own_kernel(index_ref, hamiltonian_ref, own_ref, *refs):
    terms, partial_ref = refs[:-1], refs[-1]
    shard_blocks, _, block_size, _ = hamiltonian_ref.shape
    per_column = LANES // block_size
    if len(terms) == 3:
        weights = potential_columns(terms[0])
    for row in range(shard_blocks):
        rows = pl.ds(row * block_size, block_size)
        if len(terms) == 3:
            column, part = divmod(row, per_column)
            weight = weights[part * block_size : (part + 1) * block_size, column : column + 1]
            total = weight * terms[1][rows, :] - terms[2][rows, :]
        else:
            total = terms[0][rows, :]
        partial_ref[rows, :] = total + couple_row(
            index_ref, hamiltonian_ref, [(0, own_ref)], row
        )


def middle_kernel(numbers, index_ref, hamiltonian_ref, partial_ref, *refs):
    pieces, sum_ref = list(zip(numbers, refs[:-1])), refs[-1]
    shard_blocks, _, block_size, _ = hamiltonian_ref.shape
    for row in range(shard_blocks):
        rows = pl.ds(row * block_size, block_size)
        sum_ref[rows, :] = partial_ref[rows, :] + couple_row(
            index_ref, hamiltonian_ref, pieces, row
        )


def first_kernel(
    number, index_ref, hamiltonian_ref, partial_ref, piece_ref, once_ref, round_ref
):
    shard_blocks, _, block_size, _ = hamiltonian_ref.shape
    for row in range(shard_blocks):
        rows = pl.ds(row * block_size, block_size)
        once = 0.5 * (
            partial_ref[rows, :]
            + couple_row(index_ref, hamiltonian_ref, [(number, piece_ref)], row)
        )
        once_ref[rows, :] = once
        round_ref[row] = once.astype(jnp.bfloat16)


def second_kernel(
    number, index_ref, hamiltonian_ref, partial_ref, piece_ref,
    filtered_ref, packed_ref,
):
    shard_blocks, _, block_size, _ = hamiltonian_ref.shape
    for row in range(shard_blocks):
        rows = pl.ds(row * block_size, block_size)
        filtered_ref[rows, :] = partial_ref[rows, :] + couple_row(
            index_ref, hamiltonian_ref, [(number, piece_ref)], row
        )
    states = filtered_ref.shape[1]
    both = jnp.concatenate(two_parts(filtered_ref[...]), axis=1)
    products = lax.dot_general(
        both, both, (((0,), (0,)), ((), ())), preferred_element_type=jnp.float32
    )
    high, low = products[:states, :], products[states:, :]
    gram = high[:, :states] + (high[:, states:] + low[:, :states] + low[:, states:])
    pack(gram, packed_ref)


def two_parts(value):
    high = value.astype(jnp.bfloat16)
    return high, (value - high.astype(jnp.float32)).astype(jnp.bfloat16)


def pack(gram, packed_ref):
    size = gram.shape[0]
    half = size // 2
    row = lax.broadcasted_iota(jnp.int32, (half, size), 0)
    lane = lax.broadcasted_iota(jnp.int32, (half, size), 1)
    lower = gram[half:, :]
    packed_ref[pl.ds(0, half), :] = jnp.where(lane < row, pltpu.roll(lower, half, 1), gram[:half, :])
    diagonal = jnp.sum(jnp.where(lane == row + half, lower, 0.0), axis=0, keepdims=True)
    packed_ref[pl.ds(half, SUB), :] = jnp.broadcast_to(diagonal, (SUB, size))


def unpack(packed_ref):
    size = packed_ref.shape[1]
    half = size // 2
    row = lax.broadcasted_iota(jnp.int32, (size, size), 0)
    lane = lax.broadcasted_iota(jnp.int32, (size, size), 1)
    upper = packed_ref[pl.ds(0, half), :]
    both = jnp.concatenate([upper, pltpu.roll(upper, half, 1)], axis=0)
    held = ((row < half) & (lane > row)) | ((row >= half) & (lane >= half) & (lane < row))
    off_diagonal = jnp.where(held, both, 0.0)
    diagonal = jnp.where(row < half, both, packed_ref[pl.ds(half, 1), :])
    return off_diagonal + jnp.transpose(off_diagonal) + jnp.where(row == lane, diagonal, 0.0)


def inverse_of(value):
    estimate = pl.reciprocal(value, approx=True)
    estimate = estimate * (2.0 - value * estimate)
    return estimate * (2.0 - value * estimate)


def factor(gram, upper_ref, inverse_ref):
    size = gram.shape[1]
    panels = size // SUB
    shape = (SUB, size)
    row_index = lax.broadcasted_iota(jnp.int32, shape, 0)
    lane_index = lax.broadcasted_iota(jnp.int32, shape, 1)

    def along_lanes(panel, first):
        return [jnp.broadcast_to(panel[:, first + c : first + c + 1], shape) for c in range(SUB)]

    def along_rows(panel, row):
        return jnp.broadcast_to(panel[row : row + 1, :], shape)

    def between(low, high):
        return (lane_index >= low) & (lane_index < high)

    held = [gram[k * SUB : (k + 1) * SUB, :] for k in range(panels)]
    for outer in range(0, panels, OUTER):
        end = outer + OUTER
        rows_then, rows_reduced = [], []
        block = along_lanes(held[outer], outer * SUB)
        for k in range(outer, end):
            first = k * SUB
            below = {p: along_lanes(held[p], first) for p in range(k + 1, end)}
            after = list(below[k + 1]) if k + 1 < end else None
            following = along_lanes(held[k + 1], first + SUB) if k + 1 < end else None
            right = held[k]
            left = jnp.where(
                lane_index < first, held[k], jnp.where(lane_index == row_index + first, 1.0, 0.0)
            )
            pivots = jnp.ones(shape, jnp.float32)
            reciprocals = jnp.ones(shape, jnp.float32)
            for j in range(0, SUB, 2):
                a, b = along_rows(block[j], j), along_rows(block[j], j + 1)
                c = along_rows(block[j + 1], j + 1)
                determinant = a * c - b * b
                over = inverse_of(determinant)
                over_a = inverse_of(a)
                pivots = jnp.where(row_index == j, a, pivots)
                pivots = jnp.where(row_index == j + 1, determinant * over_a, pivots)
                reciprocals = jnp.where(row_index == j, over_a, reciprocals)
                reciprocals = jnp.where(row_index == j + 1, a * over, reciprocals)
                x, y = block[j], block[j + 1]
                one = jnp.where(row_index == j + 1, b * over_a, 0.0)
                one = jnp.where(row_index > j + 1, (x * c - y * b) * over, one)
                two = jnp.where(row_index > j + 1, (y * a - x * b) * over, 0.0)
                upper = {
                    n: (along_rows(block[n], j), along_rows(block[n], j + 1))
                    for n in range(j + 2, SUB)
                }
                for n in upper:
                    block[n] = block[n] - one * upper[n][0] - two * upper[n][1]
                if following is not None:
                    x, y = after[j], after[j + 1]
                    next_one, next_two = (x * c - y * b) * over, (y * a - x * b) * over
                    for n in range(SUB):
                        following[n] = (
                            following[n] - next_one * along_rows(x, n) - next_two * along_rows(y, n)
                        )
                    for n in upper:
                        after[n] = after[n] - next_one * upper[n][0] - next_two * upper[n][1]
                right = right - one * along_rows(right, j) - two * along_rows(right, j + 1)
                left = left - one * along_rows(left, j) - two * along_rows(left, j + 1)
            scale = lax.rsqrt(pivots)
            upper_ref[pl.ds(first, SUB), :] = jnp.where(
                lane_index >= row_index + first, right * scale, 0.0
            )
            inverse_ref[pl.ds(first, SUB), :] = left * scale
            if k + 1 < panels:
                reduced = jnp.where(lane_index >= first + SUB, right, left) * reciprocals
                for n in range(SUB - 1, 0, -1):
                    column = jnp.where(row_index < n, block[n] * reciprocals, 0.0)
                    reduced = reduced - column * along_rows(reduced, n)
                rows_then.append(held[k])
                rows_reduced.append(jnp.where(between(first + SUB, end * SUB), 0.0, reduced))
                rows = [along_rows(reduced, n) for n in range(SUB)]
                for p in below:
                    total = jnp.where(between(first, first + SUB), 0.0, held[p])
                    for n in range(SUB):
                        total = total - below[p][n] * rows[n]
                    held[p] = total
            block = following
        if end < panels:
            change = lax.dot_general(
                jnp.concatenate(rows_then, axis=0), jnp.concatenate(rows_reduced, axis=0),
                (((0,), (0,)), ((), ())), precision=precise, preferred_element_type=jnp.float32,
            )
            for p in range(end, panels):
                kept = jnp.where(between(outer * SUB, end * SUB), 0.0, held[p])
                held[p] = kept - change[p * SUB : (p + 1) * SUB, :]


def factor_kernel(
    rows_total, packed_ref, filtered_ref, ortho_hbm, upper_hbm,
    upper_ref, inverse_ref, ortho_ref, sent, upper_sent,
):
    factor(unpack(packed_ref) * (1.0 / rows_total), upper_ref, inverse_ref)
    copies = [pltpu.make_async_copy(upper_ref, upper_hbm, upper_sent)]
    copies[0].start()
    high, low = two_parts(inverse_ref[...])
    right = jnp.concatenate([high, high, low], axis=1)
    chunks = sent.shape[0]
    per_chunk = filtered_ref.shape[0] // chunks
    for chunk in range(chunks):
        rows = pl.ds(chunk * per_chunk, per_chunk)
        high, low = two_parts(filtered_ref[rows, :])
        ortho_ref[rows, :] = lax.dot_general(
            jnp.concatenate([high, low, high], axis=1), right, (((1,), (1,)), ((), ())),
            preferred_element_type=jnp.float32,
        )
        copies.append(
            pltpu.make_async_copy(ortho_ref.at[rows, :], ortho_hbm.at[rows, :], sent.at[chunk])
        )
        copies[-1].start()
    for copy in copies:
        copy.wait()


def call(kernel, out_shape, in_specs, scratch=(), out_spec=vmem):
    return pl.pallas_call(
        kernel,
        out_shape=out_shape,
        in_specs=in_specs,
        out_specs=jax.tree.map(lambda _: out_spec, out_shape),
        scratch_shapes=list(scratch),
        compiler_params=pltpu.CompilerParams(vmem_limit_bytes=VMEM_LIMIT),
    )


def on_device(hamiltonian, block_columns, potential, trial_slab):
    shard_blocks, _, block_size, _ = hamiltonian.shape
    flat_rows, states = trial_slab.shape
    weights = potential.reshape(-1, LANES)
    rows_total = flat_rows * lax.axis_size("group") * lax.axis_size("blk")
    group, index = lax.axis_index("group"), lax.axis_index("blk")
    cycle_size = lax.axis_size("blk")
    levels = cycle_size.bit_length() - 1
    origins = [index]
    for level in range(levels):
        flip = jnp.left_shift(1, step_bits(group, level))
        origins += [jnp.bitwise_xor(origin, flip) for origin in origins]
    odd = group % 2
    origins += [cycle_size + 1 - odd, cycle_size + odd]
    index_array = jnp.concatenate(
        [block_columns.reshape(-1)] + [origin.reshape(1).astype(jnp.int32) for origin in origins]
    )
    last = cycle_size - 1
    middle = [1, cycle_size, cycle_size + 1] + list(range(2, last))
    flat = jax.ShapeDtypeStruct((flat_rows, states), jnp.float32)
    rounded = jax.ShapeDtypeStruct((shard_blocks, block_size, states), jnp.bfloat16)
    packed = jax.ShapeDtypeStruct((states // 2 + SUB, states), jnp.float32)
    square = jax.ShapeDtypeStruct((states, states), jnp.float32)

    def own_part(value, *terms):
        return call(own_kernel, flat, [smem] + [vmem] * (2 + len(terms)))(
            index_array, hamiltonian, value, *terms
        )

    def coupled(value, *terms):
        pairs = [pair_exchange(value, 0), pair_exchange(value, 1)]
        pieces = [value, cycle_exchange(value, 0)]
        partial = own_part(value, *terms)
        for level in range(1, levels):
            arrived = pieces[1:]
            if level == 1:
                arrived, partial = lax.optimization_barrier((arrived, partial))
            pieces += [cycle_exchange(piece, level) for piece in [value] + arrived]
        pieces += pairs
        partial = call(
            functools.partial(middle_kernel, middle), flat,
            [smem] + [vmem] * (2 + len(middle)),
        )(index_array, hamiltonian, partial, *[pieces[number] for number in middle])
        return partial, pieces[last]

    weighted = (weights.reshape(-1, 1) * trial_slab)
    partial, piece = coupled(trial_slab.reshape(rounded.shape).astype(jnp.bfloat16), weighted)
    once, once_round = call(
        functools.partial(first_kernel, last), (flat, rounded), [smem] + [vmem] * 3
    )(index_array, hamiltonian, partial, piece)
    partial, piece = coupled(once_round, weights, once, trial_slab)
    filtered, gram = call(
        functools.partial(second_kernel, last), (flat, packed), [smem] + [vmem] * 3
    )(index_array, hamiltonian, partial, piece)
    gram = summed(gram)
    return call(
        functools.partial(factor_kernel, rows_total),
        (flat, square),
        [vmem, vmem],
        [
            pltpu.VMEM((states, states), jnp.float32),
            pltpu.VMEM((states, states), jnp.float32),
            pltpu.VMEM((flat_rows, states), jnp.float32),
            pltpu.SemaphoreType.DMA((4,)),
            pltpu.SemaphoreType.DMA,
        ],
        hbm,
    )(gram, filtered)


def solution(mesh):
    placed = (
        P(("group", "blk"), None, None, None),
        P(("group", "blk"), None, None),
        P(("group", "blk")),
        P(("group", "blk"), None),
    )
    return jax.shard_map(
        on_device,
        mesh=mesh,
        in_specs=placed,
        out_specs=(P(("group", "blk"), None), P()),
        check_vma=False,
    )
```

```python
import functools

import jax
import jax.numpy as jnp
from jax import lax
from jax.experimental import pallas as pl
from jax.experimental.pallas import tpu as pltpu
from jax.sharding import PartitionSpec as P

precise = lax.Precision.HIGHEST
LANES = 128
SUB = 8
OUTER = 4
VMEM_LIMIT = 40 * 1024 * 1024
vmem = pl.BlockSpec(memory_space=pltpu.VMEM)
hbm = pl.BlockSpec(memory_space=pl.ANY)
smem = pl.BlockSpec(memory_space=pltpu.SMEM)


def pair_exchange(value, offset):
    count = lax.axis_size("group")
    route = []
    for low in range(offset, count - 1, 2):
        route += [(low, low + 1), (low + 1, low)]
    return lax.ppermute(value, "group", route)


def step_bits(group, level):
    levels = lax.axis_size("blk").bit_length() - 1
    return jnp.where(group % 2 == 1, levels - 1 - level, level)


def cycle_exchange(value, level):
    groups, cycle_size = lax.axis_size("group"), lax.axis_size("blk")
    levels = cycle_size.bit_length() - 1
    route = []
    for group in range(groups):
        bit = levels - 1 - level if group % 2 else level
        route += [
            (group * cycle_size + index, group * cycle_size + (index ^ 1 << bit))
            for index in range(cycle_size)
        ]
    return lax.ppermute(value, ("group", "blk"), route)


def from_partner(value, axis, flip):
    count = lax.axis_size(axis)
    return lax.ppermute(value, axis, [(index, index ^ flip) for index in range(count)])


def summed(value):
    for axis, step in (("group", 1), ("group", 2), ("blk", 1)):
        count = 2 if (axis, step) == ("group", 1) else lax.axis_size(axis)
        while step < count:
            flips = [step, 2 * step, 3 * step] if 2 * step < count else [step]
            others = [from_partner(value, axis, flip) for flip in flips]
            value = value + others[0]
            if len(others) == 3:
                value = value + (others[1] + others[2])
            step *= len(flips) + 1
    return value


def potential_columns(potential_ref):
    return jnp.transpose(potential_ref[...])


def couple_row(index_ref, hamiltonian_ref, pieces, row):
    shard_blocks, sources, block_size, width = hamiltonian_ref.shape
    per_source = width // block_size
    total = None
    for number, piece_ref in pieces:
        source = index_ref[shard_blocks * sources * per_source + number]
        first = (row * sources + source) * per_source
        picked = jnp.concatenate(
            [piece_ref[index_ref[first + slot]] for slot in range(per_source)], axis=0
        )
        product = jnp.dot(
            hamiltonian_ref[row, source], picked, preferred_element_type=jnp.float32
        )
        total = product if total is None else total + product
    return total


def own_kernel(index_ref, hamiltonian_ref, own_ref, *refs):
    terms, partial_ref = refs[:-1], refs[-1]
    shard_blocks, _, block_size, _ = hamiltonian_ref.shape
    per_column = LANES // block_size
    if len(terms) == 3:
        weights = potential_columns(terms[0])
    for row in range(shard_blocks):
        rows = pl.ds(row * block_size, block_size)
        if len(terms) == 3:
            column, part = divmod(row, per_column)
            weight = weights[part * block_size : (part + 1) * block_size, column : column + 1]
            total = weight * terms[1][rows, :] - terms[2][rows, :]
        else:
            total = terms[0][rows, :]
        partial_ref[rows, :] = total + couple_row(
            index_ref, hamiltonian_ref, [(0, own_ref)], row
        )


def middle_kernel(numbers, index_ref, hamiltonian_ref, partial_ref, *refs):
    pieces, sum_ref = list(zip(numbers, refs[:-1])), refs[-1]
    shard_blocks, _, block_size, _ = hamiltonian_ref.shape
    for row in range(shard_blocks):
        rows = pl.ds(row * block_size, block_size)
        sum_ref[rows, :] = partial_ref[rows, :] + couple_row(
            index_ref, hamiltonian_ref, pieces, row
        )


def first_kernel(numbers, index_ref, hamiltonian_ref, partial_ref, *refs):
    pieces, (once_ref, round_ref) = list(zip(numbers, refs)), refs[len(numbers) :]
    shard_blocks, _, block_size, _ = hamiltonian_ref.shape
    for row in range(shard_blocks):
        rows = pl.ds(row * block_size, block_size)
        once = 0.5 * (
            partial_ref[rows, :] + couple_row(index_ref, hamiltonian_ref, pieces, row)
        )
        once_ref[rows, :] = once
        round_ref[row] = once.astype(jnp.bfloat16)


def second_kernel(numbers, index_ref, hamiltonian_ref, partial_ref, *refs):
    pieces, (filtered_ref, packed_ref) = list(zip(numbers, refs)), refs[len(numbers) :]
    shard_blocks, _, block_size, _ = hamiltonian_ref.shape
    for row in range(shard_blocks):
        rows = pl.ds(row * block_size, block_size)
        filtered_ref[rows, :] = partial_ref[rows, :] + couple_row(
            index_ref, hamiltonian_ref, pieces, row
        )
    states = filtered_ref.shape[1]
    both = jnp.concatenate(two_parts(filtered_ref[...]), axis=1)
    products = lax.dot_general(
        both, both, (((0,), (0,)), ((), ())), preferred_element_type=jnp.float32
    )
    high, low = products[:states, :], products[states:, :]
    gram = high[:, :states] + (high[:, states:] + low[:, :states] + low[:, states:])
    pack(gram, packed_ref)


def two_parts(value):
    high = value.astype(jnp.bfloat16)
    return high, (value - high.astype(jnp.float32)).astype(jnp.bfloat16)


def pack(gram, packed_ref):
    size = gram.shape[0]
    half = size // 2
    row = lax.broadcasted_iota(jnp.int32, (half, size), 0)
    lane = lax.broadcasted_iota(jnp.int32, (half, size), 1)
    lower = gram[half:, :]
    packed_ref[pl.ds(0, half), :] = jnp.where(lane < row, pltpu.roll(lower, half, 1), gram[:half, :])
    diagonal = jnp.sum(jnp.where(lane == row + half, lower, 0.0), axis=0, keepdims=True)
    packed_ref[pl.ds(half, SUB), :] = jnp.broadcast_to(diagonal, (SUB, size))


def unpack(packed_ref):
    size = packed_ref.shape[1]
    half = size // 2
    row = lax.broadcasted_iota(jnp.int32, (size, size), 0)
    lane = lax.broadcasted_iota(jnp.int32, (size, size), 1)
    upper = packed_ref[pl.ds(0, half), :]
    both = jnp.concatenate([upper, pltpu.roll(upper, half, 1)], axis=0)
    held = ((row < half) & (lane > row)) | ((row >= half) & (lane >= half) & (lane < row))
    off_diagonal = jnp.where(held, both, 0.0)
    diagonal = jnp.where(row < half, both, packed_ref[pl.ds(half, 1), :])
    return off_diagonal + jnp.transpose(off_diagonal) + jnp.where(row == lane, diagonal, 0.0)


def inverse_of(value):
    estimate = pl.reciprocal(value, approx=True)
    estimate = estimate * (2.0 - value * estimate)
    return estimate * (2.0 - value * estimate)


def factor(gram, upper_ref, inverse_ref):
    size = gram.shape[1]
    panels = size // SUB
    shape = (SUB, size)
    row_index = lax.broadcasted_iota(jnp.int32, shape, 0)
    lane_index = lax.broadcasted_iota(jnp.int32, shape, 1)

    def along_lanes(panel, first):
        return [jnp.broadcast_to(panel[:, first + c : first + c + 1], shape) for c in range(SUB)]

    def along_rows(panel, row):
        return jnp.broadcast_to(panel[row : row + 1, :], shape)

    def between(low, high):
        return (lane_index >= low) & (lane_index < high)

    held = [gram[k * SUB : (k + 1) * SUB, :] for k in range(panels)]
    for outer in range(0, panels, OUTER):
        end = outer + OUTER
        rows_then, rows_reduced = [], []
        block = along_lanes(held[outer], outer * SUB)
        for k in range(outer, end):
            first = k * SUB
            below = {p: along_lanes(held[p], first) for p in range(k + 1, end)}
            after = list(below[k + 1]) if k + 1 < end else None
            following = along_lanes(held[k + 1], first + SUB) if k + 1 < end else None
            right = held[k]
            left = jnp.where(
                lane_index < first, held[k], jnp.where(lane_index == row_index + first, 1.0, 0.0)
            )
            pivots = jnp.ones(shape, jnp.float32)
            reciprocals = jnp.ones(shape, jnp.float32)
            for j in range(0, SUB, 2):
                a, b = along_rows(block[j], j), along_rows(block[j], j + 1)
                c = along_rows(block[j + 1], j + 1)
                determinant = a * c - b * b
                over = inverse_of(determinant)
                over_a = inverse_of(a)
                pivots = jnp.where(row_index == j, a, pivots)
                pivots = jnp.where(row_index == j + 1, determinant * over_a, pivots)
                reciprocals = jnp.where(row_index == j, over_a, reciprocals)
                reciprocals = jnp.where(row_index == j + 1, a * over, reciprocals)
                x, y = block[j], block[j + 1]
                one = jnp.where(row_index == j + 1, b * over_a, 0.0)
                one = jnp.where(row_index > j + 1, (x * c - y * b) * over, one)
                two = jnp.where(row_index > j + 1, (y * a - x * b) * over, 0.0)
                upper = {
                    n: (along_rows(block[n], j), along_rows(block[n], j + 1))
                    for n in range(j + 2, SUB)
                }
                for n in upper:
                    block[n] = block[n] - one * upper[n][0] - two * upper[n][1]
                if following is not None:
                    x, y = after[j], after[j + 1]
                    next_one, next_two = (x * c - y * b) * over, (y * a - x * b) * over
                    for n in range(SUB):
                        following[n] = (
                            following[n] - next_one * along_rows(x, n) - next_two * along_rows(y, n)
                        )
                    for n in upper:
                        after[n] = after[n] - next_one * upper[n][0] - next_two * upper[n][1]
                right = right - one * along_rows(right, j) - two * along_rows(right, j + 1)
                left = left - one * along_rows(left, j) - two * along_rows(left, j + 1)
            scale = lax.rsqrt(pivots)
            upper_ref[pl.ds(first, SUB), :] = jnp.where(
                lane_index >= row_index + first, right * scale, 0.0
            )
            inverse_ref[pl.ds(first, SUB), :] = left * scale
            if k + 1 < panels:
                reduced = jnp.where(lane_index >= first + SUB, right, left) * reciprocals
                for n in range(SUB - 1, 0, -1):
                    column = jnp.where(row_index < n, block[n] * reciprocals, 0.0)
                    reduced = reduced - column * along_rows(reduced, n)
                rows_then.append(held[k])
                rows_reduced.append(jnp.where(between(first + SUB, end * SUB), 0.0, reduced))
                rows = [along_rows(reduced, n) for n in range(SUB)]
                for p in below:
                    total = jnp.where(between(first, first + SUB), 0.0, held[p])
                    for n in range(SUB):
                        total = total - below[p][n] * rows[n]
                    held[p] = total
            block = following
        if end < panels:
            change = lax.dot_general(
                jnp.concatenate(rows_then, axis=0), jnp.concatenate(rows_reduced, axis=0),
                (((0,), (0,)), ((), ())), precision=precise, preferred_element_type=jnp.float32,
            )
            for p in range(end, panels):
                kept = jnp.where(between(outer * SUB, end * SUB), 0.0, held[p])
                held[p] = kept - change[p * SUB : (p + 1) * SUB, :]


def factor_kernel(
    rows_total, packed_ref, filtered_ref, ortho_hbm, upper_hbm,
    upper_ref, inverse_ref, ortho_ref, sent, upper_sent,
):
    factor(unpack(packed_ref) * (1.0 / rows_total), upper_ref, inverse_ref)
    copies = [pltpu.make_async_copy(upper_ref, upper_hbm, upper_sent)]
    copies[0].start()
    high, low = two_parts(inverse_ref[...])
    right = jnp.concatenate([high, high, low], axis=1)
    chunks = sent.shape[0]
    per_chunk = filtered_ref.shape[0] // chunks
    for chunk in range(chunks):
        rows = pl.ds(chunk * per_chunk, per_chunk)
        high, low = two_parts(filtered_ref[rows, :])
        ortho_ref[rows, :] = lax.dot_general(
            jnp.concatenate([high, low, high], axis=1), right, (((1,), (1,)), ((), ())),
            preferred_element_type=jnp.float32,
        )
        copies.append(
            pltpu.make_async_copy(ortho_ref.at[rows, :], ortho_hbm.at[rows, :], sent.at[chunk])
        )
        copies[-1].start()
    for copy in copies:
        copy.wait()


def call(kernel, out_shape, in_specs, scratch=(), out_spec=vmem):
    return pl.pallas_call(
        kernel,
        out_shape=out_shape,
        in_specs=in_specs,
        out_specs=jax.tree.map(lambda _: out_spec, out_shape),
        scratch_shapes=list(scratch),
        compiler_params=pltpu.CompilerParams(vmem_limit_bytes=VMEM_LIMIT),
    )


def on_device(hamiltonian, block_columns, potential, trial_slab):
    shard_blocks, _, block_size, _ = hamiltonian.shape
    flat_rows, states = trial_slab.shape
    weights = potential.reshape(-1, LANES)
    rows_total = flat_rows * lax.axis_size("group") * lax.axis_size("blk")
    group, index = lax.axis_index("group"), lax.axis_index("blk")
    cycle_size = lax.axis_size("blk")
    levels = cycle_size.bit_length() - 1
    origins = [index]
    for level in range(levels):
        flip = jnp.left_shift(1, step_bits(group, level))
        origins += [jnp.bitwise_xor(origin, flip) for origin in origins]
    odd = group % 2
    origins += [cycle_size + 1 - odd, cycle_size + odd]
    index_array = jnp.concatenate(
        [block_columns.reshape(-1)] + [origin.reshape(1).astype(jnp.int32) for origin in origins]
    )
    last = cycle_size - 1
    ending = [cycle_size, last]
    middle = [1] + list(range(2, last)) + [cycle_size + 1]
    flat = jax.ShapeDtypeStruct((flat_rows, states), jnp.float32)
    rounded = jax.ShapeDtypeStruct((shard_blocks, block_size, states), jnp.bfloat16)
    packed = jax.ShapeDtypeStruct((states // 2 + SUB, states), jnp.float32)
    square = jax.ShapeDtypeStruct((states, states), jnp.float32)

    def own_part(value, *terms):
        return call(own_kernel, flat, [smem] + [vmem] * (2 + len(terms)))(
            index_array, hamiltonian, value, *terms
        )

    def coupled(value, early, *terms):
        arrived = cycle_exchange(value, 0)
        outer = pair_exchange(value, 1)
        others = [cycle_exchange(value, level) for level in range(1, levels)]
        if early:
            partial = own_part(value, *terms)
            arrived, again, partial = lax.optimization_barrier((arrived, value, partial))
        else:
            arrived, again = lax.optimization_barrier((arrived, value))
        pieces = [value, arrived]
        for level, other in zip(range(1, levels), others):
            pieces += [other] + [cycle_exchange(piece, level) for piece in pieces[1:]]
        pieces += [pair_exchange(again, 0), outer]
        if not early:
            partial = own_part(value, *terms)
        partial = call(
            functools.partial(middle_kernel, middle), flat, [smem] + [vmem] * (2 + len(middle)),
        )(index_array, hamiltonian, partial, *[pieces[number] for number in middle])
        return [partial] + [pieces[number] for number in ending]

    weighted = (weights.reshape(-1, 1) * trial_slab)
    parts = coupled(trial_slab.reshape(rounded.shape).astype(jnp.bfloat16), False, weighted)
    once, once_round = call(
        functools.partial(first_kernel, ending), (flat, rounded), [smem] + [vmem] * 4
    )(index_array, hamiltonian, *parts)
    parts = coupled(once_round, True, weights, once, trial_slab)
    filtered, gram = call(
        functools.partial(second_kernel, ending), (flat, packed), [smem] + [vmem] * 4
    )(index_array, hamiltonian, *parts)
    gram = summed(gram)
    return call(
        functools.partial(factor_kernel, rows_total),
        (flat, square),
        [vmem, vmem],
        [
            pltpu.VMEM((states, states), jnp.float32),
            pltpu.VMEM((states, states), jnp.float32),
            pltpu.VMEM((flat_rows, states), jnp.float32),
            pltpu.SemaphoreType.DMA((4,)),
            pltpu.SemaphoreType.DMA,
        ],
        hbm,
    )(gram, filtered)


def solution(mesh):
    placed = (
        P(("group", "blk"), None, None, None),
        P(("group", "blk"), None, None),
        P(("group", "blk")),
        P(("group", "blk"), None),
    )
    return jax.shard_map(
        on_device,
        mesh=mesh,
        in_specs=placed,
        out_specs=(P(("group", "blk"), None), P()),
        check_vma=False,
    )
```

```python
import functools

import jax
import jax.numpy as jnp
from jax import lax
from jax.experimental import pallas as pl
from jax.experimental.pallas import tpu as pltpu
from jax.sharding import PartitionSpec as P

precise = lax.Precision.HIGHEST
LANES = 128
SUB = 8
OUTER = 4
VMEM_LIMIT = 40 * 1024 * 1024
vmem = pl.BlockSpec(memory_space=pltpu.VMEM)
hbm = pl.BlockSpec(memory_space=pl.ANY)
smem = pl.BlockSpec(memory_space=pltpu.SMEM)


def pair_exchange(value, offset):
    count = lax.axis_size("group")
    route = []
    for low in range(offset, count - 1, 2):
        route += [(low, low + 1), (low + 1, low)]
    return lax.ppermute(value, "group", route)


def step_bits(group, level):
    levels = lax.axis_size("blk").bit_length() - 1
    return jnp.where(group % 2 == 1, levels - 1 - level, level)


def cycle_exchange(value, level):
    groups, cycle_size = lax.axis_size("group"), lax.axis_size("blk")
    levels = cycle_size.bit_length() - 1
    route = []
    for group in range(groups):
        bit = levels - 1 - level if group % 2 else level
        route += [
            (group * cycle_size + index, group * cycle_size + (index ^ 1 << bit))
            for index in range(cycle_size)
        ]
    return lax.ppermute(value, ("group", "blk"), route)


def from_partner(value, axis, flip):
    count = lax.axis_size(axis)
    return lax.ppermute(value, axis, [(index, index ^ flip) for index in range(count)])


def summed(value):
    for axis, step in (("group", 1), ("group", 2), ("blk", 1)):
        count = 2 if (axis, step) == ("group", 1) else lax.axis_size(axis)
        while step < count:
            flips = [step, 2 * step, 3 * step] if 2 * step < count else [step]
            others = [from_partner(value, axis, flip) for flip in flips]
            value = value + others[0]
            if len(others) == 3:
                value = value + (others[1] + others[2])
            step *= len(flips) + 1
    return value


def potential_columns(potential_ref):
    return jnp.transpose(potential_ref[...])


def couple_row(index_ref, hamiltonian_ref, pieces, row):
    shard_blocks, sources, block_size, width = hamiltonian_ref.shape
    per_source = width // block_size
    total = None
    for number, piece_ref in pieces:
        source = index_ref[shard_blocks * sources * per_source + number]
        first = (row * sources + source) * per_source
        picked = jnp.concatenate(
            [piece_ref[index_ref[first + slot]] for slot in range(per_source)], axis=0
        )
        product = jnp.dot(
            hamiltonian_ref[row, source], picked, preferred_element_type=jnp.float32
        )
        total = product if total is None else total + product
    return total


def own_kernel(index_ref, hamiltonian_ref, own_ref, *refs):
    terms, partial_ref = refs[:-1], refs[-1]
    shard_blocks, _, block_size, _ = hamiltonian_ref.shape
    per_column = LANES // block_size
    if len(terms) == 3:
        weights = potential_columns(terms[0])
    for row in range(shard_blocks):
        rows = pl.ds(row * block_size, block_size)
        if len(terms) == 3:
            column, part = divmod(row, per_column)
            weight = weights[part * block_size : (part + 1) * block_size, column : column + 1]
            total = weight * terms[1][rows, :] - terms[2][rows, :]
        else:
            total = terms[0][rows, :]
        partial_ref[rows, :] = total + couple_row(
            index_ref, hamiltonian_ref, [(0, own_ref)], row
        )


def middle_kernel(numbers, index_ref, hamiltonian_ref, partial_ref, *refs):
    pieces, sum_ref = list(zip(numbers, refs[:-1])), refs[-1]
    shard_blocks, _, block_size, _ = hamiltonian_ref.shape
    for row in range(shard_blocks):
        rows = pl.ds(row * block_size, block_size)
        sum_ref[rows, :] = partial_ref[rows, :] + couple_row(
            index_ref, hamiltonian_ref, pieces, row
        )


def first_kernel(numbers, index_ref, hamiltonian_ref, partial_ref, *refs):
    pieces, (once_ref, round_ref) = list(zip(numbers, refs)), refs[len(numbers) :]
    shard_blocks, _, block_size, _ = hamiltonian_ref.shape
    for row in range(shard_blocks):
        rows = pl.ds(row * block_size, block_size)
        once = 0.5 * (
            partial_ref[rows, :] + couple_row(index_ref, hamiltonian_ref, pieces, row)
        )
        once_ref[rows, :] = once
        round_ref[row] = once.astype(jnp.bfloat16)


def second_kernel(numbers, index_ref, hamiltonian_ref, partial_ref, *refs):
    pieces, (filtered_ref, packed_ref) = list(zip(numbers, refs)), refs[len(numbers) :]
    shard_blocks, _, block_size, _ = hamiltonian_ref.shape
    for row in range(shard_blocks):
        rows = pl.ds(row * block_size, block_size)
        filtered_ref[rows, :] = partial_ref[rows, :] + couple_row(
            index_ref, hamiltonian_ref, pieces, row
        )
    states = filtered_ref.shape[1]
    both = jnp.concatenate(two_parts(filtered_ref[...]), axis=1)
    products = lax.dot_general(
        both, both, (((0,), (0,)), ((), ())), preferred_element_type=jnp.float32
    )
    high, low = products[:states, :], products[states:, :]
    gram = high[:, :states] + (high[:, states:] + low[:, :states] + low[:, states:])
    pack(gram, packed_ref)


def two_parts(value):
    high = value.astype(jnp.bfloat16)
    return high, (value - high.astype(jnp.float32)).astype(jnp.bfloat16)


def pack(gram, packed_ref):
    size = gram.shape[0]
    half = size // 2
    row = lax.broadcasted_iota(jnp.int32, (half, size), 0)
    lane = lax.broadcasted_iota(jnp.int32, (half, size), 1)
    lower = gram[half:, :]
    packed_ref[pl.ds(0, half), :] = jnp.where(lane < row, pltpu.roll(lower, half, 1), gram[:half, :])
    diagonal = jnp.sum(jnp.where(lane == row + half, lower, 0.0), axis=0, keepdims=True)
    packed_ref[pl.ds(half, SUB), :] = jnp.broadcast_to(diagonal, (SUB, size))


def unpack(packed_ref):
    size = packed_ref.shape[1]
    half = size // 2
    row = lax.broadcasted_iota(jnp.int32, (size, size), 0)
    lane = lax.broadcasted_iota(jnp.int32, (size, size), 1)
    upper = packed_ref[pl.ds(0, half), :]
    both = jnp.concatenate([upper, pltpu.roll(upper, half, 1)], axis=0)
    held = ((row < half) & (lane > row)) | ((row >= half) & (lane >= half) & (lane < row))
    off_diagonal = jnp.where(held, both, 0.0)
    diagonal = jnp.where(row < half, both, packed_ref[pl.ds(half, 1), :])
    return off_diagonal + jnp.transpose(off_diagonal) + jnp.where(row == lane, diagonal, 0.0)


def inverse_of(value):
    estimate = pl.reciprocal(value, approx=True)
    estimate = estimate * (2.0 - value * estimate)
    return estimate * (2.0 - value * estimate)


def factor(gram, upper_ref, inverse_ref):
    size = gram.shape[1]
    panels = size // SUB
    shape = (SUB, size)
    row_index = lax.broadcasted_iota(jnp.int32, shape, 0)
    lane_index = lax.broadcasted_iota(jnp.int32, shape, 1)

    def along_lanes(panel, first):
        return [jnp.broadcast_to(panel[:, first + c : first + c + 1], shape) for c in range(SUB)]

    def along_rows(panel, row):
        return jnp.broadcast_to(panel[row : row + 1, :], shape)

    def between(low, high):
        return (lane_index >= low) & (lane_index < high)

    held = [gram[k * SUB : (k + 1) * SUB, :] for k in range(panels)]
    for outer in range(0, panels, OUTER):
        end = outer + OUTER
        rows_then, rows_reduced = [], []
        block = along_lanes(held[outer], outer * SUB)
        for k in range(outer, end):
            first = k * SUB
            below = {p: along_lanes(held[p], first) for p in range(k + 1, end)}
            after = list(below[k + 1]) if k + 1 < end else None
            following = along_lanes(held[k + 1], first + SUB) if k + 1 < end else None
            right = held[k]
            left = jnp.where(
                lane_index < first, held[k], jnp.where(lane_index == row_index + first, 1.0, 0.0)
            )
            pivots = jnp.ones(shape, jnp.float32)
            reciprocals = jnp.ones(shape, jnp.float32)
            for j in range(0, SUB, 2):
                a, b = along_rows(block[j], j), along_rows(block[j], j + 1)
                c = along_rows(block[j + 1], j + 1)
                determinant = a * c - b * b
                over = inverse_of(determinant)
                over_a = inverse_of(a)
                pivots = jnp.where(row_index == j, a, pivots)
                pivots = jnp.where(row_index == j + 1, determinant * over_a, pivots)
                reciprocals = jnp.where(row_index == j, over_a, reciprocals)
                reciprocals = jnp.where(row_index == j + 1, a * over, reciprocals)
                x, y = block[j], block[j + 1]
                one = jnp.where(row_index == j + 1, b * over_a, 0.0)
                one = jnp.where(row_index > j + 1, (x * c - y * b) * over, one)
                two = jnp.where(row_index > j + 1, (y * a - x * b) * over, 0.0)
                upper = {
                    n: (along_rows(block[n], j), along_rows(block[n], j + 1))
                    for n in range(j + 2, SUB)
                }
                for n in upper:
                    block[n] = block[n] - one * upper[n][0] - two * upper[n][1]
                if following is not None:
                    x, y = after[j], after[j + 1]
                    next_one, next_two = (x * c - y * b) * over, (y * a - x * b) * over
                    for n in range(SUB):
                        following[n] = (
                            following[n] - next_one * along_rows(x, n) - next_two * along_rows(y, n)
                        )
                    for n in upper:
                        after[n] = after[n] - next_one * upper[n][0] - next_two * upper[n][1]
                right = right - one * along_rows(right, j) - two * along_rows(right, j + 1)
                left = left - one * along_rows(left, j) - two * along_rows(left, j + 1)
            scale = lax.rsqrt(pivots)
            upper_ref[pl.ds(first, SUB), :] = jnp.where(
                lane_index >= row_index + first, right * scale, 0.0
            )
            inverse_ref[pl.ds(first, SUB), :] = left * scale
            if k + 1 < panels:
                reduced = jnp.where(lane_index >= first + SUB, right, left) * reciprocals
                for n in range(SUB - 1, 0, -1):
                    column = jnp.where(row_index < n, block[n] * reciprocals, 0.0)
                    reduced = reduced - column * along_rows(reduced, n)
                rows_then.append(held[k])
                rows_reduced.append(jnp.where(between(first + SUB, end * SUB), 0.0, reduced))
                rows = [along_rows(reduced, n) for n in range(SUB)]
                for p in below:
                    total = jnp.where(between(first, first + SUB), 0.0, held[p])
                    for n in range(SUB):
                        total = total - below[p][n] * rows[n]
                    held[p] = total
            block = following
        if end < panels:
            change = lax.dot_general(
                jnp.concatenate(rows_then, axis=0), jnp.concatenate(rows_reduced, axis=0),
                (((0,), (0,)), ((), ())), precision=precise, preferred_element_type=jnp.float32,
            )
            for p in range(end, panels):
                kept = jnp.where(between(outer * SUB, end * SUB), 0.0, held[p])
                held[p] = kept - change[p * SUB : (p + 1) * SUB, :]


def factor_kernel(
    rows_total, packed_ref, filtered_ref, ortho_hbm, upper_hbm,
    upper_ref, inverse_ref, ortho_ref, sent, upper_sent,
):
    factor(unpack(packed_ref) * (1.0 / rows_total), upper_ref, inverse_ref)
    copies = [pltpu.make_async_copy(upper_ref, upper_hbm, upper_sent)]
    copies[0].start()
    high, low = two_parts(inverse_ref[...])
    right = jnp.concatenate([high, high, low], axis=1)
    chunks = sent.shape[0]
    per_chunk = filtered_ref.shape[0] // chunks
    for chunk in range(chunks):
        rows = pl.ds(chunk * per_chunk, per_chunk)
        high, low = two_parts(filtered_ref[rows, :])
        ortho_ref[rows, :] = lax.dot_general(
            jnp.concatenate([high, low, high], axis=1), right, (((1,), (1,)), ((), ())),
            preferred_element_type=jnp.float32,
        )
        copies.append(
            pltpu.make_async_copy(ortho_ref.at[rows, :], ortho_hbm.at[rows, :], sent.at[chunk])
        )
        copies[-1].start()
    for copy in copies:
        copy.wait()


def call(kernel, out_shape, in_specs, scratch=(), out_spec=vmem):
    return pl.pallas_call(
        kernel,
        out_shape=out_shape,
        in_specs=in_specs,
        out_specs=jax.tree.map(lambda _: out_spec, out_shape),
        scratch_shapes=list(scratch),
        compiler_params=pltpu.CompilerParams(vmem_limit_bytes=VMEM_LIMIT),
    )


def on_device(hamiltonian, block_columns, potential, trial_slab):
    shard_blocks, _, block_size, _ = hamiltonian.shape
    flat_rows, states = trial_slab.shape
    weights = potential.reshape(-1, LANES)
    rows_total = flat_rows * lax.axis_size("group") * lax.axis_size("blk")
    group, index = lax.axis_index("group"), lax.axis_index("blk")
    cycle_size = lax.axis_size("blk")
    levels = cycle_size.bit_length() - 1
    origins = [index]
    for level in range(levels):
        flip = jnp.left_shift(1, step_bits(group, level))
        origins += [jnp.bitwise_xor(origin, flip) for origin in origins]
    odd = group % 2
    origins += [cycle_size + 1 - odd, cycle_size + odd]
    index_array = jnp.concatenate(
        [block_columns.reshape(-1)] + [origin.reshape(1).astype(jnp.int32) for origin in origins]
    )
    last = cycle_size - 1
    ending = [cycle_size, last]
    middle = [1] + list(range(2, last)) + [cycle_size + 1]
    flat = jax.ShapeDtypeStruct((flat_rows, states), jnp.float32)
    rounded = jax.ShapeDtypeStruct((shard_blocks, block_size, states), jnp.bfloat16)
    packed = jax.ShapeDtypeStruct((states // 2 + SUB, states), jnp.float32)
    square = jax.ShapeDtypeStruct((states, states), jnp.float32)

    def own_part(index_array, value, *terms):
        return call(own_kernel, flat, [smem] + [vmem] * (2 + len(terms)))(
            index_array, hamiltonian, value, *terms
        )

    def coupled(value, index_array, early, *terms):
        arrived = cycle_exchange(value, 0)
        outer = pair_exchange(value, 1)
        if early:
            partial = own_part(index_array, value, *terms)
            later, partial = lax.optimization_barrier((value, partial))
        else:
            later, index_array = lax.optimization_barrier((value, index_array))
        others = [cycle_exchange(later, level) for level in range(1, levels)]
        arrived, later = lax.optimization_barrier((arrived, later))
        pieces = [value, arrived]
        for level, other in zip(range(1, levels), others):
            pieces += [other] + [cycle_exchange(piece, level) for piece in pieces[1:]]
        pieces += [pair_exchange(later, 0), outer]
        if not early:
            partial = own_part(index_array, value, *terms)
        partial = call(
            functools.partial(middle_kernel, middle), flat, [smem] + [vmem] * (2 + len(middle)),
        )(index_array, hamiltonian, partial, *[pieces[number] for number in middle])
        return [partial] + [pieces[number] for number in ending]

    weighted = (weights.reshape(-1, 1) * trial_slab)
    parts = coupled(trial_slab.reshape(rounded.shape).astype(jnp.bfloat16), index_array, False, weighted)
    once, once_round = call(
        functools.partial(first_kernel, ending), (flat, rounded), [smem] + [vmem] * 4
    )(index_array, hamiltonian, *parts)
    parts = coupled(once_round, index_array, True, weights, once, trial_slab)
    filtered, gram = call(
        functools.partial(second_kernel, ending), (flat, packed), [smem] + [vmem] * 4
    )(index_array, hamiltonian, *parts)
    gram = summed(gram)
    return call(
        functools.partial(factor_kernel, rows_total),
        (flat, square),
        [vmem, vmem],
        [
            pltpu.VMEM((states, states), jnp.float32),
            pltpu.VMEM((states, states), jnp.float32),
            pltpu.VMEM((flat_rows, states), jnp.float32),
            pltpu.SemaphoreType.DMA((4,)),
            pltpu.SemaphoreType.DMA,
        ],
        hbm,
    )(gram, filtered)


def solution(mesh):
    placed = (
        P(("group", "blk"), None, None, None),
        P(("group", "blk"), None, None),
        P(("group", "blk")),
        P(("group", "blk"), None),
    )
    return jax.shard_map(
        on_device,
        mesh=mesh,
        in_specs=placed,
        out_specs=(P(("group", "blk"), None), P()),
        check_vma=False,
    )
```

```python
import functools

import jax
import jax.numpy as jnp
from jax import lax
from jax.experimental import pallas as pl
from jax.experimental.pallas import tpu as pltpu
from jax.sharding import PartitionSpec as P

precise = lax.Precision.HIGHEST
LANES = 128
SUB = 8
OUTER = 4
VMEM_LIMIT = 40 * 1024 * 1024
vmem = pl.BlockSpec(memory_space=pltpu.VMEM)
hbm = pl.BlockSpec(memory_space=pl.ANY)
smem = pl.BlockSpec(memory_space=pltpu.SMEM)


def pair_exchange(value, offset):
    count = lax.axis_size("group")
    route = []
    for low in range(offset, count + offset, 2):
        first, second = low % count, (low + 1) % count
        route += [(first, second), (second, first)]
    return lax.ppermute(value, "group", route)


def step_bits(group, level):
    levels = lax.axis_size("blk").bit_length() - 1
    return jnp.where(group % 2 == 1, levels - 1 - level, level)


def cycle_exchange(value, level):
    groups, cycle_size = lax.axis_size("group"), lax.axis_size("blk")
    levels = cycle_size.bit_length() - 1
    route = []
    for group in range(groups):
        bit = levels - 1 - level if group % 2 else level
        route += [
            (group * cycle_size + index, group * cycle_size + (index ^ 1 << bit))
            for index in range(cycle_size)
        ]
    return lax.ppermute(value, ("group", "blk"), route)


def from_partner(value, axis, flip):
    count = lax.axis_size(axis)
    return lax.ppermute(value, axis, [(index, index ^ flip) for index in range(count)])


def summed(value):
    for axis, step in (("group", 1), ("group", 2), ("blk", 1)):
        count = 2 if (axis, step) == ("group", 1) else lax.axis_size(axis)
        while step < count:
            flips = [step, 2 * step, 3 * step] if 2 * step < count else [step]
            others = [from_partner(value, axis, flip) for flip in flips]
            value = value + others[0]
            if len(others) == 3:
                value = value + (others[1] + others[2])
            step *= len(flips) + 1
    return value


def potential_columns(potential_ref):
    return jnp.transpose(potential_ref[...])


def couple_row(index_ref, hamiltonian_ref, pieces, row):
    shard_blocks, sources, block_size, width = hamiltonian_ref.shape
    per_source = width // block_size
    total = None
    for number, piece_ref in pieces:
        source = index_ref[shard_blocks * sources * per_source + number]
        first = (row * sources + source) * per_source
        picked = jnp.concatenate(
            [piece_ref[index_ref[first + slot]] for slot in range(per_source)], axis=0
        )
        product = jnp.dot(
            hamiltonian_ref[row, source], picked, preferred_element_type=jnp.float32
        )
        if number == sources - 1:
            absent = index_ref[shard_blocks * sources * per_source + sources] != 0
            product = jnp.where(absent, 0.0, product)
        total = product if total is None else total + product
    return total


def own_kernel(index_ref, hamiltonian_ref, own_ref, *refs):
    terms, partial_ref = refs[:-1], refs[-1]
    shard_blocks, _, block_size, _ = hamiltonian_ref.shape
    per_column = LANES // block_size
    if len(terms) == 3:
        weights = potential_columns(terms[0])
    for row in range(shard_blocks):
        rows = pl.ds(row * block_size, block_size)
        if len(terms) == 3:
            column, part = divmod(row, per_column)
            weight = weights[part * block_size : (part + 1) * block_size, column : column + 1]
            total = weight * terms[1][rows, :] - terms[2][rows, :]
        else:
            total = terms[0][rows, :]
        partial_ref[rows, :] = total + couple_row(
            index_ref, hamiltonian_ref, [(0, own_ref)], row
        )


def middle_kernel(numbers, index_ref, hamiltonian_ref, partial_ref, *refs):
    pieces, sum_ref = list(zip(numbers, refs[:-1])), refs[-1]
    shard_blocks, _, block_size, _ = hamiltonian_ref.shape
    for row in range(shard_blocks):
        rows = pl.ds(row * block_size, block_size)
        sum_ref[rows, :] = partial_ref[rows, :] + couple_row(
            index_ref, hamiltonian_ref, pieces, row
        )


def first_kernel(numbers, index_ref, hamiltonian_ref, partial_ref, *refs):
    pieces, (once_ref, round_ref) = list(zip(numbers, refs)), refs[len(numbers) :]
    shard_blocks, _, block_size, _ = hamiltonian_ref.shape
    for row in range(shard_blocks):
        rows = pl.ds(row * block_size, block_size)
        once = 0.5 * (
            partial_ref[rows, :] + couple_row(index_ref, hamiltonian_ref, pieces, row)
        )
        once_ref[rows, :] = once
        round_ref[row] = once.astype(jnp.bfloat16)


def second_kernel(numbers, index_ref, hamiltonian_ref, partial_ref, *refs):
    pieces, (filtered_ref, packed_ref) = list(zip(numbers, refs)), refs[len(numbers) :]
    shard_blocks, _, block_size, _ = hamiltonian_ref.shape
    for row in range(shard_blocks):
        rows = pl.ds(row * block_size, block_size)
        filtered_ref[rows, :] = partial_ref[rows, :] + couple_row(
            index_ref, hamiltonian_ref, pieces, row
        )
    states = filtered_ref.shape[1]
    both = jnp.concatenate(two_parts(filtered_ref[...]), axis=1)
    products = lax.dot_general(
        both, both, (((0,), (0,)), ((), ())), preferred_element_type=jnp.float32
    )
    high, low = products[:states, :], products[states:, :]
    gram = high[:, :states] + (high[:, states:] + low[:, :states] + low[:, states:])
    pack(gram, packed_ref)


def two_parts(value):
    high = value.astype(jnp.bfloat16)
    return high, (value - high.astype(jnp.float32)).astype(jnp.bfloat16)


def pack(gram, packed_ref):
    size = gram.shape[0]
    half = size // 2
    row = lax.broadcasted_iota(jnp.int32, (half, size), 0)
    lane = lax.broadcasted_iota(jnp.int32, (half, size), 1)
    lower = gram[half:, :]
    packed_ref[pl.ds(0, half), :] = jnp.where(lane < row, pltpu.roll(lower, half, 1), gram[:half, :])
    diagonal = jnp.sum(jnp.where(lane == row + half, lower, 0.0), axis=0, keepdims=True)
    packed_ref[pl.ds(half, SUB), :] = jnp.broadcast_to(diagonal, (SUB, size))


def unpack(packed_ref):
    size = packed_ref.shape[1]
    half = size // 2
    row = lax.broadcasted_iota(jnp.int32, (size, size), 0)
    lane = lax.broadcasted_iota(jnp.int32, (size, size), 1)
    upper = packed_ref[pl.ds(0, half), :]
    both = jnp.concatenate([upper, pltpu.roll(upper, half, 1)], axis=0)
    held = ((row < half) & (lane > row)) | ((row >= half) & (lane >= half) & (lane < row))
    off_diagonal = jnp.where(held, both, 0.0)
    diagonal = jnp.where(row < half, both, packed_ref[pl.ds(half, 1), :])
    return off_diagonal + jnp.transpose(off_diagonal) + jnp.where(row == lane, diagonal, 0.0)


def inverse_of(value):
    estimate = pl.reciprocal(value, approx=True)
    estimate = estimate * (2.0 - value * estimate)
    return estimate * (2.0 - value * estimate)


def factor(gram, upper_ref, inverse_ref):
    size = gram.shape[1]
    panels = size // SUB
    shape = (SUB, size)
    row_index = lax.broadcasted_iota(jnp.int32, shape, 0)
    lane_index = lax.broadcasted_iota(jnp.int32, shape, 1)

    def along_lanes(panel, first):
        return [jnp.broadcast_to(panel[:, first + c : first + c + 1], shape) for c in range(SUB)]

    def along_rows(panel, row):
        return jnp.broadcast_to(panel[row : row + 1, :], shape)

    def between(low, high):
        return (lane_index >= low) & (lane_index < high)

    held = [gram[k * SUB : (k + 1) * SUB, :] for k in range(panels)]
    for outer in range(0, panels, OUTER):
        end = outer + OUTER
        rows_then, rows_reduced = [], []
        block = along_lanes(held[outer], outer * SUB)
        for k in range(outer, end):
            first = k * SUB
            below = {p: along_lanes(held[p], first) for p in range(k + 1, end)}
            after = list(below[k + 1]) if k + 1 < end else None
            following = along_lanes(held[k + 1], first + SUB) if k + 1 < end else None
            right = held[k]
            left = jnp.where(
                lane_index < first, held[k], jnp.where(lane_index == row_index + first, 1.0, 0.0)
            )
            pivots = jnp.ones(shape, jnp.float32)
            reciprocals = jnp.ones(shape, jnp.float32)
            for j in range(0, SUB, 2):
                a, b = along_rows(block[j], j), along_rows(block[j], j + 1)
                c = along_rows(block[j + 1], j + 1)
                determinant = a * c - b * b
                over = inverse_of(determinant)
                over_a = inverse_of(a)
                pivots = jnp.where(row_index == j, a, pivots)
                pivots = jnp.where(row_index == j + 1, determinant * over_a, pivots)
                reciprocals = jnp.where(row_index == j, over_a, reciprocals)
                reciprocals = jnp.where(row_index == j + 1, a * over, reciprocals)
                x, y = block[j], block[j + 1]
                one = jnp.where(row_index == j + 1, b * over_a, 0.0)
                one = jnp.where(row_index > j + 1, (x * c - y * b) * over, one)
                two = jnp.where(row_index > j + 1, (y * a - x * b) * over, 0.0)
                upper = {
                    n: (along_rows(block[n], j), along_rows(block[n], j + 1))
                    for n in range(j + 2, SUB)
                }
                for n in upper:
                    block[n] = block[n] - one * upper[n][0] - two * upper[n][1]
                if following is not None:
                    x, y = after[j], after[j + 1]
                    next_one, next_two = (x * c - y * b) * over, (y * a - x * b) * over
                    for n in range(SUB):
                        following[n] = (
                            following[n] - next_one * along_rows(x, n) - next_two * along_rows(y, n)
                        )
                    for n in upper:
                        after[n] = after[n] - next_one * upper[n][0] - next_two * upper[n][1]
                right = right - one * along_rows(right, j) - two * along_rows(right, j + 1)
                left = left - one * along_rows(left, j) - two * along_rows(left, j + 1)
            scale = lax.rsqrt(pivots)
            upper_ref[pl.ds(first, SUB), :] = jnp.where(
                lane_index >= row_index + first, right * scale, 0.0
            )
            inverse_ref[pl.ds(first, SUB), :] = left * scale
            if k + 1 < panels:
                reduced = jnp.where(lane_index >= first + SUB, right, left) * reciprocals
                for n in range(SUB - 1, 0, -1):
                    column = jnp.where(row_index < n, block[n] * reciprocals, 0.0)
                    reduced = reduced - column * along_rows(reduced, n)
                rows_then.append(held[k])
                rows_reduced.append(jnp.where(between(first + SUB, end * SUB), 0.0, reduced))
                rows = [along_rows(reduced, n) for n in range(SUB)]
                for p in below:
                    total = jnp.where(between(first, first + SUB), 0.0, held[p])
                    for n in range(SUB):
                        total = total - below[p][n] * rows[n]
                    held[p] = total
            block = following
        if end < panels:
            change = lax.dot_general(
                jnp.concatenate(rows_then, axis=0), jnp.concatenate(rows_reduced, axis=0),
                (((0,), (0,)), ((), ())), precision=precise, preferred_element_type=jnp.float32,
            )
            for p in range(end, panels):
                kept = jnp.where(between(outer * SUB, end * SUB), 0.0, held[p])
                held[p] = kept - change[p * SUB : (p + 1) * SUB, :]


def factor_kernel(
    rows_total, packed_ref, filtered_ref, ortho_hbm, upper_hbm,
    upper_ref, inverse_ref, ortho_ref, sent, upper_sent,
):
    factor(unpack(packed_ref) * (1.0 / rows_total), upper_ref, inverse_ref)
    copies = [pltpu.make_async_copy(upper_ref, upper_hbm, upper_sent)]
    copies[0].start()
    high, low = two_parts(inverse_ref[...])
    right = jnp.concatenate([high, high, low], axis=1)
    chunks = sent.shape[0]
    per_chunk = filtered_ref.shape[0] // chunks
    for chunk in range(chunks):
        rows = pl.ds(chunk * per_chunk, per_chunk)
        high, low = two_parts(filtered_ref[rows, :])
        ortho_ref[rows, :] = lax.dot_general(
            jnp.concatenate([high, low, high], axis=1), right, (((1,), (1,)), ((), ())),
            preferred_element_type=jnp.float32,
        )
        copies.append(
            pltpu.make_async_copy(ortho_ref.at[rows, :], ortho_hbm.at[rows, :], sent.at[chunk])
        )
        copies[-1].start()
    for copy in copies:
        copy.wait()


def call(kernel, out_shape, in_specs, scratch=(), out_spec=vmem):
    return pl.pallas_call(
        kernel,
        out_shape=out_shape,
        in_specs=in_specs,
        out_specs=jax.tree.map(lambda _: out_spec, out_shape),
        scratch_shapes=list(scratch),
        compiler_params=pltpu.CompilerParams(vmem_limit_bytes=VMEM_LIMIT),
    )


def on_device(hamiltonian, block_columns, potential, trial_slab):
    shard_blocks, _, block_size, _ = hamiltonian.shape
    flat_rows, states = trial_slab.shape
    weights = potential.reshape(-1, LANES)
    rows_total = flat_rows * lax.axis_size("group") * lax.axis_size("blk")
    group, index = lax.axis_index("group"), lax.axis_index("blk")
    cycle_size = lax.axis_size("blk")
    levels = cycle_size.bit_length() - 1
    origins = [index]
    for level in range(levels):
        flip = jnp.left_shift(1, step_bits(group, level))
        origins += [jnp.bitwise_xor(origin, flip) for origin in origins]
    odd = group % 2
    origins += [cycle_size + 1 - odd, cycle_size + odd]
    origins.append((group == 0) | (group == lax.axis_size("group") - 1))
    index_array = jnp.concatenate(
        [block_columns.reshape(-1)] + [origin.reshape(1).astype(jnp.int32) for origin in origins]
    )
    last = cycle_size - 1
    ending = [cycle_size, last]
    middle = list(range(1, last)) + [cycle_size + 1]
    flat = jax.ShapeDtypeStruct((flat_rows, states), jnp.float32)
    rounded = jax.ShapeDtypeStruct((shard_blocks, block_size, states), jnp.bfloat16)
    packed = jax.ShapeDtypeStruct((states // 2 + SUB, states), jnp.float32)
    square = jax.ShapeDtypeStruct((states, states), jnp.float32)

    def own_part(index_array, value, *terms):
        return call(own_kernel, flat, [smem] + [vmem] * (2 + len(terms)))(
            index_array, hamiltonian, value, *terms
        )

    def coupled(value, index_array, early, *terms):
        arrived = cycle_exchange(value, 0)
        outer = pair_exchange(value, 1)
        if early:
            partial = own_part(index_array, value, *terms)
            later, partial = lax.optimization_barrier((value, partial))
        else:
            later, index_array = lax.optimization_barrier((value, index_array))
        others = [cycle_exchange(later, level) for level in range(1, levels)]
        arrived, later = lax.optimization_barrier((arrived, later))
        pieces = [value, arrived]
        for level, other in zip(range(1, levels), others):
            pieces += [other] + [cycle_exchange(piece, level) for piece in pieces[1:]]
        pieces += [pair_exchange(later, 0), outer]
        if not early:
            partial = own_part(index_array, value, *terms)
        partial = call(
            functools.partial(middle_kernel, middle), flat, [smem] + [vmem] * (2 + len(middle)),
        )(index_array, hamiltonian, partial, *[pieces[number] for number in middle])
        return [partial] + [pieces[number] for number in ending]

    weighted = (weights.reshape(-1, 1) * trial_slab)
    parts = coupled(trial_slab.reshape(rounded.shape).astype(jnp.bfloat16), index_array, False, weighted)
    once, once_round = call(
        functools.partial(first_kernel, ending), (flat, rounded), [smem] + [vmem] * 4
    )(index_array, hamiltonian, *parts)
    parts = coupled(once_round, index_array, True, weights, once, trial_slab)
    filtered, gram = call(
        functools.partial(second_kernel, ending), (flat, packed), [smem] + [vmem] * 4
    )(index_array, hamiltonian, *parts)
    gram = summed(gram)
    return call(
        functools.partial(factor_kernel, rows_total),
        (flat, square),
        [vmem, vmem],
        [
            pltpu.VMEM((states, states), jnp.float32),
            pltpu.VMEM((states, states), jnp.float32),
            pltpu.VMEM((flat_rows, states), jnp.float32),
            pltpu.SemaphoreType.DMA((4,)),
            pltpu.SemaphoreType.DMA,
        ],
        hbm,
    )(gram, filtered)


def solution(mesh):
    placed = (
        P(("group", "blk"), None, None, None),
        P(("group", "blk"), None, None),
        P(("group", "blk")),
        P(("group", "blk"), None),
    )
    return jax.shard_map(
        on_device,
        mesh=mesh,
        in_specs=placed,
        out_specs=(P(("group", "blk"), None), P()),
        check_vma=False,
    )
```

```python
import functools

import jax
import jax.numpy as jnp
from jax import lax
from jax.experimental import pallas as pl
from jax.experimental.pallas import tpu as pltpu
from jax.sharding import PartitionSpec as P

precise = lax.Precision.HIGHEST
LANES = 128
SUB = 8
OUTER = 4
VMEM_LIMIT = 40 * 1024 * 1024
vmem = pl.BlockSpec(memory_space=pltpu.VMEM)
hbm = pl.BlockSpec(memory_space=pl.ANY)
smem = pl.BlockSpec(memory_space=pltpu.SMEM)


def pair_exchange(value, offset):
    count = lax.axis_size("group")
    route = []
    for low in range(offset, count - 1, 2):
        route += [(low, low + 1), (low + 1, low)]
    return lax.ppermute(value, "group", route)


def step_bits(group, level):
    levels = lax.axis_size("blk").bit_length() - 1
    return jnp.where(group % 2 == 1, levels - 1 - level, level)


def cycle_exchange(value, level):
    groups, cycle_size = lax.axis_size("group"), lax.axis_size("blk")
    levels = cycle_size.bit_length() - 1
    route = []
    for group in range(groups):
        bit = levels - 1 - level if group % 2 else level
        route += [
            (group * cycle_size + index, group * cycle_size + (index ^ 1 << bit))
            for index in range(cycle_size)
        ]
    return lax.ppermute(value, ("group", "blk"), route)


def from_partner(value, axis, flip):
    count = lax.axis_size(axis)
    return lax.ppermute(value, axis, [(index, index ^ flip) for index in range(count)])


def summed(value):
    for axis, step in (("group", 1), ("group", 2), ("blk", 1)):
        count = 2 if (axis, step) == ("group", 1) else lax.axis_size(axis)
        while step < count:
            flips = [step, 2 * step, 3 * step] if 2 * step < count else [step]
            others = [from_partner(value, axis, flip) for flip in flips]
            value = value + others[0]
            if len(others) == 3:
                value = value + (others[1] + others[2])
            step *= len(flips) + 1
    return value


def potential_columns(potential_ref):
    return jnp.transpose(potential_ref[...])


def couple_row(index_ref, hamiltonian_ref, pieces, row):
    shard_blocks, sources, block_size, width = hamiltonian_ref.shape
    per_source = width // block_size
    total = None
    for number, piece_ref in pieces:
        source = index_ref[shard_blocks * sources * per_source + number]
        first = (row * sources + source) * per_source
        picked = jnp.concatenate(
            [piece_ref[index_ref[first + slot]] for slot in range(per_source)], axis=0
        )
        product = jnp.dot(
            hamiltonian_ref[row, source], picked, preferred_element_type=jnp.float32
        )
        total = product if total is None else total + product
    return total


def own_kernel(index_ref, hamiltonian_ref, own_ref, *refs):
    terms, partial_ref = refs[:-1], refs[-1]
    shard_blocks, _, block_size, _ = hamiltonian_ref.shape
    per_column = LANES // block_size
    if len(terms) == 3:
        weights = potential_columns(terms[0])
    for row in range(shard_blocks):
        rows = pl.ds(row * block_size, block_size)
        if len(terms) == 3:
            column, part = divmod(row, per_column)
            weight = weights[part * block_size : (part + 1) * block_size, column : column + 1]
            total = weight * terms[1][rows, :] - terms[2][rows, :]
        else:
            total = terms[0][rows, :]
        partial_ref[rows, :] = total + couple_row(
            index_ref, hamiltonian_ref, [(0, own_ref)], row
        )


def middle_kernel(numbers, index_ref, hamiltonian_ref, partial_ref, *refs):
    pieces, sum_ref = list(zip(numbers, refs[:-1])), refs[-1]
    shard_blocks, _, block_size, _ = hamiltonian_ref.shape
    for row in range(shard_blocks):
        rows = pl.ds(row * block_size, block_size)
        sum_ref[rows, :] = partial_ref[rows, :] + couple_row(
            index_ref, hamiltonian_ref, pieces, row
        )


def first_kernel(numbers, index_ref, hamiltonian_ref, partial_ref, *refs):
    pieces, (once_ref, round_ref) = list(zip(numbers, refs)), refs[len(numbers) :]
    shard_blocks, _, block_size, _ = hamiltonian_ref.shape
    for row in range(shard_blocks):
        rows = pl.ds(row * block_size, block_size)
        once = 0.5 * (
            partial_ref[rows, :] + couple_row(index_ref, hamiltonian_ref, pieces, row)
        )
        once_ref[rows, :] = once
        round_ref[row] = once.astype(jnp.bfloat16)


def second_kernel(numbers, index_ref, hamiltonian_ref, partial_ref, *refs):
    pieces, (filtered_ref, packed_ref) = list(zip(numbers, refs)), refs[len(numbers) :]
    shard_blocks, _, block_size, _ = hamiltonian_ref.shape
    for row in range(shard_blocks):
        rows = pl.ds(row * block_size, block_size)
        filtered_ref[rows, :] = partial_ref[rows, :] + couple_row(
            index_ref, hamiltonian_ref, pieces, row
        )
    states = filtered_ref.shape[1]
    both = jnp.concatenate(two_parts(filtered_ref[...]), axis=1)
    products = lax.dot_general(
        both, both, (((0,), (0,)), ((), ())), preferred_element_type=jnp.float32
    )
    high, low = products[:states, :], products[states:, :]
    gram = high[:, :states] + (high[:, states:] + low[:, :states] + low[:, states:])
    pack(gram, packed_ref)


def two_parts(value):
    high = value.astype(jnp.bfloat16)
    return high, (value - high.astype(jnp.float32)).astype(jnp.bfloat16)


def pack(gram, packed_ref):
    size = gram.shape[0]
    half = size // 2
    row = lax.broadcasted_iota(jnp.int32, (half, size), 0)
    lane = lax.broadcasted_iota(jnp.int32, (half, size), 1)
    lower = gram[half:, :]
    packed_ref[pl.ds(0, half), :] = jnp.where(lane < row, pltpu.roll(lower, half, 1), gram[:half, :])
    diagonal = jnp.sum(jnp.where(lane == row + half, lower, 0.0), axis=0, keepdims=True)
    packed_ref[pl.ds(half, SUB), :] = jnp.broadcast_to(diagonal, (SUB, size))


def unpack(packed_ref):
    size = packed_ref.shape[1]
    half = size // 2
    row = lax.broadcasted_iota(jnp.int32, (size, size), 0)
    lane = lax.broadcasted_iota(jnp.int32, (size, size), 1)
    upper = packed_ref[pl.ds(0, half), :]
    both = jnp.concatenate([upper, pltpu.roll(upper, half, 1)], axis=0)
    held = ((row < half) & (lane > row)) | ((row >= half) & (lane >= half) & (lane < row))
    off_diagonal = jnp.where(held, both, 0.0)
    diagonal = jnp.where(row < half, both, packed_ref[pl.ds(half, 1), :])
    return off_diagonal + jnp.transpose(off_diagonal) + jnp.where(row == lane, diagonal, 0.0)


def inverse_of(value):
    estimate = pl.reciprocal(value, approx=True)
    estimate = estimate * (2.0 - value * estimate)
    return estimate * (2.0 - value * estimate)


def factor(gram, upper_ref, inverse_ref):
    size = gram.shape[1]
    panels = size // SUB
    shape = (SUB, size)
    row_index = lax.broadcasted_iota(jnp.int32, shape, 0)
    lane_index = lax.broadcasted_iota(jnp.int32, shape, 1)

    def along_lanes(panel, first):
        return [jnp.broadcast_to(panel[:, first + c : first + c + 1], shape) for c in range(SUB)]

    def along_rows(panel, row):
        return jnp.broadcast_to(panel[row : row + 1, :], shape)

    def between(low, high):
        return (lane_index >= low) & (lane_index < high)

    held = [gram[k * SUB : (k + 1) * SUB, :] for k in range(panels)]
    for outer in range(0, panels, OUTER):
        end = outer + OUTER
        rows_then, rows_reduced = [], []
        block = along_lanes(held[outer], outer * SUB)
        for k in range(outer, end):
            first = k * SUB
            below = {p: along_lanes(held[p], first) for p in range(k + 1, end)}
            after = list(below[k + 1]) if k + 1 < end else None
            following = along_lanes(held[k + 1], first + SUB) if k + 1 < end else None
            right = held[k]
            left = jnp.where(
                lane_index < first, held[k], jnp.where(lane_index == row_index + first, 1.0, 0.0)
            )
            pivots = jnp.ones(shape, jnp.float32)
            reciprocals = jnp.ones(shape, jnp.float32)
            for j in range(0, SUB, 2):
                a, b = along_rows(block[j], j), along_rows(block[j], j + 1)
                c = along_rows(block[j + 1], j + 1)
                determinant = a * c - b * b
                over = inverse_of(determinant)
                over_a = inverse_of(a)
                pivots = jnp.where(row_index == j, a, pivots)
                pivots = jnp.where(row_index == j + 1, determinant * over_a, pivots)
                reciprocals = jnp.where(row_index == j, over_a, reciprocals)
                reciprocals = jnp.where(row_index == j + 1, a * over, reciprocals)
                x, y = block[j], block[j + 1]
                one = jnp.where(row_index == j + 1, b * over_a, 0.0)
                one = jnp.where(row_index > j + 1, (x * c - y * b) * over, one)
                two = jnp.where(row_index > j + 1, (y * a - x * b) * over, 0.0)
                upper = {
                    n: (along_rows(block[n], j), along_rows(block[n], j + 1))
                    for n in range(j + 2, SUB)
                }
                for n in upper:
                    block[n] = block[n] - one * upper[n][0] - two * upper[n][1]
                if following is not None:
                    x, y = after[j], after[j + 1]
                    next_one, next_two = (x * c - y * b) * over, (y * a - x * b) * over
                    for n in range(SUB):
                        following[n] = (
                            following[n] - next_one * along_rows(x, n) - next_two * along_rows(y, n)
                        )
                    for n in upper:
                        after[n] = after[n] - next_one * upper[n][0] - next_two * upper[n][1]
                right = right - one * along_rows(right, j) - two * along_rows(right, j + 1)
                left = left - one * along_rows(left, j) - two * along_rows(left, j + 1)
            scale = lax.rsqrt(pivots)
            upper_ref[pl.ds(first, SUB), :] = jnp.where(
                lane_index >= row_index + first, right * scale, 0.0
            )
            inverse_ref[pl.ds(first, SUB), :] = left * scale
            if k + 1 < panels:
                reduced = jnp.where(lane_index >= first + SUB, right, left) * reciprocals
                for n in range(SUB - 1, 0, -1):
                    column = jnp.where(row_index < n, block[n] * reciprocals, 0.0)
                    reduced = reduced - column * along_rows(reduced, n)
                rows_then.append(held[k])
                rows_reduced.append(jnp.where(between(first + SUB, end * SUB), 0.0, reduced))
                rows = [along_rows(reduced, n) for n in range(SUB)]
                for p in below:
                    total = jnp.where(between(first, first + SUB), 0.0, held[p])
                    for n in range(SUB):
                        total = total - below[p][n] * rows[n]
                    held[p] = total
            block = following
        if end < panels:
            change = lax.dot_general(
                jnp.concatenate(rows_then, axis=0), jnp.concatenate(rows_reduced, axis=0),
                (((0,), (0,)), ((), ())), precision=precise, preferred_element_type=jnp.float32,
            )
            for p in range(end, panels):
                kept = jnp.where(between(outer * SUB, end * SUB), 0.0, held[p])
                held[p] = kept - change[p * SUB : (p + 1) * SUB, :]


def factor_kernel(
    rows_total, packed_ref, filtered_ref, ortho_hbm, upper_hbm,
    upper_ref, inverse_ref, ortho_ref, sent, upper_sent,
):
    factor(unpack(packed_ref) * (1.0 / rows_total), upper_ref, inverse_ref)
    copies = [pltpu.make_async_copy(upper_ref, upper_hbm, upper_sent)]
    copies[0].start()
    high, low = two_parts(inverse_ref[...])
    right = jnp.concatenate([high, high, low], axis=1)
    chunks = sent.shape[0]
    per_chunk = filtered_ref.shape[0] // chunks
    for chunk in range(chunks):
        rows = pl.ds(chunk * per_chunk, per_chunk)
        high, low = two_parts(filtered_ref[rows, :])
        ortho_ref[rows, :] = lax.dot_general(
            jnp.concatenate([high, low, high], axis=1), right, (((1,), (1,)), ((), ())),
            preferred_element_type=jnp.float32,
        )
        copies.append(
            pltpu.make_async_copy(ortho_ref.at[rows, :], ortho_hbm.at[rows, :], sent.at[chunk])
        )
        copies[-1].start()
    for copy in copies:
        copy.wait()


def call(kernel, out_shape, in_specs, scratch=(), out_spec=vmem):
    return pl.pallas_call(
        kernel,
        out_shape=out_shape,
        in_specs=in_specs,
        out_specs=jax.tree.map(lambda _: out_spec, out_shape),
        scratch_shapes=list(scratch),
        compiler_params=pltpu.CompilerParams(vmem_limit_bytes=VMEM_LIMIT),
    )


def on_device(hamiltonian, block_columns, potential, trial_slab):
    shard_blocks, _, block_size, _ = hamiltonian.shape
    flat_rows, states = trial_slab.shape
    weights = potential.reshape(-1, LANES)
    rows_total = flat_rows * lax.axis_size("group") * lax.axis_size("blk")
    group, index = lax.axis_index("group"), lax.axis_index("blk")
    cycle_size = lax.axis_size("blk")
    levels = cycle_size.bit_length() - 1
    origins = [index]
    for level in range(levels):
        flip = jnp.left_shift(1, step_bits(group, level))
        origins += [jnp.bitwise_xor(origin, flip) for origin in origins]
    odd = group % 2
    origins += [cycle_size + 1 - odd, cycle_size + odd]
    index_array = jnp.concatenate(
        [block_columns.reshape(-1)] + [origin.reshape(1).astype(jnp.int32) for origin in origins]
    )
    last = cycle_size - 1
    ending = [last]
    middle = [cycle_size, 1] + list(range(2, last)) + [cycle_size + 1]
    flat = jax.ShapeDtypeStruct((flat_rows, states), jnp.float32)
    rounded = jax.ShapeDtypeStruct((shard_blocks, block_size, states), jnp.bfloat16)
    packed = jax.ShapeDtypeStruct((states // 2 + SUB, states), jnp.float32)
    square = jax.ShapeDtypeStruct((states, states), jnp.float32)

    def own_part(index_array, value, *terms):
        return call(own_kernel, flat, [smem] + [vmem] * (2 + len(terms)))(
            index_array, hamiltonian, value, *terms
        )

    def coupled(value, index_array, early, *terms):
        arrived = cycle_exchange(value, 0)
        pairs = [pair_exchange(value, 0), pair_exchange(value, 1)]
        if early:
            partial = own_part(index_array, value, *terms)
            later, pairs[0], partial = lax.optimization_barrier((value, pairs[0], partial))
        else:
            later, pairs[0], index_array = lax.optimization_barrier((value, pairs[0], index_array))
        others = [cycle_exchange(later, level) for level in range(1, levels)]
        pieces = [value, arrived]
        for level, other in zip(range(1, levels), others):
            pieces += [other] + [cycle_exchange(piece, level) for piece in pieces[1:]]
        pieces += pairs
        if not early:
            partial = own_part(index_array, value, *terms)
        partial = call(
            functools.partial(middle_kernel, middle), flat, [smem] + [vmem] * (2 + len(middle)),
        )(index_array, hamiltonian, partial, *[pieces[number] for number in middle])
        return [partial] + [pieces[number] for number in ending]

    weighted = (weights.reshape(-1, 1) * trial_slab)
    parts = coupled(trial_slab.reshape(rounded.shape).astype(jnp.bfloat16), index_array, False, weighted)
    once, once_round = call(
        functools.partial(first_kernel, ending), (flat, rounded), [smem] + [vmem] * (2 + len(ending))
    )(index_array, hamiltonian, *parts)
    parts = coupled(once_round, index_array, True, weights, once, trial_slab)
    filtered, gram = call(
        functools.partial(second_kernel, ending), (flat, packed), [smem] + [vmem] * (2 + len(ending))
    )(index_array, hamiltonian, *parts)
    gram = summed(gram)
    return call(
        functools.partial(factor_kernel, rows_total),
        (flat, square),
        [vmem, vmem],
        [
            pltpu.VMEM((states, states), jnp.float32),
            pltpu.VMEM((states, states), jnp.float32),
            pltpu.VMEM((flat_rows, states), jnp.float32),
            pltpu.SemaphoreType.DMA((4,)),
            pltpu.SemaphoreType.DMA,
        ],
        hbm,
    )(gram, filtered)


def solution(mesh):
    placed = (
        P(("group", "blk"), None, None, None),
        P(("group", "blk"), None, None),
        P(("group", "blk")),
        P(("group", "blk"), None),
    )
    return jax.shard_map(
        on_device,
        mesh=mesh,
        in_specs=placed,
        out_specs=(P(("group", "blk"), None), P()),
        check_vma=False,
    )
```

```python
import functools

import jax
import jax.numpy as jnp
from jax import lax
from jax.experimental import pallas as pl
from jax.experimental.pallas import tpu as pltpu
from jax.sharding import PartitionSpec as P

precise = lax.Precision.HIGHEST
LANES = 128
SUB = 8
OUTER = 4
VMEM_LIMIT = 40 * 1024 * 1024
vmem = pl.BlockSpec(memory_space=pltpu.VMEM)
hbm = pl.BlockSpec(memory_space=pl.ANY)
smem = pl.BlockSpec(memory_space=pltpu.SMEM)


def pair_exchange(value, offset):
    count = lax.axis_size("group")
    route = []
    for low in range(offset, count - 1, 2):
        route += [(low, low + 1), (low + 1, low)]
    return lax.ppermute(value, "group", route)


def step_bits(group, level):
    levels = lax.axis_size("blk").bit_length() - 1
    return jnp.where(group % 2 == 1, levels - 1 - level, level)


def cycle_exchange(value, level):
    groups, cycle_size = lax.axis_size("group"), lax.axis_size("blk")
    levels = cycle_size.bit_length() - 1
    route = []
    for group in range(groups):
        bit = levels - 1 - level if group % 2 else level
        route += [
            (group * cycle_size + index, group * cycle_size + (index ^ 1 << bit))
            for index in range(cycle_size)
        ]
    return lax.ppermute(value, ("group", "blk"), route)


def from_partner(value, axis, flip):
    count = lax.axis_size(axis)
    return lax.ppermute(value, axis, [(index, index ^ flip) for index in range(count)])


def summed(value):
    for axis, step in (("group", 1), ("group", 2), ("blk", 1)):
        count = 2 if (axis, step) == ("group", 1) else lax.axis_size(axis)
        while step < count:
            flips = [step, 2 * step, 3 * step] if 2 * step < count else [step]
            others = [from_partner(value, axis, flip) for flip in flips]
            value = others[0] + value
            if len(others) == 3:
                value = (others[2] + others[1]) + value
            step *= len(flips) + 1
    return value


def potential_columns(potential_ref):
    return jnp.transpose(potential_ref[...])


def couple_row(index_ref, hamiltonian_ref, pieces, row):
    shard_blocks, sources, block_size, width = hamiltonian_ref.shape
    per_source = width // block_size
    total = None
    for number, piece_ref in pieces:
        source = index_ref[shard_blocks * sources * per_source + number]
        first = (row * sources + source) * per_source
        picked = jnp.concatenate(
            [piece_ref[index_ref[first + slot]] for slot in range(per_source)], axis=0
        )
        product = jnp.dot(
            hamiltonian_ref[row, source], picked, preferred_element_type=jnp.float32
        )
        total = product if total is None else total + product
    return total


def own_kernel(index_ref, hamiltonian_ref, own_ref, *refs):
    terms, partial_ref = refs[:-1], refs[-1]
    shard_blocks, _, block_size, _ = hamiltonian_ref.shape
    per_column = LANES // block_size
    if len(terms) == 3:
        weights = potential_columns(terms[0])
    for row in range(shard_blocks):
        rows = pl.ds(row * block_size, block_size)
        if len(terms) == 3:
            column, part = divmod(row, per_column)
            weight = weights[part * block_size : (part + 1) * block_size, column : column + 1]
            total = weight * terms[1][rows, :] - terms[2][rows, :]
        else:
            total = terms[0][rows, :]
        partial_ref[rows, :] = total + couple_row(
            index_ref, hamiltonian_ref, [(0, own_ref)], row
        )


def middle_kernel(numbers, index_ref, hamiltonian_ref, partial_ref, *refs):
    pieces, sum_ref = list(zip(numbers, refs[:-1])), refs[-1]
    shard_blocks, _, block_size, _ = hamiltonian_ref.shape
    for row in range(shard_blocks):
        rows = pl.ds(row * block_size, block_size)
        sum_ref[rows, :] = partial_ref[rows, :] + couple_row(
            index_ref, hamiltonian_ref, pieces, row
        )


def first_kernel(numbers, index_ref, hamiltonian_ref, partial_ref, *refs):
    pieces, (once_ref, round_ref) = list(zip(numbers, refs)), refs[len(numbers) :]
    shard_blocks, _, block_size, _ = hamiltonian_ref.shape
    for row in range(shard_blocks):
        rows = pl.ds(row * block_size, block_size)
        once = 0.5 * (
            partial_ref[rows, :] + couple_row(index_ref, hamiltonian_ref, pieces, row)
        )
        once_ref[rows, :] = once
        round_ref[row] = once.astype(jnp.bfloat16)


def second_kernel(numbers, index_ref, hamiltonian_ref, partial_ref, *refs):
    pieces, (filtered_ref, packed_ref) = list(zip(numbers, refs)), refs[len(numbers) :]
    shard_blocks, _, block_size, _ = hamiltonian_ref.shape
    for row in range(shard_blocks):
        rows = pl.ds(row * block_size, block_size)
        filtered_ref[rows, :] = partial_ref[rows, :] + couple_row(
            index_ref, hamiltonian_ref, pieces, row
        )
    states = filtered_ref.shape[1]
    both = jnp.concatenate(two_parts(filtered_ref[...]), axis=1)
    products = lax.dot_general(
        both, both, (((0,), (0,)), ((), ())), preferred_element_type=jnp.float32
    )
    high, low = products[:states, :], products[states:, :]
    gram = high[:, :states] + (high[:, states:] + low[:, :states] + low[:, states:])
    pack(gram, packed_ref)


def two_parts(value):
    high = value.astype(jnp.bfloat16)
    return high, (value - high.astype(jnp.float32)).astype(jnp.bfloat16)


def pack(gram, packed_ref):
    size = gram.shape[0]
    half = size // 2
    row = lax.broadcasted_iota(jnp.int32, (half, size), 0)
    lane = lax.broadcasted_iota(jnp.int32, (half, size), 1)
    lower = gram[half:, :]
    packed_ref[pl.ds(0, half), :] = jnp.where(lane < row, pltpu.roll(lower, half, 1), gram[:half, :])
    diagonal = jnp.sum(jnp.where(lane == row + half, lower, 0.0), axis=0, keepdims=True)
    packed_ref[pl.ds(half, SUB), :] = jnp.broadcast_to(diagonal, (SUB, size))


def unpack(packed_ref):
    size = packed_ref.shape[1]
    half = size // 2
    row = lax.broadcasted_iota(jnp.int32, (size, size), 0)
    lane = lax.broadcasted_iota(jnp.int32, (size, size), 1)
    upper = packed_ref[pl.ds(0, half), :]
    both = jnp.concatenate([upper, pltpu.roll(upper, half, 1)], axis=0)
    held = ((row < half) & (lane > row)) | ((row >= half) & (lane >= half) & (lane < row))
    off_diagonal = jnp.where(held, both, 0.0)
    diagonal = jnp.where(row < half, both, packed_ref[pl.ds(half, 1), :])
    return off_diagonal + jnp.transpose(off_diagonal) + jnp.where(row == lane, diagonal, 0.0)


def inverse_of(value):
    estimate = pl.reciprocal(value, approx=True)
    estimate = estimate * (2.0 - value * estimate)
    return estimate * (2.0 - value * estimate)


def factor(gram, upper_ref, inverse_ref):
    size = gram.shape[1]
    panels = size // SUB
    shape = (SUB, size)
    row_index = lax.broadcasted_iota(jnp.int32, shape, 0)
    lane_index = lax.broadcasted_iota(jnp.int32, shape, 1)

    def along_lanes(panel, first):
        return [jnp.broadcast_to(panel[:, first + c : first + c + 1], shape) for c in range(SUB)]

    def along_rows(panel, row):
        return jnp.broadcast_to(panel[row : row + 1, :], shape)

    def between(low, high):
        return (lane_index >= low) & (lane_index < high)

    held = [gram[k * SUB : (k + 1) * SUB, :] for k in range(panels)]
    for outer in range(0, panels, OUTER):
        end = outer + OUTER
        rows_then, rows_reduced = [], []
        block = along_lanes(held[outer], outer * SUB)
        for k in range(outer, end):
            first = k * SUB
            below = {p: along_lanes(held[p], first) for p in range(k + 1, end)}
            after = list(below[k + 1]) if k + 1 < end else None
            following = along_lanes(held[k + 1], first + SUB) if k + 1 < end else None
            right = held[k]
            left = jnp.where(
                lane_index < first, held[k], jnp.where(lane_index == row_index + first, 1.0, 0.0)
            )
            pivots = jnp.ones(shape, jnp.float32)
            reciprocals = jnp.ones(shape, jnp.float32)
            for j in range(0, SUB, 2):
                a, b = along_rows(block[j], j), along_rows(block[j], j + 1)
                c = along_rows(block[j + 1], j + 1)
                determinant = a * c - b * b
                over = inverse_of(determinant)
                over_a = inverse_of(a)
                pivots = jnp.where(row_index == j, a, pivots)
                pivots = jnp.where(row_index == j + 1, determinant * over_a, pivots)
                reciprocals = jnp.where(row_index == j, over_a, reciprocals)
                reciprocals = jnp.where(row_index == j + 1, a * over, reciprocals)
                x, y = block[j], block[j + 1]
                one = jnp.where(row_index == j + 1, b * over_a, 0.0)
                one = jnp.where(row_index > j + 1, (x * c - y * b) * over, one)
                two = jnp.where(row_index > j + 1, (y * a - x * b) * over, 0.0)
                upper = {
                    n: (along_rows(block[n], j), along_rows(block[n], j + 1))
                    for n in range(j + 2, SUB)
                }
                for n in upper:
                    block[n] = block[n] - one * upper[n][0] - two * upper[n][1]
                if following is not None:
                    x, y = after[j], after[j + 1]
                    next_one, next_two = (x * c - y * b) * over, (y * a - x * b) * over
                    for n in range(SUB):
                        following[n] = (
                            following[n] - next_one * along_rows(x, n) - next_two * along_rows(y, n)
                        )
                    for n in upper:
                        after[n] = after[n] - next_one * upper[n][0] - next_two * upper[n][1]
                right = right - one * along_rows(right, j) - two * along_rows(right, j + 1)
                left = left - one * along_rows(left, j) - two * along_rows(left, j + 1)
            scale = lax.rsqrt(pivots)
            upper_ref[pl.ds(first, SUB), :] = jnp.where(
                lane_index >= row_index + first, right * scale, 0.0
            )
            inverse_ref[pl.ds(first, SUB), :] = left * scale
            if k + 1 < panels:
                reduced = jnp.where(lane_index >= first + SUB, right, left) * reciprocals
                for n in range(SUB - 1, 0, -1):
                    column = jnp.where(row_index < n, block[n] * reciprocals, 0.0)
                    reduced = reduced - column * along_rows(reduced, n)
                rows_then.append(held[k])
                rows_reduced.append(jnp.where(between(first + SUB, end * SUB), 0.0, reduced))
                rows = [along_rows(reduced, n) for n in range(SUB)]
                for p in below:
                    total = jnp.where(between(first, first + SUB), 0.0, held[p])
                    for n in range(SUB):
                        total = total - below[p][n] * rows[n]
                    held[p] = total
            block = following
        if end < panels:
            change = lax.dot_general(
                jnp.concatenate(rows_then, axis=0), jnp.concatenate(rows_reduced, axis=0),
                (((0,), (0,)), ((), ())), precision=precise, preferred_element_type=jnp.float32,
            )
            for p in range(end, panels):
                kept = jnp.where(between(outer * SUB, end * SUB), 0.0, held[p])
                held[p] = kept - change[p * SUB : (p + 1) * SUB, :]


def factor_kernel(
    rows_total, packed_ref, filtered_ref, ortho_hbm, upper_hbm,
    upper_ref, inverse_ref, ortho_ref, sent, upper_sent,
):
    factor(unpack(packed_ref) * (1.0 / rows_total), upper_ref, inverse_ref)
    copies = [pltpu.make_async_copy(upper_ref, upper_hbm, upper_sent)]
    copies[0].start()
    high, low = two_parts(inverse_ref[...])
    right = jnp.concatenate([high, high, low], axis=1)
    chunks = sent.shape[0]
    per_chunk = filtered_ref.shape[0] // chunks
    for chunk in range(chunks):
        rows = pl.ds(chunk * per_chunk, per_chunk)
        high, low = two_parts(filtered_ref[rows, :])
        ortho_ref[rows, :] = lax.dot_general(
            jnp.concatenate([high, low, high], axis=1), right, (((1,), (1,)), ((), ())),
            preferred_element_type=jnp.float32,
        )
        copies.append(
            pltpu.make_async_copy(ortho_ref.at[rows, :], ortho_hbm.at[rows, :], sent.at[chunk])
        )
        copies[-1].start()
    for copy in copies:
        copy.wait()


def call(kernel, out_shape, in_specs, scratch=(), out_spec=vmem):
    return pl.pallas_call(
        kernel,
        out_shape=out_shape,
        in_specs=in_specs,
        out_specs=jax.tree.map(lambda _: out_spec, out_shape),
        scratch_shapes=list(scratch),
        compiler_params=pltpu.CompilerParams(vmem_limit_bytes=VMEM_LIMIT),
    )


def on_device(hamiltonian, block_columns, potential, trial_slab):
    shard_blocks, _, block_size, _ = hamiltonian.shape
    flat_rows, states = trial_slab.shape
    weights = potential.reshape(-1, LANES)
    rows_total = flat_rows * lax.axis_size("group") * lax.axis_size("blk")
    group, index = lax.axis_index("group"), lax.axis_index("blk")
    cycle_size = lax.axis_size("blk")
    levels = cycle_size.bit_length() - 1
    origins = [index]
    for level in range(levels):
        flip = jnp.left_shift(1, step_bits(group, level))
        origins += [jnp.bitwise_xor(origin, flip) for origin in origins]
    odd = group % 2
    origins += [cycle_size + 1 - odd, cycle_size + odd]
    index_array = jnp.concatenate(
        [block_columns.reshape(-1)] + [origin.reshape(1).astype(jnp.int32) for origin in origins]
    )
    last = cycle_size - 1
    ending = [last]
    middle = [cycle_size, 1] + list(range(2, last)) + [cycle_size + 1]
    flat = jax.ShapeDtypeStruct((flat_rows, states), jnp.float32)
    rounded = jax.ShapeDtypeStruct((shard_blocks, block_size, states), jnp.bfloat16)
    packed = jax.ShapeDtypeStruct((states // 2 + SUB, states), jnp.float32)
    square = jax.ShapeDtypeStruct((states, states), jnp.float32)

    def own_part(index_array, value, *terms):
        return call(own_kernel, flat, [smem] + [vmem] * (2 + len(terms)))(
            index_array, hamiltonian, value, *terms
        )

    def coupled(value, index_array, early, *terms):
        arrived = cycle_exchange(value, 0)
        pairs = [pair_exchange(value, 0), pair_exchange(value, 1)]
        if early:
            partial = own_part(index_array, value, *terms)
            later, pairs[0], partial = lax.optimization_barrier((value, pairs[0], partial))
        else:
            later, pairs[0], index_array = lax.optimization_barrier((value, pairs[0], index_array))
        others = [cycle_exchange(later, level) for level in range(1, levels)]
        pieces = [value, arrived]
        for level, other in zip(range(1, levels), others):
            pieces += [other] + [cycle_exchange(piece, level) for piece in pieces[1:]]
        pieces += pairs
        if not early:
            partial = own_part(index_array, value, *terms)
        partial = call(
            functools.partial(middle_kernel, middle), flat, [smem] + [vmem] * (2 + len(middle)),
        )(index_array, hamiltonian, partial, *[pieces[number] for number in middle])
        return [partial] + [pieces[number] for number in ending]

    weighted = (weights.reshape(-1, 1) * trial_slab)
    parts = coupled(trial_slab.reshape(rounded.shape).astype(jnp.bfloat16), index_array, False, weighted)
    once, once_round = call(
        functools.partial(first_kernel, ending), (flat, rounded), [smem] + [vmem] * (2 + len(ending))
    )(index_array, hamiltonian, *parts)
    parts = coupled(once_round, index_array, True, weights, once, trial_slab)
    filtered, gram = call(
        functools.partial(second_kernel, ending), (flat, packed), [smem] + [vmem] * (2 + len(ending))
    )(index_array, hamiltonian, *parts)
    gram = summed(gram)
    return call(
        functools.partial(factor_kernel, rows_total),
        (flat, square),
        [vmem, vmem],
        [
            pltpu.VMEM((states, states), jnp.float32),
            pltpu.VMEM((states, states), jnp.float32),
            pltpu.VMEM((flat_rows, states), jnp.float32),
            pltpu.SemaphoreType.DMA((4,)),
            pltpu.SemaphoreType.DMA,
        ],
        hbm,
    )(gram, filtered)


def solution(mesh):
    placed = (
        P(("group", "blk"), None, None, None),
        P(("group", "blk"), None, None),
        P(("group", "blk")),
        P(("group", "blk"), None),
    )
    return jax.shard_map(
        on_device,
        mesh=mesh,
        in_specs=placed,
        out_specs=(P(("group", "blk"), None), P()),
        check_vma=False,
    )
```

```python
import functools

import jax
import jax.numpy as jnp
from jax import lax
from jax.experimental import pallas as pl
from jax.experimental.pallas import tpu as pltpu
from jax.sharding import PartitionSpec as P

precise = lax.Precision.HIGHEST
LANES = 128
SUB = 8
OUTER = 4
VMEM_LIMIT = 40 * 1024 * 1024
vmem = pl.BlockSpec(memory_space=pltpu.VMEM)
hbm = pl.BlockSpec(memory_space=pl.ANY)
smem = pl.BlockSpec(memory_space=pltpu.SMEM)


def pair_exchange(value, offset):
    count = lax.axis_size("group")
    route = []
    for low in range(offset, count - 1, 2):
        route += [(low, low + 1), (low + 1, low)]
    return lax.ppermute(value, "group", route)


def step_bits(group, level):
    levels = lax.axis_size("blk").bit_length() - 1
    return jnp.where(group % 2 == 1, levels - 1 - level, level)


def cycle_exchange(value, level):
    groups, cycle_size = lax.axis_size("group"), lax.axis_size("blk")
    levels = cycle_size.bit_length() - 1
    route = []
    for group in range(groups):
        bit = levels - 1 - level if group % 2 else level
        route += [
            (group * cycle_size + index, group * cycle_size + (index ^ 1 << bit))
            for index in range(cycle_size)
        ]
    return lax.ppermute(value, ("group", "blk"), route)


def from_partner(value, axis, flip):
    count = lax.axis_size(axis)
    return lax.ppermute(value, axis, [(index, index ^ flip) for index in range(count)])


def summed(value):
    for axis, step in (("group", 1), ("group", 2), ("blk", 1)):
        count = 2 if (axis, step) == ("group", 1) else lax.axis_size(axis)
        while step < count:
            flips = [step, 3 * step, 2 * step] if 2 * step < count else [step]
            if axis == "blk":
                flips[1:] = flips[:0:-1]
            others = [from_partner(value, axis, flip) for flip in flips]
            value = others[0] + value
            if len(others) == 3:
                value = (others[2] + others[1]) + value
            step *= len(flips) + 1
    return value


def potential_columns(potential_ref):
    return jnp.transpose(potential_ref[...])


def couple_row(index_ref, hamiltonian_ref, pieces, row):
    shard_blocks, sources, block_size, width = hamiltonian_ref.shape
    per_source = width // block_size
    total = None
    for number, piece_ref in pieces:
        source = index_ref[shard_blocks * sources * per_source + number]
        first = (row * sources + source) * per_source
        picked = jnp.concatenate(
            [piece_ref[index_ref[first + slot]] for slot in range(per_source)], axis=0
        )
        product = jnp.dot(
            hamiltonian_ref[row, source], picked, preferred_element_type=jnp.float32
        )
        total = product if total is None else total + product
    return total


def own_kernel(index_ref, hamiltonian_ref, own_ref, *refs):
    terms, partial_ref = refs[:-1], refs[-1]
    shard_blocks, _, block_size, _ = hamiltonian_ref.shape
    per_column = LANES // block_size
    if len(terms) == 3:
        weights = potential_columns(terms[0])
    for row in range(shard_blocks):
        rows = pl.ds(row * block_size, block_size)
        if len(terms) == 3:
            column, part = divmod(row, per_column)
            weight = weights[part * block_size : (part + 1) * block_size, column : column + 1]
            total = weight * terms[1][rows, :] - terms[2][rows, :]
        else:
            total = terms[0][rows, :]
        partial_ref[rows, :] = total + couple_row(
            index_ref, hamiltonian_ref, [(0, own_ref)], row
        )


def middle_kernel(numbers, index_ref, hamiltonian_ref, partial_ref, *refs):
    pieces, sum_ref = list(zip(numbers, refs[:-1])), refs[-1]
    shard_blocks, _, block_size, _ = hamiltonian_ref.shape
    for row in range(shard_blocks):
        rows = pl.ds(row * block_size, block_size)
        sum_ref[rows, :] = partial_ref[rows, :] + couple_row(
            index_ref, hamiltonian_ref, pieces, row
        )


def first_kernel(numbers, index_ref, hamiltonian_ref, partial_ref, *refs):
    pieces, (once_ref, round_ref) = list(zip(numbers, refs)), refs[len(numbers) :]
    shard_blocks, _, block_size, _ = hamiltonian_ref.shape
    for row in range(shard_blocks):
        rows = pl.ds(row * block_size, block_size)
        once = 0.5 * (
            partial_ref[rows, :] + couple_row(index_ref, hamiltonian_ref, pieces, row)
        )
        once_ref[rows, :] = once
        round_ref[row] = once.astype(jnp.bfloat16)


def second_kernel(numbers, index_ref, hamiltonian_ref, partial_ref, *refs):
    pieces, (both_ref, packed_ref) = list(zip(numbers, refs)), refs[len(numbers) :]
    states = both_ref.shape[1] // 2
    shard_blocks, _, block_size, _ = hamiltonian_ref.shape
    for row in range(shard_blocks):
        rows = pl.ds(row * block_size, block_size)
        filtered = partial_ref[rows, :] + couple_row(index_ref, hamiltonian_ref, pieces, row)
        both_ref[rows, :states], both_ref[rows, states:] = two_parts(filtered)
    both = both_ref[...]
    products = lax.dot_general(
        both, both, (((0,), (0,)), ((), ())), preferred_element_type=jnp.float32
    )
    high, low = products[:states, :], products[states:, :]
    gram = high[:, :states] + (high[:, states:] + low[:, :states] + low[:, states:])
    pack(gram, packed_ref)


def two_parts(value):
    high = value.astype(jnp.bfloat16)
    return high, (value - high.astype(jnp.float32)).astype(jnp.bfloat16)


def pack(gram, packed_ref):
    size = gram.shape[0]
    half = size // 2
    row = lax.broadcasted_iota(jnp.int32, (half, size), 0)
    lane = lax.broadcasted_iota(jnp.int32, (half, size), 1)
    lower = gram[half:, :]
    packed_ref[pl.ds(0, half), :] = jnp.where(lane < row, pltpu.roll(lower, half, 1), gram[:half, :])
    diagonal = jnp.sum(jnp.where(lane == row + half, lower, 0.0), axis=0, keepdims=True)
    packed_ref[pl.ds(half, SUB), :] = jnp.broadcast_to(diagonal, (SUB, size))


def unpack(packed_ref):
    size = packed_ref.shape[1]
    half = size // 2
    row = lax.broadcasted_iota(jnp.int32, (size, size), 0)
    lane = lax.broadcasted_iota(jnp.int32, (size, size), 1)
    upper = packed_ref[pl.ds(0, half), :]
    both = jnp.concatenate([upper, pltpu.roll(upper, half, 1)], axis=0)
    held = ((row < half) & (lane > row)) | ((row >= half) & (lane >= half) & (lane < row))
    off_diagonal = jnp.where(held, both, 0.0)
    diagonal = jnp.where(row < half, both, packed_ref[pl.ds(half, 1), :])
    return off_diagonal + jnp.transpose(off_diagonal) + jnp.where(row == lane, diagonal, 0.0)


def inverse_of(value):
    estimate = pl.reciprocal(value, approx=True)
    estimate = estimate * (2.0 - value * estimate)
    return estimate * (2.0 - value * estimate)


def factor(gram, upper_ref, inverse_ref):
    size = gram.shape[1]
    panels = size // SUB
    shape = (SUB, size)
    row_index = lax.broadcasted_iota(jnp.int32, shape, 0)
    lane_index = lax.broadcasted_iota(jnp.int32, shape, 1)

    def along_lanes(panel, first):
        return [jnp.broadcast_to(panel[:, first + c : first + c + 1], shape) for c in range(SUB)]

    def along_rows(panel, row):
        return jnp.broadcast_to(panel[row : row + 1, :], shape)

    def between(low, high):
        return (lane_index >= low) & (lane_index < high)

    held = [gram[k * SUB : (k + 1) * SUB, :] for k in range(panels)]
    for outer in range(0, panels, OUTER):
        end = outer + OUTER
        rows_then, rows_reduced = [], []
        block = along_lanes(held[outer], outer * SUB)
        for k in range(outer, end):
            first = k * SUB
            below = {p: along_lanes(held[p], first) for p in range(k + 1, end)}
            after = list(below[k + 1]) if k + 1 < end else None
            following = along_lanes(held[k + 1], first + SUB) if k + 1 < end else None
            right = held[k]
            left = jnp.where(
                lane_index < first, held[k], jnp.where(lane_index == row_index + first, 1.0, 0.0)
            )
            pivots = jnp.ones(shape, jnp.float32)
            reciprocals = jnp.ones(shape, jnp.float32)
            for j in range(0, SUB, 2):
                a, b = along_rows(block[j], j), along_rows(block[j], j + 1)
                c = along_rows(block[j + 1], j + 1)
                determinant = a * c - b * b
                over = inverse_of(determinant)
                over_a = inverse_of(a)
                pivots = jnp.where(row_index == j, a, pivots)
                pivots = jnp.where(row_index == j + 1, determinant * over_a, pivots)
                reciprocals = jnp.where(row_index == j, over_a, reciprocals)
                reciprocals = jnp.where(row_index == j + 1, a * over, reciprocals)
                x, y = block[j], block[j + 1]
                one = jnp.where(row_index == j + 1, b * over_a, 0.0)
                one = jnp.where(row_index > j + 1, (x * c - y * b) * over, one)
                two = jnp.where(row_index > j + 1, (y * a - x * b) * over, 0.0)
                upper = {
                    n: (along_rows(block[n], j), along_rows(block[n], j + 1))
                    for n in range(j + 2, SUB)
                }
                for n in upper:
                    block[n] = block[n] - one * upper[n][0] - two * upper[n][1]
                if following is not None:
                    x, y = after[j], after[j + 1]
                    next_one, next_two = (x * c - y * b) * over, (y * a - x * b) * over
                    for n in range(SUB):
                        following[n] = (
                            following[n] - next_one * along_rows(x, n) - next_two * along_rows(y, n)
                        )
                    for n in upper:
                        after[n] = after[n] - next_one * upper[n][0] - next_two * upper[n][1]
                right = right - one * along_rows(right, j) - two * along_rows(right, j + 1)
                left = left - one * along_rows(left, j) - two * along_rows(left, j + 1)
            scale = lax.rsqrt(pivots)
            upper_ref[pl.ds(first, SUB), :] = jnp.where(
                lane_index >= row_index + first, right * scale, 0.0
            )
            inverse_ref[pl.ds(first, SUB), :] = left * scale
            if k + 1 < panels:
                reduced = jnp.where(lane_index >= first + SUB, right, left) * reciprocals
                for n in range(SUB - 1, 0, -1):
                    column = jnp.where(row_index < n, block[n] * reciprocals, 0.0)
                    reduced = reduced - column * along_rows(reduced, n)
                rows_then.append(held[k])
                rows_reduced.append(jnp.where(between(first + SUB, end * SUB), 0.0, reduced))
                rows = [along_rows(reduced, n) for n in range(SUB)]
                for p in below:
                    total = jnp.where(between(first, first + SUB), 0.0, held[p])
                    for n in range(SUB):
                        total = total - below[p][n] * rows[n]
                    held[p] = total
            block = following
        if end < panels:
            change = lax.dot_general(
                jnp.concatenate(rows_then, axis=0), jnp.concatenate(rows_reduced, axis=0),
                (((0,), (0,)), ((), ())), precision=precise, preferred_element_type=jnp.float32,
            )
            for p in range(end, panels):
                kept = jnp.where(between(outer * SUB, end * SUB), 0.0, held[p])
                held[p] = kept - change[p * SUB : (p + 1) * SUB, :]


def factor_kernel(
    rows_total, packed_ref, both_ref, ortho_hbm, upper_hbm,
    upper_ref, inverse_ref, ortho_ref, sent, upper_sent,
):
    states = upper_ref.shape[0]
    factor(unpack(packed_ref) * (1.0 / rows_total), upper_ref, inverse_ref)
    copies = [pltpu.make_async_copy(upper_ref, upper_hbm, upper_sent)]
    copies[0].start()
    high, low = two_parts(inverse_ref[...])
    right = jnp.concatenate(
        [
            jnp.concatenate([high, high], axis=1),
            jnp.concatenate([low, jnp.zeros_like(low)], axis=1),
        ],
        axis=0,
    )
    chunks = sent.shape[0]
    per_chunk = both_ref.shape[0] // chunks
    for chunk in range(chunks):
        rows = pl.ds(chunk * per_chunk, per_chunk)
        product = lax.dot_general(
            both_ref[rows, :], right, (((1,), (1,)), ((), ())),
            preferred_element_type=jnp.float32,
        )
        ortho_ref[rows, :] = product[:, :states] + product[:, states:]
        copies.append(
            pltpu.make_async_copy(ortho_ref.at[rows, :], ortho_hbm.at[rows, :], sent.at[chunk])
        )
        copies[-1].start()
    for copy in copies:
        copy.wait()


def call(kernel, out_shape, in_specs, scratch=(), out_spec=vmem):
    return pl.pallas_call(
        kernel,
        out_shape=out_shape,
        in_specs=in_specs,
        out_specs=jax.tree.map(lambda _: out_spec, out_shape),
        scratch_shapes=list(scratch),
        compiler_params=pltpu.CompilerParams(vmem_limit_bytes=VMEM_LIMIT),
    )


def on_device(hamiltonian, block_columns, potential, trial_slab):
    shard_blocks, _, block_size, _ = hamiltonian.shape
    flat_rows, states = trial_slab.shape
    weights = potential.reshape(-1, LANES)
    rows_total = flat_rows * lax.axis_size("group") * lax.axis_size("blk")
    group, index = lax.axis_index("group"), lax.axis_index("blk")
    cycle_size = lax.axis_size("blk")
    levels = cycle_size.bit_length() - 1
    origins = [index]
    for level in range(levels):
        flip = jnp.left_shift(1, step_bits(group, level))
        origins += [jnp.bitwise_xor(origin, flip) for origin in origins]
    odd = group % 2
    origins += [cycle_size + 1 - odd, cycle_size + odd]
    index_array = jnp.concatenate(
        [block_columns.reshape(-1)] + [origin.reshape(1).astype(jnp.int32) for origin in origins]
    )
    last = cycle_size - 1
    ending = [last]
    middle = [cycle_size, 1] + list(range(2, last)) + [cycle_size + 1]
    flat = jax.ShapeDtypeStruct((flat_rows, states), jnp.float32)
    rounded = jax.ShapeDtypeStruct((shard_blocks, block_size, states), jnp.bfloat16)
    packed = jax.ShapeDtypeStruct((states // 2 + SUB, states), jnp.float32)
    square = jax.ShapeDtypeStruct((states, states), jnp.float32)

    def own_part(index_array, value, *terms):
        return call(own_kernel, flat, [smem] + [vmem] * (2 + len(terms)))(
            index_array, hamiltonian, value, *terms
        )

    def coupled(value, index_array, early, *terms):
        arrived = cycle_exchange(value, 0)
        pairs = [pair_exchange(value, 0), pair_exchange(value, 1)]
        if early:
            partial = own_part(index_array, value, *terms)
            later, pairs[0], partial = lax.optimization_barrier((value, pairs[0], partial))
        else:
            later, pairs[0], index_array, slab = lax.optimization_barrier(
                (value, pairs[0], index_array, trial_slab)
            )
            terms = (weights.reshape(-1, 1) * slab,)
        others = [cycle_exchange(later, level) for level in range(1, levels)]
        pieces = [value, arrived]
        for level, other in zip(range(1, levels), others):
            pieces += [other] + [cycle_exchange(piece, level) for piece in pieces[1:]]
        pieces += pairs
        if not early:
            partial = own_part(index_array, value, *terms)
        partial = call(
            functools.partial(middle_kernel, middle), flat, [smem] + [vmem] * (2 + len(middle)),
        )(index_array, hamiltonian, partial, *[pieces[number] for number in middle])
        return [partial] + [pieces[number] for number in ending]

    parts = coupled(trial_slab.reshape(rounded.shape).astype(jnp.bfloat16), index_array, False)
    once, once_round = call(
        functools.partial(first_kernel, ending), (flat, rounded), [smem] + [vmem] * (2 + len(ending))
    )(index_array, hamiltonian, *parts)
    parts = coupled(once_round, index_array, True, weights, once, trial_slab)
    both = jax.ShapeDtypeStruct((flat_rows, 2 * states), jnp.bfloat16)
    filtered, gram = call(
        functools.partial(second_kernel, ending), (both, packed), [smem] + [vmem] * (2 + len(ending))
    )(index_array, hamiltonian, *parts)
    gram = summed(gram)
    return call(
        functools.partial(factor_kernel, rows_total),
        (flat, square),
        [vmem, vmem],
        [
            pltpu.VMEM((states, states), jnp.float32),
            pltpu.VMEM((states, states), jnp.float32),
            pltpu.VMEM((flat_rows, states), jnp.float32),
            pltpu.SemaphoreType.DMA((4,)),
            pltpu.SemaphoreType.DMA,
        ],
        hbm,
    )(gram, filtered)


def solution(mesh):
    placed = (
        P(("group", "blk"), None, None, None),
        P(("group", "blk"), None, None),
        P(("group", "blk")),
        P(("group", "blk"), None),
    )
    return jax.shard_map(
        on_device,
        mesh=mesh,
        in_specs=placed,
        out_specs=(P(("group", "blk"), None), P()),
        check_vma=False,
    )
```

```python
import functools

import jax
import jax.numpy as jnp
from jax import lax
from jax.experimental import pallas as pl
from jax.experimental.pallas import tpu as pltpu
from jax.sharding import PartitionSpec as P

precise = lax.Precision.HIGHEST
LANES = 128
SUB = 8
OUTER = 4
VMEM_LIMIT = 40 * 1024 * 1024
vmem = pl.BlockSpec(memory_space=pltpu.VMEM)
hbm = pl.BlockSpec(memory_space=pl.ANY)
smem = pl.BlockSpec(memory_space=pltpu.SMEM)


def pair_exchange(value, offset):
    count = lax.axis_size("group")
    route = []
    for low in range(offset, count - 1, 2):
        route += [(low, low + 1), (low + 1, low)]
    return lax.ppermute(value, "group", route)


def step_bits(group, level):
    levels = lax.axis_size("blk").bit_length() - 1
    return jnp.where(group % 2 == 1, levels - 1 - level, level)


def cycle_exchange(value, level):
    groups, cycle_size = lax.axis_size("group"), lax.axis_size("blk")
    levels = cycle_size.bit_length() - 1
    route = []
    for group in range(groups):
        bit = levels - 1 - level if group % 2 else level
        route += [
            (group * cycle_size + index, group * cycle_size + (index ^ 1 << bit))
            for index in range(cycle_size)
        ]
    return lax.ppermute(value, ("group", "blk"), route)


def from_partner(value, axis, flip):
    count = lax.axis_size(axis)
    return lax.ppermute(value, axis, [(index, index ^ flip) for index in range(count)])


def summed(value):
    for axis, step in (("group", 1), ("group", 2), ("blk", 1)):
        count = 2 if (axis, step) == ("group", 1) else lax.axis_size(axis)
        while step < count:
            flips = [step, 3 * step, 2 * step] if 2 * step < count else [step]
            if axis == "blk":
                flips[1:] = flips[:0:-1]
            others = [from_partner(value, axis, flip) for flip in flips]
            value = others[0] + value
            if len(others) == 3:
                value = (others[2] + others[1]) + value
            step *= len(flips) + 1
    return value


def potential_columns(potential_ref):
    return jnp.transpose(potential_ref[...])


def couple_row(index_ref, hamiltonian_ref, pieces, row):
    shard_blocks, sources, block_size, width = hamiltonian_ref.shape
    per_source = width // block_size
    total = None
    for number, piece_ref in pieces:
        source = index_ref[shard_blocks * sources * per_source + number]
        first = (row * sources + source) * per_source
        picked = jnp.concatenate(
            [piece_ref[index_ref[first + slot]] for slot in range(per_source)], axis=0
        )
        product = jnp.dot(
            hamiltonian_ref[row, source], picked, preferred_element_type=jnp.float32
        )
        total = product if total is None else total + product
    return total


def own_kernel(index_ref, hamiltonian_ref, own_ref, *refs):
    terms, partial_ref = refs[:-1], refs[-1]
    shard_blocks, _, block_size, _ = hamiltonian_ref.shape
    per_column = LANES // block_size
    if len(terms) == 3:
        weights = potential_columns(terms[0])
    for row in range(shard_blocks):
        rows = pl.ds(row * block_size, block_size)
        if len(terms) == 3:
            column, part = divmod(row, per_column)
            weight = weights[part * block_size : (part + 1) * block_size, column : column + 1]
            total = weight * terms[1][rows, :] - terms[2][rows, :]
        else:
            total = terms[0][rows, :]
        partial_ref[rows, :] = total + couple_row(
            index_ref, hamiltonian_ref, [(0, own_ref)], row
        )


def middle_kernel(numbers, index_ref, hamiltonian_ref, partial_ref, *refs):
    pieces, sum_ref = list(zip(numbers, refs[:-1])), refs[-1]
    shard_blocks, _, block_size, _ = hamiltonian_ref.shape
    for row in range(shard_blocks):
        rows = pl.ds(row * block_size, block_size)
        sum_ref[rows, :] = partial_ref[rows, :] + couple_row(
            index_ref, hamiltonian_ref, pieces, row
        )


def first_kernel(numbers, index_ref, hamiltonian_ref, partial_ref, *refs):
    pieces, (once_ref, round_ref) = list(zip(numbers, refs)), refs[len(numbers) :]
    shard_blocks, _, block_size, _ = hamiltonian_ref.shape
    for row in range(shard_blocks):
        rows = pl.ds(row * block_size, block_size)
        once = 0.5 * (
            partial_ref[rows, :] + couple_row(index_ref, hamiltonian_ref, pieces, row)
        )
        once_ref[rows, :] = once
        round_ref[row] = once.astype(jnp.bfloat16)


def second_kernel(numbers, index_ref, hamiltonian_ref, partial_ref, *refs):
    pieces, (both_ref, packed_ref) = list(zip(numbers, refs)), refs[len(numbers) :]
    states = both_ref.shape[1] // 2
    shard_blocks, _, block_size, _ = hamiltonian_ref.shape
    for row in range(shard_blocks):
        rows = pl.ds(row * block_size, block_size)
        filtered = partial_ref[rows, :] + couple_row(index_ref, hamiltonian_ref, pieces, row)
        both_ref[rows, :states], both_ref[rows, states:] = two_parts(filtered)
    both = both_ref[...]
    products = lax.dot_general(
        both, both, (((0,), (0,)), ((), ())), preferred_element_type=jnp.float32
    )
    high, low = products[:states, :], products[states:, :]
    gram = high[:, :states] + (high[:, states:] + low[:, :states] + low[:, states:])
    pack(gram, packed_ref)


def two_parts(value):
    high = value.astype(jnp.bfloat16)
    return high, (value - high.astype(jnp.float32)).astype(jnp.bfloat16)


def pack(gram, packed_ref):
    size = gram.shape[0]
    half = size // 2
    row = lax.broadcasted_iota(jnp.int32, (half, size), 0)
    lane = lax.broadcasted_iota(jnp.int32, (half, size), 1)
    lower = gram[half:, :]
    packed_ref[pl.ds(0, half), :] = jnp.where(lane < row, pltpu.roll(lower, half, 1), gram[:half, :])
    diagonal = jnp.sum(jnp.where(lane == row + half, lower, 0.0), axis=0, keepdims=True)
    packed_ref[pl.ds(half, SUB), :] = jnp.broadcast_to(diagonal, (SUB, size))


def unpack(packed_ref):
    size = packed_ref.shape[1]
    half = size // 2
    row = lax.broadcasted_iota(jnp.int32, (size, size), 0)
    lane = lax.broadcasted_iota(jnp.int32, (size, size), 1)
    upper = packed_ref[pl.ds(0, half), :]
    both = jnp.concatenate([upper, pltpu.roll(upper, half, 1)], axis=0)
    held = ((row < half) & (lane > row)) | ((row >= half) & (lane >= half) & (lane < row))
    off_diagonal = jnp.where(held, both, 0.0)
    diagonal = jnp.where(row < half, both, packed_ref[pl.ds(half, 1), :])
    return off_diagonal + jnp.transpose(off_diagonal) + jnp.where(row == lane, diagonal, 0.0)


def factor(gram, upper_ref, inverse_ref):
    size = gram.shape[1]
    panels = size // SUB
    shape = (SUB, size)
    row_index = lax.broadcasted_iota(jnp.int32, shape, 0)
    lane_index = lax.broadcasted_iota(jnp.int32, shape, 1)

    def along_lanes(panel, first):
        return [jnp.broadcast_to(panel[:, first + c : first + c + 1], shape) for c in range(SUB)]

    def along_rows(panel, row):
        return jnp.broadcast_to(panel[row : row + 1, :], shape)

    def between(low, high):
        return (lane_index >= low) & (lane_index < high)

    held = [gram[k * SUB : (k + 1) * SUB, :] for k in range(panels)]
    for outer in range(0, panels, OUTER):
        end = outer + OUTER
        rows_then, rows_reduced = [], []
        block = along_lanes(held[outer], outer * SUB)
        for k in range(outer, end):
            first = k * SUB
            below = {p: along_lanes(held[p], first) for p in range(k + 1, end)}
            after = list(below[k + 1]) if k + 1 < end else None
            following = along_lanes(held[k + 1], first + SUB) if k + 1 < end else None
            right = held[k]
            left = jnp.where(
                lane_index < first, held[k], jnp.where(lane_index == row_index + first, 1.0, 0.0)
            )
            pivots = jnp.ones(shape, jnp.float32)
            reciprocals = jnp.ones(shape, jnp.float32)
            columns = [jnp.zeros(shape, jnp.float32)] * SUB
            for j in range(0, SUB, 2):
                a, b = along_rows(block[j], j), along_rows(block[j], j + 1)
                c = along_rows(block[j + 1], j + 1)
                determinant = a * c - b * b
                over = pltpu.reciprocal(determinant, approx=True)
                over_a = pltpu.reciprocal(a, approx=True)
                over_c, shift = a * over, b * over_a
                pivots = jnp.where(row_index == j, a, pivots)
                pivots = jnp.where(row_index == j + 1, determinant * over_a, pivots)
                reciprocals = jnp.where(row_index == j, over_a, reciprocals)
                reciprocals = jnp.where(row_index == j + 1, over_c, reciprocals)
                one, two = block[j] * c - block[j + 1] * b, block[j + 1] * a - block[j] * b
                upper = {
                    n: (along_rows(block[n], j), along_rows(block[n], j + 1))
                    for n in range(j + 2, SUB)
                }
                for n in upper:
                    block[n] = block[n] - over * (one * upper[n][0] + two * upper[n][1])
                if following is not None:
                    x, y = after[j], after[j + 1]
                    next_one, next_two = x * c - y * b, y * a - x * b
                    for n in range(SUB):
                        following[n] = following[n] - over * (
                            next_one * along_rows(x, n) + next_two * along_rows(y, n)
                        )
                    for n in upper:
                        after[n] = after[n] - over * (
                            next_one * upper[n][0] + next_two * upper[n][1]
                        )
                one = jnp.where(row_index > j + 1, one * over, jnp.where(row_index == j + 1, shift, 0.0))
                two = jnp.where(row_index > j + 1, two * over, 0.0)
                right = right - one * along_rows(right, j) - two * along_rows(right, j + 1)
                left = left - one * along_rows(left, j) - two * along_rows(left, j + 1)
                columns[j + 1] = jnp.where(row_index == j, shift, columns[j + 1])
                for n in upper:
                    unit = (upper[n][1] - shift * upper[n][0]) * over_c
                    columns[n] = jnp.where(row_index == j, upper[n][0] * over_a, columns[n])
                    columns[n] = jnp.where(row_index == j + 1, unit, columns[n])
            scale = lax.rsqrt(pivots)
            upper_ref[pl.ds(first, SUB), :] = jnp.where(
                lane_index >= row_index + first, right * scale, 0.0
            )
            inverse_ref[pl.ds(first, SUB), :] = left * scale
            if k + 1 < panels:
                reduced = jnp.where(lane_index >= first + SUB, right, left) * reciprocals
                for n in range(SUB - 1, 0, -1):
                    reduced = reduced - columns[n] * along_rows(reduced, n)
                rows_then.append(held[k])
                rows_reduced.append(jnp.where(between(first + SUB, end * SUB), 0.0, reduced))
                rows = [along_rows(reduced, n) for n in range(SUB)]
                for p in below:
                    total = jnp.where(between(first, first + SUB), 0.0, held[p])
                    for n in range(SUB):
                        total = total - below[p][n] * rows[n]
                    held[p] = total
            block = following
        if end < panels:
            change = lax.dot_general(
                jnp.concatenate(rows_then, axis=0), jnp.concatenate(rows_reduced, axis=0),
                (((0,), (0,)), ((), ())), precision=precise, preferred_element_type=jnp.float32,
            )
            for p in range(end, panels):
                kept = jnp.where(between(outer * SUB, end * SUB), 0.0, held[p])
                held[p] = kept - change[p * SUB : (p + 1) * SUB, :]


def factor_kernel(
    rows_total, packed_ref, both_ref, ortho_hbm, upper_hbm,
    upper_ref, inverse_ref, ortho_ref, sent, upper_sent,
):
    states = upper_ref.shape[0]
    factor(unpack(packed_ref) * (1.0 / rows_total), upper_ref, inverse_ref)
    copies = [pltpu.make_async_copy(upper_ref, upper_hbm, upper_sent)]
    copies[0].start()
    high, low = two_parts(inverse_ref[...])
    right = jnp.concatenate(
        [
            jnp.concatenate([high, high], axis=1),
            jnp.concatenate([low, jnp.zeros_like(low)], axis=1),
        ],
        axis=0,
    )
    chunks = sent.shape[0]
    per_chunk = both_ref.shape[0] // chunks
    for chunk in range(chunks):
        rows = pl.ds(chunk * per_chunk, per_chunk)
        product = lax.dot_general(
            both_ref[rows, :], right, (((1,), (1,)), ((), ())),
            preferred_element_type=jnp.float32,
        )
        ortho_ref[rows, :] = product[:, :states] + product[:, states:]
        copies.append(
            pltpu.make_async_copy(ortho_ref.at[rows, :], ortho_hbm.at[rows, :], sent.at[chunk])
        )
        copies[-1].start()
    for copy in copies:
        copy.wait()


def call(kernel, out_shape, in_specs, scratch=(), out_spec=vmem):
    return pl.pallas_call(
        kernel,
        out_shape=out_shape,
        in_specs=in_specs,
        out_specs=jax.tree.map(lambda _: out_spec, out_shape),
        scratch_shapes=list(scratch),
        compiler_params=pltpu.CompilerParams(vmem_limit_bytes=VMEM_LIMIT),
    )


def on_device(hamiltonian, block_columns, potential, trial_slab):
    shard_blocks, _, block_size, _ = hamiltonian.shape
    flat_rows, states = trial_slab.shape
    weights = potential.reshape(-1, LANES)
    rows_total = flat_rows * lax.axis_size("group") * lax.axis_size("blk")
    group, index = lax.axis_index("group"), lax.axis_index("blk")
    cycle_size = lax.axis_size("blk")
    levels = cycle_size.bit_length() - 1
    origins = [index]
    for level in range(levels):
        flip = jnp.left_shift(1, step_bits(group, level))
        origins += [jnp.bitwise_xor(origin, flip) for origin in origins]
    odd = group % 2
    origins += [cycle_size + 1 - odd, cycle_size + odd]
    index_array = jnp.concatenate(
        [block_columns.reshape(-1)] + [origin.reshape(1).astype(jnp.int32) for origin in origins]
    )
    last = cycle_size - 1
    ending = [last]
    middle = [cycle_size, 1] + list(range(2, last)) + [cycle_size + 1]
    flat = jax.ShapeDtypeStruct((flat_rows, states), jnp.float32)
    rounded = jax.ShapeDtypeStruct((shard_blocks, block_size, states), jnp.bfloat16)
    packed = jax.ShapeDtypeStruct((states // 2 + SUB, states), jnp.float32)
    square = jax.ShapeDtypeStruct((states, states), jnp.float32)

    def own_part(index_array, value, *terms):
        return call(own_kernel, flat, [smem] + [vmem] * (2 + len(terms)))(
            index_array, hamiltonian, value, *terms
        )

    def coupled(value, index_array, early, *terms):
        arrived = cycle_exchange(value, 0)
        pairs = [pair_exchange(value, 0), pair_exchange(value, 1)]
        if early:
            partial = own_part(index_array, value, *terms)
            later, pairs[0], partial = lax.optimization_barrier((value, pairs[0], partial))
        else:
            later, pairs[0], index_array = lax.optimization_barrier((value, pairs[0], index_array))
        others = [cycle_exchange(later, level) for level in range(1, levels)]
        pieces = [value, arrived]
        for level, other in zip(range(1, levels), others):
            pieces += [other] + [cycle_exchange(piece, level) for piece in pieces[1:]]
        pieces += pairs
        if not early:
            partial = own_part(index_array, value, *terms)
        partial = call(
            functools.partial(middle_kernel, middle), flat, [smem] + [vmem] * (2 + len(middle)),
        )(index_array, hamiltonian, partial, *[pieces[number] for number in middle])
        return [partial] + [pieces[number] for number in ending]

    weighted = weights.reshape(-1, 1) * trial_slab
    parts = coupled(trial_slab.reshape(rounded.shape).astype(jnp.bfloat16), index_array, False, weighted)
    once, once_round = call(
        functools.partial(first_kernel, ending), (flat, rounded), [smem] + [vmem] * (2 + len(ending))
    )(index_array, hamiltonian, *parts)
    parts = coupled(once_round, index_array, True, weights, once, trial_slab)
    both = jax.ShapeDtypeStruct((flat_rows, 2 * states), jnp.bfloat16)
    filtered, gram = call(
        functools.partial(second_kernel, ending), (both, packed), [smem] + [vmem] * (2 + len(ending))
    )(index_array, hamiltonian, *parts)
    gram = summed(gram)
    return call(
        functools.partial(factor_kernel, rows_total),
        (flat, square),
        [vmem, vmem],
        [
            pltpu.VMEM((states, states), jnp.float32),
            pltpu.VMEM((states, states), jnp.float32),
            pltpu.VMEM((flat_rows, states), jnp.float32),
            pltpu.SemaphoreType.DMA((4,)),
            pltpu.SemaphoreType.DMA,
        ],
        hbm,
    )(gram, filtered)


def solution(mesh):
    placed = (
        P(("group", "blk"), None, None, None),
        P(("group", "blk"), None, None),
        P(("group", "blk")),
        P(("group", "blk"), None),
    )
    return jax.shard_map(
        on_device,
        mesh=mesh,
        in_specs=placed,
        out_specs=(P(("group", "blk"), None), P()),
        check_vma=False,
    )
```

```python
import functools

import jax
import jax.numpy as jnp
from jax import lax
from jax.experimental import pallas as pl
from jax.experimental.pallas import tpu as pltpu
from jax.sharding import PartitionSpec as P

precise = lax.Precision.HIGHEST
LANES = 128
SUB = 8
OUTER = 4
VMEM_LIMIT = 40 * 1024 * 1024
vmem = pl.BlockSpec(memory_space=pltpu.VMEM)
hbm = pl.BlockSpec(memory_space=pl.ANY)
smem = pl.BlockSpec(memory_space=pltpu.SMEM)


def pair_exchange(value, offset):
    count = lax.axis_size("group")
    route = []
    for low in range(offset, count - 1, 2):
        route += [(low, low + 1), (low + 1, low)]
    return lax.ppermute(value, "group", route)


def step_bits(group, level):
    levels = lax.axis_size("blk").bit_length() - 1
    return jnp.where(group % 2 == 1, levels - 1 - level, level)


def cycle_exchange(value, level):
    groups, cycle_size = lax.axis_size("group"), lax.axis_size("blk")
    levels = cycle_size.bit_length() - 1
    route = []
    for group in range(groups):
        bit = levels - 1 - level if group % 2 else level
        route += [
            (group * cycle_size + index, group * cycle_size + (index ^ 1 << bit))
            for index in range(cycle_size)
        ]
    return lax.ppermute(value, ("group", "blk"), route)


def from_partner(value, axis, flip):
    count = lax.axis_size(axis)
    return lax.ppermute(value, axis, [(index, index ^ flip) for index in range(count)])


def summed(value):
    for axis, step in (("group", 1), ("group", 2), ("blk", 1)):
        count = 2 if (axis, step) == ("group", 1) else lax.axis_size(axis)
        while step < count:
            flips = [step, 3 * step, 2 * step] if 2 * step < count else [step]
            if axis == "blk":
                flips[1:] = flips[:0:-1]
            others = [from_partner(value, axis, flip) for flip in flips]
            value = others[0] + value
            if len(others) == 3:
                value = (others[2] + others[1]) + value
            step *= len(flips) + 1
    return value


def potential_columns(potential_ref):
    return jnp.transpose(potential_ref[...])


def couple_row(index_ref, hamiltonian_ref, pieces, row):
    shard_blocks, sources, block_size, width = hamiltonian_ref.shape
    per_source = width // block_size
    total = None
    for number, piece_ref in pieces:
        source = index_ref[shard_blocks * sources * per_source + number]
        first = (row * sources + source) * per_source
        picked = jnp.concatenate(
            [piece_ref[index_ref[first + slot]] for slot in range(per_source)], axis=0
        )
        product = jnp.dot(
            hamiltonian_ref[row, source], picked, preferred_element_type=jnp.float32
        )
        total = product if total is None else total + product
    return total


def own_kernel(index_ref, hamiltonian_ref, own_ref, *refs):
    terms, partial_ref = refs[:-1], refs[-1]
    shard_blocks, _, block_size, _ = hamiltonian_ref.shape
    per_column = LANES // block_size
    if len(terms) == 3:
        weights = potential_columns(terms[0])
    for row in range(shard_blocks):
        rows = pl.ds(row * block_size, block_size)
        if len(terms) == 3:
            column, part = divmod(row, per_column)
            weight = weights[part * block_size : (part + 1) * block_size, column : column + 1]
            total = weight * terms[1][rows, :] - terms[2][rows, :]
        else:
            total = terms[0][rows, :]
        partial_ref[rows, :] = total + couple_row(
            index_ref, hamiltonian_ref, [(0, own_ref)], row
        )


def middle_kernel(numbers, index_ref, hamiltonian_ref, partial_ref, *refs):
    pieces, sum_ref = list(zip(numbers, refs[:-1])), refs[-1]
    shard_blocks, _, block_size, _ = hamiltonian_ref.shape
    for row in range(shard_blocks):
        rows = pl.ds(row * block_size, block_size)
        sum_ref[rows, :] = partial_ref[rows, :] + couple_row(
            index_ref, hamiltonian_ref, pieces, row
        )


def first_kernel(numbers, index_ref, hamiltonian_ref, partial_ref, *refs):
    pieces, (once_ref, round_ref) = list(zip(numbers, refs)), refs[len(numbers) :]
    shard_blocks, _, block_size, _ = hamiltonian_ref.shape
    for row in range(shard_blocks):
        rows = pl.ds(row * block_size, block_size)
        once = 0.5 * (
            partial_ref[rows, :] + couple_row(index_ref, hamiltonian_ref, pieces, row)
        )
        once_ref[rows, :] = once
        round_ref[row] = once.astype(jnp.bfloat16)


def second_kernel(numbers, index_ref, hamiltonian_ref, partial_ref, *refs):
    pieces, (both_ref, packed_ref) = list(zip(numbers, refs)), refs[len(numbers) :]
    states = both_ref.shape[1] // 2
    shard_blocks, _, block_size, _ = hamiltonian_ref.shape
    for row in range(shard_blocks):
        rows = pl.ds(row * block_size, block_size)
        filtered = partial_ref[rows, :] + couple_row(index_ref, hamiltonian_ref, pieces, row)
        both_ref[rows, :states], both_ref[rows, states:] = two_parts(filtered)
    both = both_ref[...]
    products = lax.dot_general(
        both, both, (((0,), (0,)), ((), ())), preferred_element_type=jnp.float32
    )
    high, low = products[:states, :], products[states:, :]
    gram = high[:, :states] + (high[:, states:] + low[:, :states] + low[:, states:])
    pack(gram, packed_ref)


def two_parts(value):
    high = value.astype(jnp.bfloat16)
    return high, (value - high.astype(jnp.float32)).astype(jnp.bfloat16)


def pack(gram, packed_ref):
    size = gram.shape[0]
    half = size // 2
    row = lax.broadcasted_iota(jnp.int32, (half, size), 0)
    lane = lax.broadcasted_iota(jnp.int32, (half, size), 1)
    lower = gram[half:, :]
    packed_ref[pl.ds(0, half), :] = jnp.where(lane < row, pltpu.roll(lower, half, 1), gram[:half, :])
    diagonal = jnp.sum(jnp.where(lane == row + half, lower, 0.0), axis=0, keepdims=True)
    packed_ref[pl.ds(half, SUB), :] = jnp.broadcast_to(diagonal, (SUB, size))


def unpack(packed_ref):
    size = packed_ref.shape[1]
    half = size // 2
    row = lax.broadcasted_iota(jnp.int32, (size, size), 0)
    lane = lax.broadcasted_iota(jnp.int32, (size, size), 1)
    upper = packed_ref[pl.ds(0, half), :]
    both = jnp.concatenate([upper, pltpu.roll(upper, half, 1)], axis=0)
    held = ((row < half) & (lane > row)) | ((row >= half) & (lane >= half) & (lane < row))
    off_diagonal = jnp.where(held, both, 0.0)
    diagonal = jnp.where(row < half, both, packed_ref[pl.ds(half, 1), :])
    return off_diagonal + jnp.transpose(off_diagonal) + jnp.where(row == lane, diagonal, 0.0)


def factor(work_ref, upper_ref, inverse_ref):
    size = work_ref.shape[0]
    panels = size // SUB
    shape = (SUB, size)
    row_index = lax.broadcasted_iota(jnp.int32, shape, 0)
    lane_index = lax.broadcasted_iota(jnp.int32, shape, 1)
    width = OUTER * SUB

    def along_lanes(panel, first):
        return [jnp.broadcast_to(panel[:, first + c : first + c + 1], shape) for c in range(SUB)]

    def along_rows(panel, row):
        return jnp.broadcast_to(panel[row : row + 1, :], shape)

    def between(low, high):
        return (lane_index >= low) & (lane_index < high)

    def outer_block(outer, carry):
        limit = size - outer * width
        held = [work_ref[pl.ds(k * SUB, SUB), :] for k in range(panels)]
        rows_then, rows_reduced = [], []
        block = along_lanes(held[0], 0)
        for k in range(OUTER):
            first = k * SUB
            below = {p: along_lanes(held[p], first) for p in range(k + 1, OUTER)}
            after = list(below[k + 1]) if k + 1 < OUTER else None
            following = along_lanes(held[k + 1], first + SUB) if k + 1 < OUTER else None
            right = held[k]
            left = jnp.where(
                (lane_index < first) | (lane_index >= limit), held[k],
                jnp.where(lane_index == row_index + first, 1.0, 0.0),
            )
            pivots = jnp.ones(shape, jnp.float32)
            reciprocals = jnp.ones(shape, jnp.float32)
            columns = [jnp.zeros(shape, jnp.float32)] * SUB
            for j in range(0, SUB, 2):
                a, b = along_rows(block[j], j), along_rows(block[j], j + 1)
                c = along_rows(block[j + 1], j + 1)
                determinant = a * c - b * b
                over = pltpu.reciprocal(determinant, approx=True)
                over_a = pltpu.reciprocal(a, approx=True)
                over_c, shift = a * over, b * over_a
                pivots = jnp.where(row_index == j, a, pivots)
                pivots = jnp.where(row_index == j + 1, determinant * over_a, pivots)
                reciprocals = jnp.where(row_index == j, over_a, reciprocals)
                reciprocals = jnp.where(row_index == j + 1, over_c, reciprocals)
                one, two = block[j] * c - block[j + 1] * b, block[j + 1] * a - block[j] * b
                upper = {
                    n: (along_rows(block[n], j), along_rows(block[n], j + 1))
                    for n in range(j + 2, SUB)
                }
                for n in upper:
                    block[n] = block[n] - over * (one * upper[n][0] + two * upper[n][1])
                if following is not None:
                    x, y = after[j], after[j + 1]
                    next_one, next_two = x * c - y * b, y * a - x * b
                    for n in range(SUB):
                        following[n] = following[n] - over * (
                            next_one * along_rows(x, n) + next_two * along_rows(y, n)
                        )
                    for n in upper:
                        after[n] = after[n] - over * (
                            next_one * upper[n][0] + next_two * upper[n][1]
                        )
                one = jnp.where(row_index > j + 1, one * over, jnp.where(row_index == j + 1, shift, 0.0))
                two = jnp.where(row_index > j + 1, two * over, 0.0)
                right = right - one * along_rows(right, j) - two * along_rows(right, j + 1)
                left = left - one * along_rows(left, j) - two * along_rows(left, j + 1)
                columns[j + 1] = jnp.where(row_index == j, shift, columns[j + 1])
                for n in upper:
                    unit = (upper[n][1] - shift * upper[n][0]) * over_c
                    columns[n] = jnp.where(row_index == j, upper[n][0] * over_a, columns[n])
                    columns[n] = jnp.where(row_index == j + 1, unit, columns[n])
            scale = lax.rsqrt(pivots)
            rows_out = pl.ds(pl.multiple_of(outer * width + first, SUB), SUB)
            kept = (lane_index >= row_index + first) & (lane_index < limit)
            upper_ref[rows_out, :] = pltpu.roll(
                jnp.where(kept, right * scale, 0.0), outer * width, 1
            )
            inverse_ref[rows_out, :] = pltpu.roll(left * scale, outer * width, 1)
            reduced = jnp.where(between(first + SUB, limit), right, left) * reciprocals
            for n in range(SUB - 1, 0, -1):
                reduced = reduced - columns[n] * along_rows(reduced, n)
            rows_then.append(held[k])
            rows_reduced.append(jnp.where(between(first + SUB, width), 0.0, reduced))
            rows = [along_rows(reduced, n) for n in range(SUB)]
            for p in below:
                total = jnp.where(between(first, first + SUB), 0.0, held[p])
                for n in range(SUB):
                    total = total - below[p][n] * rows[n]
                held[p] = total
            block = following
        change = lax.dot_general(
            jnp.concatenate(rows_then, axis=0), jnp.concatenate(rows_reduced, axis=0),
            (((0,), (0,)), ((), ())), precision=precise, preferred_element_type=jnp.float32,
        )
        for p in range(OUTER, panels):
            total = jnp.where(between(0, width), 0.0, held[p]) - change[p * SUB : (p + 1) * SUB, :]
            work_ref[pl.ds((p - OUTER) * SUB, SUB), :] = pltpu.roll(total, size - width, 1)
        return carry

    lax.fori_loop(0, panels // OUTER, outer_block, 0)


def factor_kernel(
    rows_total, packed_ref, both_ref, ortho_hbm, upper_hbm,
    work_ref, upper_ref, inverse_ref, ortho_ref, sent, upper_sent,
):
    states = upper_ref.shape[0]
    work_ref[...] = unpack(packed_ref) * (1.0 / rows_total)
    factor(work_ref, upper_ref, inverse_ref)
    upper_copy = pltpu.make_async_copy(upper_ref, upper_hbm, upper_sent)
    upper_copy.start()
    high, low = two_parts(inverse_ref[...])
    right = jnp.concatenate(
        [
            jnp.concatenate([high, high], axis=1),
            jnp.concatenate([low, jnp.zeros_like(low)], axis=1),
        ],
        axis=0,
    )
    chunks = sent.shape[0]
    per_chunk = both_ref.shape[0] // chunks
    copies = []
    for chunk in range(chunks):
        rows = pl.ds(chunk * per_chunk, per_chunk)
        product = lax.dot_general(
            both_ref[rows, :], right, (((1,), (1,)), ((), ())),
            preferred_element_type=jnp.float32,
        )
        ortho_ref[rows, :] = product[:, :states] + product[:, states:]
        copies.append(
            pltpu.make_async_copy(ortho_ref.at[rows, :], ortho_hbm.at[rows, :], sent.at[chunk])
        )
        copies[-1].start()
    upper_copy.wait()
    for copy in copies:
        copy.wait()


def call(kernel, out_shape, in_specs, scratch=(), out_spec=vmem):
    return pl.pallas_call(
        kernel,
        out_shape=out_shape,
        in_specs=in_specs,
        out_specs=jax.tree.map(lambda _: out_spec, out_shape),
        scratch_shapes=list(scratch),
        compiler_params=pltpu.CompilerParams(vmem_limit_bytes=VMEM_LIMIT),
    )


def on_device(hamiltonian, block_columns, potential, trial_slab):
    shard_blocks, _, block_size, _ = hamiltonian.shape
    flat_rows, states = trial_slab.shape
    weights = potential.reshape(-1, LANES)
    rows_total = flat_rows * lax.axis_size("group") * lax.axis_size("blk")
    group, index = lax.axis_index("group"), lax.axis_index("blk")
    cycle_size = lax.axis_size("blk")
    levels = cycle_size.bit_length() - 1
    origins = [index]
    for level in range(levels):
        flip = jnp.left_shift(1, step_bits(group, level))
        origins += [jnp.bitwise_xor(origin, flip) for origin in origins]
    odd = group % 2
    origins += [cycle_size + 1 - odd, cycle_size + odd]
    index_array = jnp.concatenate(
        [block_columns.reshape(-1)] + [origin.reshape(1).astype(jnp.int32) for origin in origins]
    )
    last = cycle_size - 1
    ending = [last]
    middle = [cycle_size, 1] + list(range(2, last)) + [cycle_size + 1]
    flat = jax.ShapeDtypeStruct((flat_rows, states), jnp.float32)
    rounded = jax.ShapeDtypeStruct((shard_blocks, block_size, states), jnp.bfloat16)
    packed = jax.ShapeDtypeStruct((states // 2 + SUB, states), jnp.float32)
    square = jax.ShapeDtypeStruct((states, states), jnp.float32)

    def own_part(index_array, value, *terms):
        return call(own_kernel, flat, [smem] + [vmem] * (2 + len(terms)))(
            index_array, hamiltonian, value, *terms
        )

    def coupled(value, index_array, early, *terms):
        arrived = cycle_exchange(value, 0)
        pairs = [pair_exchange(value, 0), pair_exchange(value, 1)]
        if early:
            partial = own_part(index_array, value, *terms)
            later, pairs[0], partial = lax.optimization_barrier((value, pairs[0], partial))
        else:
            later, pairs[0], index_array = lax.optimization_barrier((value, pairs[0], index_array))
        others = [cycle_exchange(later, level) for level in range(1, levels)]
        pieces = [value, arrived]
        for level, other in zip(range(1, levels), others):
            pieces += [other] + [cycle_exchange(piece, level) for piece in pieces[1:]]
        pieces += pairs
        if not early:
            partial = own_part(index_array, value, *terms)
        partial = call(
            functools.partial(middle_kernel, middle), flat, [smem] + [vmem] * (2 + len(middle)),
        )(index_array, hamiltonian, partial, *[pieces[number] for number in middle])
        return [partial] + [pieces[number] for number in ending]

    weighted = weights.reshape(-1, 1) * trial_slab
    parts = coupled(trial_slab.reshape(rounded.shape).astype(jnp.bfloat16), index_array, False, weighted)
    once, once_round = call(
        functools.partial(first_kernel, ending), (flat, rounded), [smem] + [vmem] * (2 + len(ending))
    )(index_array, hamiltonian, *parts)
    parts = coupled(once_round, index_array, True, weights, once, trial_slab)
    both = jax.ShapeDtypeStruct((flat_rows, 2 * states), jnp.bfloat16)
    filtered, gram = call(
        functools.partial(second_kernel, ending), (both, packed), [smem] + [vmem] * (2 + len(ending))
    )(index_array, hamiltonian, *parts)
    gram = summed(gram)
    return call(
        functools.partial(factor_kernel, rows_total),
        (flat, square),
        [vmem, vmem],
        [
            pltpu.VMEM((states, states), jnp.float32),
            pltpu.VMEM((states, states), jnp.float32),
            pltpu.VMEM((states, states), jnp.float32),
            pltpu.VMEM((flat_rows, states), jnp.float32),
            pltpu.SemaphoreType.DMA((4,)),
            pltpu.SemaphoreType.DMA,
        ],
        hbm,
    )(gram, filtered)


def solution(mesh):
    placed = (
        P(("group", "blk"), None, None, None),
        P(("group", "blk"), None, None),
        P(("group", "blk")),
        P(("group", "blk"), None),
    )
    return jax.shard_map(
        on_device,
        mesh=mesh,
        in_specs=placed,
        out_specs=(P(("group", "blk"), None), P()),
        check_vma=False,
    )
```

```python
import functools

import jax
import jax.numpy as jnp
from jax import lax
from jax.experimental import pallas as pl
from jax.experimental.pallas import tpu as pltpu
from jax.sharding import PartitionSpec as P

precise = lax.Precision.HIGHEST
LANES = 128
SUB = 8
OUTER = 4
VMEM_LIMIT = 40 * 1024 * 1024
vmem = pl.BlockSpec(memory_space=pltpu.VMEM)
hbm = pl.BlockSpec(memory_space=pl.ANY)
smem = pl.BlockSpec(memory_space=pltpu.SMEM)


def pair_exchange(value, offset):
    count = lax.axis_size("group")
    route = []
    for low in range(offset, count - 1, 2):
        route += [(low, low + 1), (low + 1, low)]
    return lax.ppermute(value, "group", route)


def step_bits(group, level):
    levels = lax.axis_size("blk").bit_length() - 1
    return jnp.where(group % 2 == 1, levels - 1 - level, level)


def cycle_exchange(value, level):
    groups, cycle_size = lax.axis_size("group"), lax.axis_size("blk")
    levels = cycle_size.bit_length() - 1
    route = []
    for group in range(groups):
        bit = levels - 1 - level if group % 2 else level
        route += [
            (group * cycle_size + index, group * cycle_size + (index ^ 1 << bit))
            for index in range(cycle_size)
        ]
    return lax.ppermute(value, ("group", "blk"), route)


def from_partner(value, axis, flip):
    count = lax.axis_size(axis)
    return lax.ppermute(value, axis, [(index, index ^ flip) for index in range(count)])


def summed(value):
    for axis, step in (("group", 1), ("group", 2), ("blk", 1)):
        count = 2 if (axis, step) == ("group", 1) else lax.axis_size(axis)
        while step < count:
            flips = [step, 3 * step, 2 * step] if 2 * step < count else [step]
            if axis == "blk":
                flips[1:] = flips[:0:-1]
            others = [from_partner(value, axis, flip) for flip in flips]
            value = others[0] + value
            if len(others) == 3:
                value = (others[2] + others[1]) + value
            step *= len(flips) + 1
    return value


def potential_columns(potential_ref):
    return jnp.transpose(potential_ref[...])


def couple_row(index_ref, hamiltonian_ref, pieces, row):
    shard_blocks, sources, block_size, width = hamiltonian_ref.shape
    per_source = width // block_size
    total = None
    for number, piece_ref in pieces:
        source = index_ref[shard_blocks * sources * per_source + number]
        first = (row * sources + source) * per_source
        picked = jnp.concatenate(
            [piece_ref[index_ref[first + slot]] for slot in range(per_source)], axis=0
        )
        product = jnp.dot(
            hamiltonian_ref[row, source], picked, preferred_element_type=jnp.float32
        )
        total = product if total is None else total + product
    return total


def own_kernel(index_ref, hamiltonian_ref, own_ref, *refs):
    terms, partial_ref = refs[:-1], refs[-1]
    shard_blocks, _, block_size, _ = hamiltonian_ref.shape
    per_column = LANES // block_size
    if len(terms) == 3:
        weights = potential_columns(terms[0])
    for row in range(shard_blocks):
        rows = pl.ds(row * block_size, block_size)
        if len(terms) == 3:
            column, part = divmod(row, per_column)
            weight = weights[part * block_size : (part + 1) * block_size, column : column + 1]
            total = weight * terms[1][rows, :] - terms[2][rows, :]
        else:
            total = terms[0][rows, :]
        partial_ref[rows, :] = total + couple_row(
            index_ref, hamiltonian_ref, [(0, own_ref)], row
        )


def middle_kernel(numbers, index_ref, hamiltonian_ref, partial_ref, *refs):
    pieces, sum_ref = list(zip(numbers, refs[:-1])), refs[-1]
    shard_blocks, _, block_size, _ = hamiltonian_ref.shape
    for row in range(shard_blocks):
        rows = pl.ds(row * block_size, block_size)
        sum_ref[rows, :] = partial_ref[rows, :] + couple_row(
            index_ref, hamiltonian_ref, pieces, row
        )


def first_kernel(numbers, index_ref, hamiltonian_ref, partial_ref, *refs):
    pieces, (once_ref, round_ref) = list(zip(numbers, refs)), refs[len(numbers) :]
    shard_blocks, _, block_size, _ = hamiltonian_ref.shape
    for row in range(shard_blocks):
        rows = pl.ds(row * block_size, block_size)
        once = 0.5 * (
            partial_ref[rows, :] + couple_row(index_ref, hamiltonian_ref, pieces, row)
        )
        once_ref[rows, :] = once
        round_ref[row] = once.astype(jnp.bfloat16)


def second_kernel(numbers, index_ref, hamiltonian_ref, partial_ref, *refs):
    pieces, (both_ref, packed_ref) = list(zip(numbers, refs)), refs[len(numbers) :]
    states = both_ref.shape[1] // 2
    shard_blocks, _, block_size, _ = hamiltonian_ref.shape
    for row in range(shard_blocks):
        rows = pl.ds(row * block_size, block_size)
        filtered = partial_ref[rows, :] + couple_row(index_ref, hamiltonian_ref, pieces, row)
        both_ref[rows, :states], both_ref[rows, states:] = two_parts(filtered)
    both = both_ref[...]
    products = lax.dot_general(
        both, both, (((0,), (0,)), ((), ())), preferred_element_type=jnp.float32
    )
    high, low = products[:states, :], products[states:, :]
    gram = high[:, :states] + (high[:, states:] + low[:, :states] + low[:, states:])
    pack(gram, packed_ref)


def two_parts(value):
    high = value.astype(jnp.bfloat16)
    return high, (value - high.astype(jnp.float32)).astype(jnp.bfloat16)


def pack(gram, packed_ref):
    size = gram.shape[0]
    half = size // 2
    row = lax.broadcasted_iota(jnp.int32, (half, size), 0)
    lane = lax.broadcasted_iota(jnp.int32, (half, size), 1)
    lower = gram[half:, :]
    packed_ref[pl.ds(0, half), :] = jnp.where(lane < row, pltpu.roll(lower, half, 1), gram[:half, :])
    diagonal = jnp.sum(jnp.where(lane == row + half, lower, 0.0), axis=0, keepdims=True)
    packed_ref[pl.ds(half, SUB), :] = jnp.broadcast_to(diagonal, (SUB, size))


def unpack(packed_ref):
    size = packed_ref.shape[1]
    half = size // 2
    row = lax.broadcasted_iota(jnp.int32, (size, size), 0)
    lane = lax.broadcasted_iota(jnp.int32, (size, size), 1)
    upper = packed_ref[pl.ds(0, half), :]
    both = jnp.concatenate([upper, pltpu.roll(upper, half, 1)], axis=0)
    held = ((row < half) & (lane > row)) | ((row >= half) & (lane >= half) & (lane < row))
    off_diagonal = jnp.where(held, both, 0.0)
    diagonal = jnp.where(row < half, both, packed_ref[pl.ds(half, 1), :])
    return off_diagonal + jnp.transpose(off_diagonal) + jnp.where(row == lane, diagonal, 0.0)


def factor(gram, upper_ref, inverse_ref):
    size = gram.shape[1]
    panels = size // SUB
    shape = (SUB, size)
    row_index = lax.broadcasted_iota(jnp.int32, shape, 0)
    lane_index = lax.broadcasted_iota(jnp.int32, shape, 1)

    def along_lanes(panel, first):
        return [jnp.broadcast_to(panel[:, first + c : first + c + 1], shape) for c in range(SUB)]

    def along_rows(panel, row):
        return jnp.broadcast_to(panel[row : row + 1, :], shape)

    def between(low, high):
        return (lane_index >= low) & (lane_index < high)

    def stacked(rows):
        panel = rows[0]
        for n in range(1, SUB):
            panel = jnp.where(row_index == n, rows[n], panel)
        return panel

    held = [gram[k * SUB : (k + 1) * SUB, :] for k in range(panels)]
    for outer in range(0, panels, OUTER):
        end = outer + OUTER
        rows_then, rows_reduced = [], []
        block = along_lanes(held[outer], outer * SUB)
        for k in range(outer, end):
            first = k * SUB
            below = {p: along_lanes(held[p], first) for p in range(k + 1, end)}
            after = list(below[k + 1]) if k + 1 < end else None
            following = along_lanes(held[k + 1], first + SUB) if k + 1 < end else None
            left = jnp.where(
                lane_index < first, held[k], jnp.where(lane_index == row_index + first, 1.0, 0.0)
            )
            rights = [along_rows(held[k], n) for n in range(SUB)]
            lefts = [along_rows(left, n) for n in range(SUB)]
            entry = {(n, m): along_rows(block[m], n) for m in range(SUB) for n in range(m + 1)}
            unit, pivots, reciprocals = {}, [], []
            for j in range(0, SUB, 2):
                a, b, c = entry[j, j], entry[j, j + 1], entry[j + 1, j + 1]
                rest = range(j + 2, SUB)
                determinant = a * c - b * b
                over = pltpu.reciprocal(determinant, approx=True)
                over_a = pltpu.reciprocal(a, approx=True)
                over_c, shift = a * over, b * over_a
                pivots += [a, determinant * over_a]
                reciprocals += [over_a, over_c]
                one = {n: entry[j, n] * c - entry[j + 1, n] * b for n in rest}
                two = {n: entry[j + 1, n] * a - entry[j, n] * b for n in rest}
                for n in rest:
                    for m in range(n, SUB):
                        entry[n, m] = entry[n, m] - over * (
                            one[n] * entry[j, m] + two[n] * entry[j + 1, m]
                        )
                if following is not None:
                    x, y = after[j], after[j + 1]
                    next_one, next_two = x * c - y * b, y * a - x * b
                    for n in range(SUB):
                        following[n] = following[n] - over * (
                            next_one * along_rows(x, n) + next_two * along_rows(y, n)
                        )
                    for n in rest:
                        after[n] = after[n] - over * (
                            next_one * entry[j, n] + next_two * entry[j + 1, n]
                        )
                for rows in (rights, lefts):
                    for n in rest:
                        rows[n] = rows[n] - over * (one[n] * rows[j] + two[n] * rows[j + 1])
                    rows[j + 1] = rows[j + 1] - shift * rows[j]
                unit[j, j + 1] = shift
                for n in rest:
                    unit[j, n] = entry[j, n] * over_a
                    unit[j + 1, n] = (entry[j + 1, n] - shift * entry[j, n]) * over_c
            scales = [lax.rsqrt(pivot) for pivot in pivots]
            upper = stacked([row * scale for row, scale in zip(rights, scales)])
            upper_ref[pl.ds(first, SUB), :] = jnp.where(lane_index >= row_index + first, upper, 0.0)
            inverse_ref[pl.ds(first, SUB), :] = stacked(
                [row * scale for row, scale in zip(lefts, scales)]
            )
            if k + 1 < panels:
                rows = [
                    jnp.where(lane_index >= first + SUB, rights[n], lefts[n]) * reciprocals[n]
                    for n in range(SUB)
                ]
                for m in range(SUB - 1, 0, -1):
                    for n in range(m):
                        rows[n] = rows[n] - unit[n, m] * rows[m]
                rows_then.append(held[k])
                rows_reduced.append(
                    jnp.where(between(first + SUB, end * SUB), 0.0, stacked(rows))
                )
                for p in below:
                    total = jnp.where(between(first, first + SUB), 0.0, held[p])
                    for n in range(SUB):
                        total = total - below[p][n] * rows[n]
                    held[p] = total
            block = following
        if end < panels:
            change = lax.dot_general(
                jnp.concatenate(rows_then, axis=0), jnp.concatenate(rows_reduced, axis=0),
                (((0,), (0,)), ((), ())), precision=precise, preferred_element_type=jnp.float32,
            )
            for p in range(end, panels):
                kept = jnp.where(between(outer * SUB, end * SUB), 0.0, held[p])
                held[p] = kept - change[p * SUB : (p + 1) * SUB, :]


def factor_kernel(
    rows_total, packed_ref, both_ref, ortho_hbm, upper_hbm,
    upper_ref, inverse_ref, ortho_ref, sent, upper_sent,
):
    states = upper_ref.shape[0]
    factor(unpack(packed_ref) * (1.0 / rows_total), upper_ref, inverse_ref)
    copies = [pltpu.make_async_copy(upper_ref, upper_hbm, upper_sent)]
    copies[0].start()
    high, low = two_parts(inverse_ref[...])
    right = jnp.concatenate(
        [
            jnp.concatenate([high, high], axis=1),
            jnp.concatenate([low, jnp.zeros_like(low)], axis=1),
        ],
        axis=0,
    )
    chunks = sent.shape[0]
    per_chunk = both_ref.shape[0] // chunks
    for chunk in range(chunks):
        rows = pl.ds(chunk * per_chunk, per_chunk)
        product = lax.dot_general(
            both_ref[rows, :], right, (((1,), (1,)), ((), ())),
            preferred_element_type=jnp.float32,
        )
        ortho_ref[rows, :] = product[:, :states] + product[:, states:]
        copies.append(
            pltpu.make_async_copy(ortho_ref.at[rows, :], ortho_hbm.at[rows, :], sent.at[chunk])
        )
        copies[-1].start()
    for copy in copies:
        copy.wait()


def call(kernel, out_shape, in_specs, scratch=(), out_spec=vmem):
    return pl.pallas_call(
        kernel,
        out_shape=out_shape,
        in_specs=in_specs,
        out_specs=jax.tree.map(lambda _: out_spec, out_shape),
        scratch_shapes=list(scratch),
        compiler_params=pltpu.CompilerParams(vmem_limit_bytes=VMEM_LIMIT),
    )


def on_device(hamiltonian, block_columns, potential, trial_slab):
    shard_blocks, _, block_size, _ = hamiltonian.shape
    flat_rows, states = trial_slab.shape
    weights = potential.reshape(-1, LANES)
    rows_total = flat_rows * lax.axis_size("group") * lax.axis_size("blk")
    group, index = lax.axis_index("group"), lax.axis_index("blk")
    cycle_size = lax.axis_size("blk")
    levels = cycle_size.bit_length() - 1
    origins = [index]
    for level in range(levels):
        flip = jnp.left_shift(1, step_bits(group, level))
        origins += [jnp.bitwise_xor(origin, flip) for origin in origins]
    odd = group % 2
    origins += [cycle_size + 1 - odd, cycle_size + odd]
    index_array = jnp.concatenate(
        [block_columns.reshape(-1)] + [origin.reshape(1).astype(jnp.int32) for origin in origins]
    )
    last = cycle_size - 1
    ending = [last]
    middle = [cycle_size, 1] + list(range(2, last)) + [cycle_size + 1]
    flat = jax.ShapeDtypeStruct((flat_rows, states), jnp.float32)
    rounded = jax.ShapeDtypeStruct((shard_blocks, block_size, states), jnp.bfloat16)
    packed = jax.ShapeDtypeStruct((states // 2 + SUB, states), jnp.float32)
    square = jax.ShapeDtypeStruct((states, states), jnp.float32)

    def own_part(index_array, value, *terms):
        return call(own_kernel, flat, [smem] + [vmem] * (2 + len(terms)))(
            index_array, hamiltonian, value, *terms
        )

    def coupled(value, index_array, early, *terms):
        arrived = cycle_exchange(value, 0)
        pairs = [pair_exchange(value, 0), pair_exchange(value, 1)]
        if early:
            partial = own_part(index_array, value, *terms)
            later, pairs[0], partial = lax.optimization_barrier((value, pairs[0], partial))
        else:
            later, pairs[0], index_array = lax.optimization_barrier((value, pairs[0], index_array))
        others = [cycle_exchange(later, level) for level in range(1, levels)]
        pieces = [value, arrived]
        for level, other in zip(range(1, levels), others):
            pieces += [other] + [cycle_exchange(piece, level) for piece in pieces[1:]]
        pieces += pairs
        if not early:
            partial = own_part(index_array, value, *terms)
        partial = call(
            functools.partial(middle_kernel, middle), flat, [smem] + [vmem] * (2 + len(middle)),
        )(index_array, hamiltonian, partial, *[pieces[number] for number in middle])
        return [partial] + [pieces[number] for number in ending]

    weighted = weights.reshape(-1, 1) * trial_slab
    parts = coupled(trial_slab.reshape(rounded.shape).astype(jnp.bfloat16), index_array, False, weighted)
    once, once_round = call(
        functools.partial(first_kernel, ending), (flat, rounded), [smem] + [vmem] * (2 + len(ending))
    )(index_array, hamiltonian, *parts)
    parts = coupled(once_round, index_array, True, weights, once, trial_slab)
    both = jax.ShapeDtypeStruct((flat_rows, 2 * states), jnp.bfloat16)
    filtered, gram = call(
        functools.partial(second_kernel, ending), (both, packed), [smem] + [vmem] * (2 + len(ending))
    )(index_array, hamiltonian, *parts)
    gram = summed(gram)
    return call(
        functools.partial(factor_kernel, rows_total),
        (flat, square),
        [vmem, vmem],
        [
            pltpu.VMEM((states, states), jnp.float32),
            pltpu.VMEM((states, states), jnp.float32),
            pltpu.VMEM((flat_rows, states), jnp.float32),
            pltpu.SemaphoreType.DMA((4,)),
            pltpu.SemaphoreType.DMA,
        ],
        hbm,
    )(gram, filtered)


def solution(mesh):
    placed = (
        P(("group", "blk"), None, None, None),
        P(("group", "blk"), None, None),
        P(("group", "blk")),
        P(("group", "blk"), None),
    )
    return jax.shard_map(
        on_device,
        mesh=mesh,
        in_specs=placed,
        out_specs=(P(("group", "blk"), None), P()),
        check_vma=False,
    )
```

```python
import functools

import jax
import jax.numpy as jnp
from jax import lax
from jax.experimental import pallas as pl
from jax.experimental.pallas import tpu as pltpu
from jax.sharding import PartitionSpec as P

precise = lax.Precision.HIGHEST
LANES = 128
SUB = 8
OUTER = 4
VMEM_LIMIT = 40 * 1024 * 1024
vmem = pl.BlockSpec(memory_space=pltpu.VMEM)
hbm = pl.BlockSpec(memory_space=pl.ANY)
smem = pl.BlockSpec(memory_space=pltpu.SMEM)


def pair_exchange(value, offset):
    count = lax.axis_size("group")
    route = []
    for low in range(offset, count - 1, 2):
        route += [(low, low + 1), (low + 1, low)]
    return lax.ppermute(value, "group", route)


def step_bits(group, level):
    levels = lax.axis_size("blk").bit_length() - 1
    return jnp.where(group % 2 == 1, levels - 1 - level, level)


def cycle_exchange(value, level):
    groups, cycle_size = lax.axis_size("group"), lax.axis_size("blk")
    levels = cycle_size.bit_length() - 1
    route = []
    for group in range(groups):
        bit = levels - 1 - level if group % 2 else level
        route += [
            (group * cycle_size + index, group * cycle_size + (index ^ 1 << bit))
            for index in range(cycle_size)
        ]
    return lax.ppermute(value, ("group", "blk"), route)


def from_partner(value, axis, flip):
    count = lax.axis_size(axis)
    return lax.ppermute(value, axis, [(index, index ^ flip) for index in range(count)])


def summed(value):
    for axis, step in (("group", 1), ("group", 2), ("blk", 1)):
        count = 2 if (axis, step) == ("group", 1) else lax.axis_size(axis)
        while step < count:
            flips = [step, 3 * step, 2 * step] if 2 * step < count else [step]
            if axis == "blk":
                flips[1:] = flips[:0:-1]
            others = [from_partner(value, axis, flip) for flip in flips]
            value = others[0] + value
            if len(others) == 3:
                value = (others[2] + others[1]) + value
            step *= len(flips) + 1
    return value


def potential_columns(potential_ref):
    return jnp.transpose(potential_ref[...])


def couple_row(index_ref, hamiltonian_ref, pieces, row):
    shard_blocks, sources, block_size, width = hamiltonian_ref.shape
    per_source = width // block_size
    total = None
    for number, piece_ref in pieces:
        source = index_ref[shard_blocks * sources * per_source + number]
        first = (row * sources + source) * per_source
        picked = jnp.concatenate(
            [piece_ref[index_ref[first + slot]] for slot in range(per_source)], axis=0
        )
        product = jnp.dot(
            hamiltonian_ref[row, source], picked, preferred_element_type=jnp.float32
        )
        total = product if total is None else total + product
    return total


def weight_of(weights, block_size, row):
    column, part = divmod(row, LANES // block_size)
    return weights[part * block_size : (part + 1) * block_size, column : column + 1]


def own_kernel(index_ref, hamiltonian_ref, own_ref, *refs):
    terms, partial_ref = refs[:-1], refs[-1]
    shard_blocks, _, block_size, _ = hamiltonian_ref.shape
    if terms:
        weights = potential_columns(terms[0])
    for row in range(shard_blocks):
        rows = pl.ds(row * block_size, block_size)
        total = couple_row(index_ref, hamiltonian_ref, [(0, own_ref)], row)
        if terms:
            weight = weight_of(weights, block_size, row)
            total = total + (weight * terms[1][rows, :] - terms[2][rows, :])
        partial_ref[rows, :] = total


def middle_kernel(numbers, index_ref, hamiltonian_ref, partial_ref, *refs):
    pieces, sum_ref = list(zip(numbers, refs[:-1])), refs[-1]
    shard_blocks, _, block_size, _ = hamiltonian_ref.shape
    for row in range(shard_blocks):
        rows = pl.ds(row * block_size, block_size)
        sum_ref[rows, :] = partial_ref[rows, :] + couple_row(
            index_ref, hamiltonian_ref, pieces, row
        )


def first_kernel(numbers, index_ref, hamiltonian_ref, potential_ref, trial_ref, partial_ref, *refs):
    pieces, (once_ref, round_ref) = list(zip(numbers, refs)), refs[len(numbers) :]
    shard_blocks, _, block_size, _ = hamiltonian_ref.shape
    weights = potential_columns(potential_ref)
    for row in range(shard_blocks):
        rows = pl.ds(row * block_size, block_size)
        partial = partial_ref[rows, :] + weight_of(weights, block_size, row) * trial_ref[rows, :]
        once = 0.5 * (partial + couple_row(index_ref, hamiltonian_ref, pieces, row))
        once_ref[rows, :] = once
        round_ref[row] = once.astype(jnp.bfloat16)


def second_kernel(numbers, index_ref, hamiltonian_ref, partial_ref, *refs):
    pieces, (both_ref, packed_ref) = list(zip(numbers, refs)), refs[len(numbers) :]
    states = both_ref.shape[1] // 2
    shard_blocks, _, block_size, _ = hamiltonian_ref.shape
    for row in range(shard_blocks):
        rows = pl.ds(row * block_size, block_size)
        filtered = partial_ref[rows, :] + couple_row(index_ref, hamiltonian_ref, pieces, row)
        both_ref[rows, :states], both_ref[rows, states:] = two_parts(filtered)
    both = both_ref[...]
    products = lax.dot_general(
        both, both, (((0,), (0,)), ((), ())), preferred_element_type=jnp.float32
    )
    high, low = products[:states, :], products[states:, :]
    gram = high[:, :states] + (high[:, states:] + low[:, :states] + low[:, states:])
    pack(gram, packed_ref)


def two_parts(value):
    high = value.astype(jnp.bfloat16)
    return high, (value - high.astype(jnp.float32)).astype(jnp.bfloat16)


def pack(gram, packed_ref):
    size = gram.shape[0]
    half = size // 2
    row = lax.broadcasted_iota(jnp.int32, (half, size), 0)
    lane = lax.broadcasted_iota(jnp.int32, (half, size), 1)
    lower = gram[half:, :]
    packed_ref[pl.ds(0, half), :] = jnp.where(lane < row, pltpu.roll(lower, half, 1), gram[:half, :])
    diagonal = jnp.sum(jnp.where(lane == row + half, lower, 0.0), axis=0, keepdims=True)
    packed_ref[pl.ds(half, SUB), :] = jnp.broadcast_to(diagonal, (SUB, size))


def unpack(packed_ref):
    size = packed_ref.shape[1]
    half = size // 2
    row = lax.broadcasted_iota(jnp.int32, (size, size), 0)
    lane = lax.broadcasted_iota(jnp.int32, (size, size), 1)
    upper = packed_ref[pl.ds(0, half), :]
    both = jnp.concatenate([upper, pltpu.roll(upper, half, 1)], axis=0)
    held = ((row < half) & (lane > row)) | ((row >= half) & (lane >= half) & (lane < row))
    off_diagonal = jnp.where(held, both, 0.0)
    diagonal = jnp.where(row < half, both, packed_ref[pl.ds(half, 1), :])
    return off_diagonal + jnp.transpose(off_diagonal) + jnp.where(row == lane, diagonal, 0.0)


def factor(gram, upper_ref, inverse_ref):
    size = gram.shape[1]
    panels = size // SUB
    shape = (SUB, size)
    row_index = lax.broadcasted_iota(jnp.int32, shape, 0)
    lane_index = lax.broadcasted_iota(jnp.int32, shape, 1)

    def along_lanes(panel, first):
        return [jnp.broadcast_to(panel[:, first + c : first + c + 1], shape) for c in range(SUB)]

    def along_rows(panel, row):
        return jnp.broadcast_to(panel[row : row + 1, :], shape)

    def between(low, high):
        return (lane_index >= low) & (lane_index < high)

    held = [gram[k * SUB : (k + 1) * SUB, :] for k in range(panels)]
    for outer in range(0, panels, OUTER):
        end = outer + OUTER
        rows_then, rows_reduced = [], []
        block = along_lanes(held[outer], outer * SUB)
        for k in range(outer, end):
            first = k * SUB
            below = {p: along_lanes(held[p], first) for p in range(k + 1, end)}
            after = list(below[k + 1]) if k + 1 < end else None
            following = along_lanes(held[k + 1], first + SUB) if k + 1 < end else None
            right = held[k]
            left = jnp.where(
                lane_index < first, held[k], jnp.where(lane_index == row_index + first, 1.0, 0.0)
            )
            pivots = jnp.ones(shape, jnp.float32)
            reciprocals = jnp.ones(shape, jnp.float32)
            columns = [jnp.zeros(shape, jnp.float32)] * SUB
            for j in range(0, SUB, 2):
                a, b = along_rows(block[j], j), along_rows(block[j], j + 1)
                c = along_rows(block[j + 1], j + 1)
                determinant = a * c - b * b
                over = pltpu.reciprocal(determinant, approx=True)
                over_a = pltpu.reciprocal(a, approx=True)
                over_c, shift = a * over, b * over_a
                pivots = jnp.where(row_index == j, a, pivots)
                pivots = jnp.where(row_index == j + 1, determinant * over_a, pivots)
                reciprocals = jnp.where(row_index == j, over_a, reciprocals)
                reciprocals = jnp.where(row_index == j + 1, over_c, reciprocals)
                one, two = block[j] * c - block[j + 1] * b, block[j + 1] * a - block[j] * b
                upper = {
                    n: (along_rows(block[n], j), along_rows(block[n], j + 1))
                    for n in range(j + 2, SUB)
                }
                for n in upper:
                    block[n] = block[n] - over * (one * upper[n][0] + two * upper[n][1])
                if following is not None:
                    x, y = after[j], after[j + 1]
                    next_one, next_two = x * c - y * b, y * a - x * b
                    for n in range(SUB):
                        following[n] = following[n] - over * (
                            next_one * along_rows(x, n) + next_two * along_rows(y, n)
                        )
                    for n in upper:
                        after[n] = after[n] - over * (
                            next_one * upper[n][0] + next_two * upper[n][1]
                        )
                one = jnp.where(row_index > j + 1, one * over, jnp.where(row_index == j + 1, shift, 0.0))
                two = jnp.where(row_index > j + 1, two * over, 0.0)
                right = right - one * along_rows(right, j) - two * along_rows(right, j + 1)
                left = left - one * along_rows(left, j) - two * along_rows(left, j + 1)
                columns[j + 1] = jnp.where(row_index == j, shift, columns[j + 1])
                for n in upper:
                    unit = (upper[n][1] - shift * upper[n][0]) * over_c
                    columns[n] = jnp.where(row_index == j, upper[n][0] * over_a, columns[n])
                    columns[n] = jnp.where(row_index == j + 1, unit, columns[n])
            scale = lax.rsqrt(pivots)
            upper_ref[pl.ds(first, SUB), :] = jnp.where(
                lane_index >= row_index + first, right * scale, 0.0
            )
            inverse_ref[pl.ds(first, SUB), :] = left * scale
            if k + 1 < panels:
                reduced = jnp.where(lane_index >= first + SUB, right, left) * reciprocals
                for n in range(SUB - 1, 0, -1):
                    reduced = reduced - columns[n] * along_rows(reduced, n)
                rows_then.append(held[k])
                rows_reduced.append(jnp.where(between(first + SUB, end * SUB), 0.0, reduced))
                rows = [along_rows(reduced, n) for n in range(SUB)]
                for p in below:
                    total = jnp.where(between(first, first + SUB), 0.0, held[p])
                    for n in range(SUB):
                        total = total - below[p][n] * rows[n]
                    held[p] = total
            block = following
        if end < panels:
            change = lax.dot_general(
                jnp.concatenate(rows_then, axis=0), jnp.concatenate(rows_reduced, axis=0),
                (((0,), (0,)), ((), ())), precision=precise, preferred_element_type=jnp.float32,
            )
            for p in range(end, panels):
                kept = jnp.where(between(outer * SUB, end * SUB), 0.0, held[p])
                held[p] = kept - change[p * SUB : (p + 1) * SUB, :]


def factor_kernel(
    rows_total, packed_ref, both_ref, ortho_hbm, upper_hbm,
    upper_ref, inverse_ref, ortho_ref, sent, upper_sent,
):
    states = upper_ref.shape[0]
    factor(unpack(packed_ref) * (1.0 / rows_total), upper_ref, inverse_ref)
    copies = [pltpu.make_async_copy(upper_ref, upper_hbm, upper_sent)]
    copies[0].start()
    high, low = two_parts(inverse_ref[...])
    right = jnp.concatenate(
        [
            jnp.concatenate([high, high], axis=1),
            jnp.concatenate([low, jnp.zeros_like(low)], axis=1),
        ],
        axis=0,
    )
    chunks = sent.shape[0]
    per_chunk = both_ref.shape[0] // chunks
    for chunk in range(chunks):
        rows = pl.ds(chunk * per_chunk, per_chunk)
        product = lax.dot_general(
            both_ref[rows, :], right, (((1,), (1,)), ((), ())),
            preferred_element_type=jnp.float32,
        )
        ortho_ref[rows, :] = product[:, :states] + product[:, states:]
        copies.append(
            pltpu.make_async_copy(ortho_ref.at[rows, :], ortho_hbm.at[rows, :], sent.at[chunk])
        )
        copies[-1].start()
    for copy in copies:
        copy.wait()


def call(kernel, out_shape, in_specs, scratch=(), out_spec=vmem):
    return pl.pallas_call(
        kernel,
        out_shape=out_shape,
        in_specs=in_specs,
        out_specs=jax.tree.map(lambda _: out_spec, out_shape),
        scratch_shapes=list(scratch),
        compiler_params=pltpu.CompilerParams(vmem_limit_bytes=VMEM_LIMIT),
    )


def on_device(hamiltonian, block_columns, potential, trial_slab):
    shard_blocks, _, block_size, _ = hamiltonian.shape
    flat_rows, states = trial_slab.shape
    weights = potential.reshape(-1, LANES)
    rows_total = flat_rows * lax.axis_size("group") * lax.axis_size("blk")
    group, index = lax.axis_index("group"), lax.axis_index("blk")
    cycle_size = lax.axis_size("blk")
    levels = cycle_size.bit_length() - 1
    origins = [index]
    for level in range(levels):
        flip = jnp.left_shift(1, step_bits(group, level))
        origins += [jnp.bitwise_xor(origin, flip) for origin in origins]
    odd = group % 2
    origins += [cycle_size + 1 - odd, cycle_size + odd]
    index_array = jnp.concatenate(
        [block_columns.reshape(-1)] + [origin.reshape(1).astype(jnp.int32) for origin in origins]
    )
    last = cycle_size - 1
    ending = [last]
    middle = [cycle_size, 1] + list(range(2, last)) + [cycle_size + 1]
    flat = jax.ShapeDtypeStruct((flat_rows, states), jnp.float32)
    rounded = jax.ShapeDtypeStruct((shard_blocks, block_size, states), jnp.bfloat16)
    packed = jax.ShapeDtypeStruct((states // 2 + SUB, states), jnp.float32)
    square = jax.ShapeDtypeStruct((states, states), jnp.float32)

    def own_part(index_array, value, *terms):
        return call(own_kernel, flat, [smem] + [vmem] * (2 + len(terms)))(
            index_array, hamiltonian, value, *terms
        )

    def coupled(value, index_array, early, *terms):
        arrived = cycle_exchange(value, 0)
        pairs = [pair_exchange(value, 0), pair_exchange(value, 1)]
        if early:
            partial = own_part(index_array, value, *terms)
            later, pairs[0], partial = lax.optimization_barrier((value, pairs[0], partial))
        else:
            later, pairs[0], index_array = lax.optimization_barrier((value, pairs[0], index_array))
        others = [cycle_exchange(later, level) for level in range(1, levels)]
        pieces = [value, arrived]
        for level, other in zip(range(1, levels), others):
            pieces += [other] + [cycle_exchange(piece, level) for piece in pieces[1:]]
        pieces += pairs
        if not early:
            partial = own_part(index_array, value, *terms)
        partial = call(
            functools.partial(middle_kernel, middle), flat, [smem] + [vmem] * (2 + len(middle)),
        )(index_array, hamiltonian, partial, *[pieces[number] for number in middle])
        return [partial] + [pieces[number] for number in ending]

    parts = coupled(trial_slab.reshape(rounded.shape).astype(jnp.bfloat16), index_array, False)
    once, once_round = call(
        functools.partial(first_kernel, ending), (flat, rounded), [smem] + [vmem] * (4 + len(ending))
    )(index_array, hamiltonian, weights, trial_slab, *parts)
    parts = coupled(once_round, index_array, True, weights, once, trial_slab)
    both = jax.ShapeDtypeStruct((flat_rows, 2 * states), jnp.bfloat16)
    filtered, gram = call(
        functools.partial(second_kernel, ending), (both, packed), [smem] + [vmem] * (2 + len(ending))
    )(index_array, hamiltonian, *parts)
    gram = summed(gram)
    return call(
        functools.partial(factor_kernel, rows_total),
        (flat, square),
        [vmem, vmem],
        [
            pltpu.VMEM((states, states), jnp.float32),
            pltpu.VMEM((states, states), jnp.float32),
            pltpu.VMEM((flat_rows, states), jnp.float32),
            pltpu.SemaphoreType.DMA((4,)),
            pltpu.SemaphoreType.DMA,
        ],
        hbm,
    )(gram, filtered)


def solution(mesh):
    placed = (
        P(("group", "blk"), None, None, None),
        P(("group", "blk"), None, None),
        P(("group", "blk")),
        P(("group", "blk"), None),
    )
    return jax.shard_map(
        on_device,
        mesh=mesh,
        in_specs=placed,
        out_specs=(P(("group", "blk"), None), P()),
        check_vma=False,
    )
```

```python
import functools

import jax
import jax.numpy as jnp
from jax import lax
from jax.experimental import pallas as pl
from jax.experimental.pallas import tpu as pltpu
from jax.sharding import PartitionSpec as P

precise = lax.Precision.HIGHEST
LANES = 128
SUB = 8
OUTER = 4
VMEM_LIMIT = 40 * 1024 * 1024
vmem = pl.BlockSpec(memory_space=pltpu.VMEM)
hbm = pl.BlockSpec(memory_space=pl.ANY)
smem = pl.BlockSpec(memory_space=pltpu.SMEM)


def pair_exchange(value, offset):
    count = lax.axis_size("group")
    route = []
    for low in range(offset, count + offset, 2):
        first, second = low % count, (low + 1) % count
        route += [(first, second), (second, first)]
    return lax.ppermute(value, "group", route)


def step_bits(group, level):
    levels = lax.axis_size("blk").bit_length() - 1
    return jnp.where(group % 2 == 1, levels - 1 - level, level)


def cycle_exchange(value, level):
    groups, cycle_size = lax.axis_size("group"), lax.axis_size("blk")
    levels = cycle_size.bit_length() - 1
    route = []
    for group in range(groups):
        bit = levels - 1 - level if group % 2 else level
        route += [
            (group * cycle_size + index, group * cycle_size + (index ^ 1 << bit))
            for index in range(cycle_size)
        ]
    return lax.ppermute(value, ("group", "blk"), route)


def from_partner(value, axis, flip):
    count = lax.axis_size(axis)
    return lax.ppermute(value, axis, [(index, index ^ flip) for index in range(count)])


def summed(value):
    for axis, step in (("group", 1), ("group", 2), ("blk", 1)):
        count = 2 if (axis, step) == ("group", 1) else lax.axis_size(axis)
        while step < count:
            flips = [step, 3 * step, 2 * step] if 2 * step < count else [step]
            if axis == "blk":
                flips[1:] = flips[:0:-1]
            others = [from_partner(value, axis, flip) for flip in flips]
            value = others[0] + value
            if len(others) == 3:
                value = (others[2] + others[1]) + value
            step *= len(flips) + 1
    return value


def potential_columns(potential_ref):
    return jnp.transpose(potential_ref[...])


def couple_row(index_ref, hamiltonian_ref, pieces, row):
    shard_blocks, sources, block_size, width = hamiltonian_ref.shape
    per_source = width // block_size
    total = None
    for number, piece_ref in pieces:
        source = index_ref[shard_blocks * sources * per_source + number]
        first = (row * sources + source) * per_source
        picked = jnp.concatenate(
            [piece_ref[index_ref[first + slot]] for slot in range(per_source)], axis=0
        )
        product = jnp.dot(
            hamiltonian_ref[row, source], picked, preferred_element_type=jnp.float32
        )
        if number == sources - 1:
            absent = index_ref[shard_blocks * sources * per_source + sources] != 0
            product = jnp.where(absent, 0.0, product)
        total = product if total is None else total + product
    return total


def weight_of(weights, block_size, row):
    column, part = divmod(row, LANES // block_size)
    return weights[part * block_size : (part + 1) * block_size, column : column + 1]


def own_kernel(index_ref, hamiltonian_ref, own_ref, *refs):
    terms, partial_ref = refs[:-1], refs[-1]
    shard_blocks, _, block_size, _ = hamiltonian_ref.shape
    if terms:
        weights = potential_columns(terms[0])
    for row in range(shard_blocks):
        rows = pl.ds(row * block_size, block_size)
        total = couple_row(index_ref, hamiltonian_ref, [(0, own_ref)], row)
        if terms:
            weight = weight_of(weights, block_size, row)
            total = total + (weight * terms[1][rows, :] - terms[2][rows, :])
        partial_ref[rows, :] = total


def middle_kernel(numbers, index_ref, hamiltonian_ref, partial_ref, *refs):
    pieces, sum_ref = list(zip(numbers, refs[:-1])), refs[-1]
    shard_blocks, _, block_size, _ = hamiltonian_ref.shape
    for row in range(shard_blocks):
        rows = pl.ds(row * block_size, block_size)
        sum_ref[rows, :] = partial_ref[rows, :] + couple_row(
            index_ref, hamiltonian_ref, pieces, row
        )


def first_kernel(numbers, index_ref, hamiltonian_ref, potential_ref, trial_ref, partial_ref, *refs):
    pieces, (once_ref, round_ref) = list(zip(numbers, refs)), refs[len(numbers) :]
    shard_blocks, _, block_size, _ = hamiltonian_ref.shape
    weights = potential_columns(potential_ref)
    for row in range(shard_blocks):
        rows = pl.ds(row * block_size, block_size)
        partial = partial_ref[rows, :] + weight_of(weights, block_size, row) * trial_ref[rows, :]
        once = 0.5 * (partial + couple_row(index_ref, hamiltonian_ref, pieces, row))
        once_ref[rows, :] = once
        round_ref[row] = once.astype(jnp.bfloat16)


def second_kernel(numbers, index_ref, hamiltonian_ref, partial_ref, *refs):
    pieces, (both_ref, packed_ref) = list(zip(numbers, refs)), refs[len(numbers) :]
    states = both_ref.shape[1] // 2
    shard_blocks, _, block_size, _ = hamiltonian_ref.shape
    for row in range(shard_blocks):
        rows = pl.ds(row * block_size, block_size)
        filtered = partial_ref[rows, :] + couple_row(index_ref, hamiltonian_ref, pieces, row)
        both_ref[rows, :states], both_ref[rows, states:] = two_parts(filtered)
    both = both_ref[...]
    products = lax.dot_general(
        both, both, (((0,), (0,)), ((), ())), preferred_element_type=jnp.float32
    )
    high, low = products[:states, :], products[states:, :]
    gram = high[:, :states] + (high[:, states:] + low[:, :states] + low[:, states:])
    pack(gram, packed_ref)


def two_parts(value):
    high = value.astype(jnp.bfloat16)
    return high, (value - high.astype(jnp.float32)).astype(jnp.bfloat16)


def pack(gram, packed_ref):
    size = gram.shape[0]
    half = size // 2
    row = lax.broadcasted_iota(jnp.int32, (half, size), 0)
    lane = lax.broadcasted_iota(jnp.int32, (half, size), 1)
    lower = gram[half:, :]
    packed_ref[pl.ds(0, half), :] = jnp.where(lane < row, pltpu.roll(lower, half, 1), gram[:half, :])
    diagonal = jnp.sum(jnp.where(lane == row + half, lower, 0.0), axis=0, keepdims=True)
    packed_ref[pl.ds(half, SUB), :] = jnp.broadcast_to(diagonal, (SUB, size))


def unpack(packed_ref):
    size = packed_ref.shape[1]
    half = size // 2
    row = lax.broadcasted_iota(jnp.int32, (size, size), 0)
    lane = lax.broadcasted_iota(jnp.int32, (size, size), 1)
    upper = packed_ref[pl.ds(0, half), :]
    both = jnp.concatenate([upper, pltpu.roll(upper, half, 1)], axis=0)
    held = ((row < half) & (lane > row)) | ((row >= half) & (lane >= half) & (lane < row))
    off_diagonal = jnp.where(held, both, 0.0)
    diagonal = jnp.where(row < half, both, packed_ref[pl.ds(half, 1), :])
    return off_diagonal + jnp.transpose(off_diagonal) + jnp.where(row == lane, diagonal, 0.0)


def factor(gram, upper_ref, inverse_ref):
    size = gram.shape[1]
    panels = size // SUB
    shape = (SUB, size)
    row_index = lax.broadcasted_iota(jnp.int32, shape, 0)
    lane_index = lax.broadcasted_iota(jnp.int32, shape, 1)

    def along_lanes(panel, first):
        return [jnp.broadcast_to(panel[:, first + c : first + c + 1], shape) for c in range(SUB)]

    def along_rows(panel, row):
        return jnp.broadcast_to(panel[row : row + 1, :], shape)

    def between(low, high):
        return (lane_index >= low) & (lane_index < high)

    held = [gram[k * SUB : (k + 1) * SUB, :] for k in range(panels)]
    for outer in range(0, panels, OUTER):
        end = outer + OUTER
        rows_then, rows_reduced = [], []
        block = along_lanes(held[outer], outer * SUB)
        for k in range(outer, end):
            first = k * SUB
            below = {p: along_lanes(held[p], first) for p in range(k + 1, end)}
            after = list(below[k + 1]) if k + 1 < end else None
            following = along_lanes(held[k + 1], first + SUB) if k + 1 < end else None
            right = held[k]
            left = jnp.where(
                lane_index < first, held[k], jnp.where(lane_index == row_index + first, 1.0, 0.0)
            )
            pivots = jnp.ones(shape, jnp.float32)
            reciprocals = jnp.ones(shape, jnp.float32)
            columns = [jnp.zeros(shape, jnp.float32)] * SUB
            for j in range(0, SUB, 2):
                a, b = along_rows(block[j], j), along_rows(block[j], j + 1)
                c = along_rows(block[j + 1], j + 1)
                determinant = a * c - b * b
                over = pltpu.reciprocal(determinant, approx=True)
                over_a = pltpu.reciprocal(a, approx=True)
                over_c, shift = a * over, b * over_a
                pivots = jnp.where(row_index == j, a, pivots)
                pivots = jnp.where(row_index == j + 1, determinant * over_a, pivots)
                reciprocals = jnp.where(row_index == j, over_a, reciprocals)
                reciprocals = jnp.where(row_index == j + 1, over_c, reciprocals)
                one, two = block[j] * c - block[j + 1] * b, block[j + 1] * a - block[j] * b
                upper = {
                    n: (along_rows(block[n], j), along_rows(block[n], j + 1))
                    for n in range(j + 2, SUB)
                }
                for n in upper:
                    block[n] = block[n] - over * (one * upper[n][0] + two * upper[n][1])
                if following is not None:
                    x, y = after[j], after[j + 1]
                    next_one, next_two = x * c - y * b, y * a - x * b
                    for n in range(SUB):
                        following[n] = following[n] - over * (
                            next_one * along_rows(x, n) + next_two * along_rows(y, n)
                        )
                    for n in upper:
                        after[n] = after[n] - over * (
                            next_one * upper[n][0] + next_two * upper[n][1]
                        )
                one = jnp.where(row_index > j + 1, one * over, jnp.where(row_index == j + 1, shift, 0.0))
                two = jnp.where(row_index > j + 1, two * over, 0.0)
                right = right - one * along_rows(right, j) - two * along_rows(right, j + 1)
                left = left - one * along_rows(left, j) - two * along_rows(left, j + 1)
                columns[j + 1] = jnp.where(row_index == j, shift, columns[j + 1])
                for n in upper:
                    unit = (upper[n][1] - shift * upper[n][0]) * over_c
                    columns[n] = jnp.where(row_index == j, upper[n][0] * over_a, columns[n])
                    columns[n] = jnp.where(row_index == j + 1, unit, columns[n])
            scale = lax.rsqrt(pivots)
            upper_ref[pl.ds(first, SUB), :] = jnp.where(
                lane_index >= row_index + first, right * scale, 0.0
            )
            inverse_ref[pl.ds(first, SUB), :] = left * scale
            if k + 1 < panels:
                reduced = jnp.where(lane_index >= first + SUB, right, left) * reciprocals
                for n in range(SUB - 1, 0, -1):
                    reduced = reduced - columns[n] * along_rows(reduced, n)
                rows_then.append(held[k])
                rows_reduced.append(jnp.where(between(first + SUB, end * SUB), 0.0, reduced))
                rows = [along_rows(reduced, n) for n in range(SUB)]
                for p in below:
                    total = jnp.where(between(first, first + SUB), 0.0, held[p])
                    for n in range(SUB):
                        total = total - below[p][n] * rows[n]
                    held[p] = total
            block = following
        if end < panels:
            change = lax.dot_general(
                jnp.concatenate(rows_then, axis=0), jnp.concatenate(rows_reduced, axis=0),
                (((0,), (0,)), ((), ())), precision=precise, preferred_element_type=jnp.float32,
            )
            for p in range(end, panels):
                kept = jnp.where(between(outer * SUB, end * SUB), 0.0, held[p])
                held[p] = kept - change[p * SUB : (p + 1) * SUB, :]


def factor_kernel(
    rows_total, packed_ref, both_ref, ortho_hbm, upper_hbm,
    upper_ref, inverse_ref, ortho_ref, sent, upper_sent,
):
    states = upper_ref.shape[0]
    factor(unpack(packed_ref) * (1.0 / rows_total), upper_ref, inverse_ref)
    copies = [pltpu.make_async_copy(upper_ref, upper_hbm, upper_sent)]
    copies[0].start()
    high, low = two_parts(inverse_ref[...])
    right = jnp.concatenate(
        [
            jnp.concatenate([high, high], axis=1),
            jnp.concatenate([low, jnp.zeros_like(low)], axis=1),
        ],
        axis=0,
    )
    chunks = sent.shape[0]
    per_chunk = both_ref.shape[0] // chunks
    for chunk in range(chunks):
        rows = pl.ds(chunk * per_chunk, per_chunk)
        product = lax.dot_general(
            both_ref[rows, :], right, (((1,), (1,)), ((), ())),
            preferred_element_type=jnp.float32,
        )
        ortho_ref[rows, :] = product[:, :states] + product[:, states:]
        copies.append(
            pltpu.make_async_copy(ortho_ref.at[rows, :], ortho_hbm.at[rows, :], sent.at[chunk])
        )
        copies[-1].start()
    for copy in copies:
        copy.wait()


def call(kernel, out_shape, in_specs, scratch=(), out_spec=vmem):
    return pl.pallas_call(
        kernel,
        out_shape=out_shape,
        in_specs=in_specs,
        out_specs=jax.tree.map(lambda _: out_spec, out_shape),
        scratch_shapes=list(scratch),
        compiler_params=pltpu.CompilerParams(vmem_limit_bytes=VMEM_LIMIT),
    )


def on_device(hamiltonian, block_columns, potential, trial_slab):
    shard_blocks, _, block_size, _ = hamiltonian.shape
    flat_rows, states = trial_slab.shape
    weights = potential.reshape(-1, LANES)
    rows_total = flat_rows * lax.axis_size("group") * lax.axis_size("blk")
    group, index = lax.axis_index("group"), lax.axis_index("blk")
    cycle_size = lax.axis_size("blk")
    levels = cycle_size.bit_length() - 1
    origins = [index]
    for level in range(levels):
        flip = jnp.left_shift(1, step_bits(group, level))
        origins += [jnp.bitwise_xor(origin, flip) for origin in origins]
    odd = group % 2
    origins += [cycle_size + 1 - odd, cycle_size + odd]
    origins.append((group == 0) | (group == lax.axis_size("group") - 1))
    index_array = jnp.concatenate(
        [block_columns.reshape(-1)] + [origin.reshape(1).astype(jnp.int32) for origin in origins]
    )
    last = cycle_size - 1
    ending = [last]
    middle = [cycle_size, 1] + list(range(2, last)) + [cycle_size + 1]
    flat = jax.ShapeDtypeStruct((flat_rows, states), jnp.float32)
    rounded = jax.ShapeDtypeStruct((shard_blocks, block_size, states), jnp.bfloat16)
    packed = jax.ShapeDtypeStruct((states // 2 + SUB, states), jnp.float32)
    square = jax.ShapeDtypeStruct((states, states), jnp.float32)

    def own_part(index_array, value, *terms):
        return call(own_kernel, flat, [smem] + [vmem] * (2 + len(terms)))(
            index_array, hamiltonian, value, *terms
        )

    def coupled(value, index_array, early, *terms):
        arrived = cycle_exchange(value, 0)
        pairs = [pair_exchange(value, 0), pair_exchange(value, 1)]
        if early:
            partial = own_part(index_array, value, *terms)
            later, pairs[0], partial = lax.optimization_barrier((value, pairs[0], partial))
        else:
            later, pairs[0], index_array = lax.optimization_barrier((value, pairs[0], index_array))
        others = [cycle_exchange(later, level) for level in range(1, levels)]
        pieces = [value, arrived]
        for level, other in zip(range(1, levels), others):
            pieces += [other] + [cycle_exchange(piece, level) for piece in pieces[1:]]
        pieces += pairs
        if not early:
            partial = own_part(index_array, value, *terms)
        partial = call(
            functools.partial(middle_kernel, middle), flat, [smem] + [vmem] * (2 + len(middle)),
        )(index_array, hamiltonian, partial, *[pieces[number] for number in middle])
        return [partial] + [pieces[number] for number in ending]

    parts = coupled(trial_slab.reshape(rounded.shape).astype(jnp.bfloat16), index_array, False)
    once, once_round = call(
        functools.partial(first_kernel, ending), (flat, rounded), [smem] + [vmem] * (4 + len(ending))
    )(index_array, hamiltonian, weights, trial_slab, *parts)
    parts = coupled(once_round, index_array, True, weights, once, trial_slab)
    both = jax.ShapeDtypeStruct((flat_rows, 2 * states), jnp.bfloat16)
    filtered, gram = call(
        functools.partial(second_kernel, ending), (both, packed), [smem] + [vmem] * (2 + len(ending))
    )(index_array, hamiltonian, *parts)
    gram = summed(gram)
    return call(
        functools.partial(factor_kernel, rows_total),
        (flat, square),
        [vmem, vmem],
        [
            pltpu.VMEM((states, states), jnp.float32),
            pltpu.VMEM((states, states), jnp.float32),
            pltpu.VMEM((flat_rows, states), jnp.float32),
            pltpu.SemaphoreType.DMA((4,)),
            pltpu.SemaphoreType.DMA,
        ],
        hbm,
    )(gram, filtered)


def solution(mesh):
    placed = (
        P(("group", "blk"), None, None, None),
        P(("group", "blk"), None, None),
        P(("group", "blk")),
        P(("group", "blk"), None),
    )
    return jax.shard_map(
        on_device,
        mesh=mesh,
        in_specs=placed,
        out_specs=(P(("group", "blk"), None), P()),
        check_vma=False,
    )
```

```python
import functools

import jax
import jax.numpy as jnp
from jax import lax
from jax.experimental import pallas as pl
from jax.experimental.pallas import tpu as pltpu
from jax.sharding import PartitionSpec as P

precise = lax.Precision.HIGHEST
LANES = 128
SUB = 8
OUTER = 4
VMEM_LIMIT = 40 * 1024 * 1024
vmem = pl.BlockSpec(memory_space=pltpu.VMEM)
hbm = pl.BlockSpec(memory_space=pl.ANY)
smem = pl.BlockSpec(memory_space=pltpu.SMEM)


def pair_exchange(value, offset):
    count = lax.axis_size("group")
    route = []
    for low in range(offset, count - 1, 2):
        route += [(low, low + 1), (low + 1, low)]
    return lax.ppermute(value, "group", route)


def step_bits(group, level):
    levels = lax.axis_size("blk").bit_length() - 1
    return jnp.where(group % 2 == 1, levels - 1 - level, level)


def cycle_exchange(value, level):
    groups, cycle_size = lax.axis_size("group"), lax.axis_size("blk")
    levels = cycle_size.bit_length() - 1
    route = []
    for group in range(groups):
        bit = levels - 1 - level if group % 2 else level
        route += [
            (group * cycle_size + index, group * cycle_size + (index ^ 1 << bit))
            for index in range(cycle_size)
        ]
    return lax.ppermute(value, ("group", "blk"), route)


def from_partner(value, axis, flip):
    count = lax.axis_size(axis)
    return lax.ppermute(value, axis, [(index, index ^ flip) for index in range(count)])


def summed(value):
    for axis, step in (("group", 1), ("group", 2), ("blk", 1)):
        count = 2 if (axis, step) == ("group", 1) else lax.axis_size(axis)
        while step < count:
            flips = [step, 3 * step, 2 * step] if 2 * step < count else [step]
            if axis == "blk":
                flips[1:] = flips[:0:-1]
            others = [from_partner(value, axis, flip) for flip in flips]
            value = others[0] + value
            if len(others) == 3:
                value = (others[2] + others[1]) + value
            step *= len(flips) + 1
    return value


def potential_columns(potential_ref):
    return jnp.transpose(potential_ref[...])


def couple_row(index_ref, hamiltonian_ref, pieces, row):
    shard_blocks, sources, block_size, width = hamiltonian_ref.shape
    per_source = width // block_size
    total = None
    for number, piece_ref in pieces:
        source = index_ref[shard_blocks * sources * per_source + number]
        first = (row * sources + source) * per_source
        picked = jnp.concatenate(
            [piece_ref[index_ref[first + slot]] for slot in range(per_source)], axis=0
        )
        product = jnp.dot(
            hamiltonian_ref[row, source], picked, preferred_element_type=jnp.float32
        )
        total = product if total is None else total + product
    return total


def weight_of(weights, block_size, row):
    column, part = divmod(row, LANES // block_size)
    return weights[part * block_size : (part + 1) * block_size, column : column + 1]


def own_kernel(index_ref, hamiltonian_ref, own_ref, *refs):
    terms, partial_ref = refs[:-1], refs[-1]
    shard_blocks, _, block_size, _ = hamiltonian_ref.shape
    if terms:
        weights = potential_columns(terms[0])
    for row in range(shard_blocks):
        rows = pl.ds(row * block_size, block_size)
        total = couple_row(index_ref, hamiltonian_ref, [(0, own_ref)], row)
        if terms:
            weight = weight_of(weights, block_size, row)
            total = total + (weight * terms[1][rows, :] - terms[2][rows, :])
        partial_ref[rows, :] = total


def middle_kernel(numbers, index_ref, hamiltonian_ref, partial_ref, *refs):
    pieces, sum_ref = list(zip(numbers, refs[:-1])), refs[-1]
    shard_blocks, _, block_size, _ = hamiltonian_ref.shape
    for row in range(shard_blocks):
        rows = pl.ds(row * block_size, block_size)
        sum_ref[rows, :] = partial_ref[rows, :] + couple_row(
            index_ref, hamiltonian_ref, pieces, row
        )


def first_kernel(numbers, index_ref, hamiltonian_ref, potential_ref, trial_ref, partial_ref, *refs):
    pieces, (once_ref, round_ref) = list(zip(numbers, refs)), refs[len(numbers) :]
    shard_blocks, _, block_size, _ = hamiltonian_ref.shape
    weights = potential_columns(potential_ref)
    for row in range(shard_blocks):
        rows = pl.ds(row * block_size, block_size)
        partial = partial_ref[rows, :] + weight_of(weights, block_size, row) * trial_ref[rows, :]
        once = 0.5 * (partial + couple_row(index_ref, hamiltonian_ref, pieces, row))
        once_ref[rows, :] = once
        round_ref[row] = once.astype(jnp.bfloat16)


def second_kernel(numbers, index_ref, hamiltonian_ref, partial_ref, *refs):
    pieces, (both_ref, packed_ref) = list(zip(numbers, refs)), refs[len(numbers) :]
    states = both_ref.shape[1] // 2
    shard_blocks, _, block_size, _ = hamiltonian_ref.shape
    for row in range(shard_blocks):
        rows = pl.ds(row * block_size, block_size)
        filtered = partial_ref[rows, :] + couple_row(index_ref, hamiltonian_ref, pieces, row)
        both_ref[rows, :states], both_ref[rows, states:] = two_parts(filtered)
    both = both_ref[...]
    products = lax.dot_general(
        both, both, (((0,), (0,)), ((), ())), preferred_element_type=jnp.float32
    )
    high, low = products[:states, :], products[states:, :]
    gram = high[:, :states] + (high[:, states:] + low[:, :states] + low[:, states:])
    pack(gram, packed_ref)


def two_parts(value):
    high = value.astype(jnp.bfloat16)
    return high, (value - high.astype(jnp.float32)).astype(jnp.bfloat16)


def pack(gram, packed_ref):
    size = gram.shape[0]
    half = size // 2
    row = lax.broadcasted_iota(jnp.int32, (half, size), 0)
    lane = lax.broadcasted_iota(jnp.int32, (half, size), 1)
    lower = gram[half:, :]
    packed_ref[pl.ds(0, half), :] = jnp.where(lane < row, pltpu.roll(lower, half, 1), gram[:half, :])
    diagonal = jnp.sum(jnp.where(lane == row + half, lower, 0.0), axis=0, keepdims=True)
    packed_ref[pl.ds(half, SUB), :] = jnp.broadcast_to(diagonal, (SUB, size))


def unpack(packed_ref):
    size = packed_ref.shape[1]
    half = size // 2
    row = lax.broadcasted_iota(jnp.int32, (size, size), 0)
    lane = lax.broadcasted_iota(jnp.int32, (size, size), 1)
    upper = packed_ref[pl.ds(0, half), :]
    both = jnp.concatenate([upper, pltpu.roll(upper, half, 1)], axis=0)
    held = ((row < half) & (lane > row)) | ((row >= half) & (lane >= half) & (lane < row))
    off_diagonal = jnp.where(held, both, 0.0)
    diagonal = jnp.where(row < half, both, packed_ref[pl.ds(half, 1), :])
    return off_diagonal + jnp.transpose(off_diagonal) + jnp.where(row == lane, diagonal, 0.0)


def factor(gram, upper_ref, inverse_ref):
    size = gram.shape[1]
    panels = size // SUB
    shape = (SUB, size)
    row_index = lax.broadcasted_iota(jnp.int32, shape, 0)
    lane_index = lax.broadcasted_iota(jnp.int32, shape, 1)

    def along_lanes(panel, first):
        return [jnp.broadcast_to(panel[:, first + c : first + c + 1], shape) for c in range(SUB)]

    def along_rows(panel, row):
        return jnp.broadcast_to(panel[row : row + 1, :], shape)

    def between(low, high):
        return (lane_index >= low) & (lane_index < high)

    held = [gram[k * SUB : (k + 1) * SUB, :] for k in range(panels)]
    for outer in range(0, panels, OUTER):
        end = outer + OUTER
        rows_then, rows_reduced = [], []
        block = along_lanes(held[outer], outer * SUB)
        for k in range(outer, end):
            first = k * SUB
            below = {p: along_lanes(held[p], first) for p in range(k + 1, end)}
            after = list(below[k + 1]) if k + 1 < end else None
            following = along_lanes(held[k + 1], first + SUB) if k + 1 < end else None
            right = held[k]
            left = jnp.where(
                lane_index < first, held[k], jnp.where(lane_index == row_index + first, 1.0, 0.0)
            )
            pivots = jnp.ones(shape, jnp.float32)
            reciprocals = jnp.ones(shape, jnp.float32)
            columns = [jnp.zeros(shape, jnp.float32)] * SUB
            for j in range(0, SUB, 2):
                a, b = along_rows(block[j], j), along_rows(block[j], j + 1)
                c = along_rows(block[j + 1], j + 1)
                determinant = a * c - b * b
                over = pltpu.reciprocal(determinant, approx=True)
                over_a = pltpu.reciprocal(a, approx=True)
                over_c, shift = a * over, b * over_a
                pivots = jnp.where(row_index == j, a, pivots)
                pivots = jnp.where(row_index == j + 1, determinant * over_a, pivots)
                reciprocals = jnp.where(row_index == j, over_a, reciprocals)
                reciprocals = jnp.where(row_index == j + 1, over_c, reciprocals)
                one, two = block[j] * c - block[j + 1] * b, block[j + 1] * a - block[j] * b
                upper = {
                    n: (along_rows(block[n], j), along_rows(block[n], j + 1))
                    for n in range(j + 2, SUB)
                }
                for n in upper:
                    block[n] = block[n] - over * (one * upper[n][0] + two * upper[n][1])
                if following is not None:
                    x, y = after[j], after[j + 1]
                    next_one, next_two = x * c - y * b, y * a - x * b
                    for n in range(SUB):
                        following[n] = following[n] - over * (
                            next_one * along_rows(x, n) + next_two * along_rows(y, n)
                        )
                    for n in upper:
                        after[n] = after[n] - over * (
                            next_one * upper[n][0] + next_two * upper[n][1]
                        )
                one = jnp.where(row_index > j + 1, one * over, jnp.where(row_index == j + 1, shift, 0.0))
                two = jnp.where(row_index > j + 1, two * over, 0.0)
                right = right - one * along_rows(right, j) - two * along_rows(right, j + 1)
                left = left - one * along_rows(left, j) - two * along_rows(left, j + 1)
                columns[j + 1] = jnp.where(row_index == j, shift, columns[j + 1])
                for n in upper:
                    unit = (upper[n][1] - shift * upper[n][0]) * over_c
                    columns[n] = jnp.where(row_index == j, upper[n][0] * over_a, columns[n])
                    columns[n] = jnp.where(row_index == j + 1, unit, columns[n])
            scale = lax.rsqrt(pivots)
            upper_ref[pl.ds(first, SUB), :] = jnp.where(
                lane_index >= row_index + first, right * scale, 0.0
            )
            inverse_ref[pl.ds(first, SUB), :] = left * scale
            if k + 1 < panels:
                reduced = jnp.where(lane_index >= first + SUB, right, left) * reciprocals
                for n in range(SUB - 1, 0, -1):
                    reduced = reduced - columns[n] * along_rows(reduced, n)
                rows_then.append(held[k])
                rows_reduced.append(jnp.where(between(first + SUB, end * SUB), 0.0, reduced))
                rows = [along_rows(reduced, n) for n in range(SUB)]
                for p in below:
                    total = jnp.where(between(first, first + SUB), 0.0, held[p])
                    for n in range(SUB):
                        total = total - below[p][n] * rows[n]
                    held[p] = total
            block = following
        if end < panels:
            change = lax.dot_general(
                jnp.concatenate(rows_then, axis=0), jnp.concatenate(rows_reduced, axis=0),
                (((0,), (0,)), ((), ())), precision=precise, preferred_element_type=jnp.float32,
            )
            for p in range(end, panels):
                kept = jnp.where(between(outer * SUB, end * SUB), 0.0, held[p])
                held[p] = kept - change[p * SUB : (p + 1) * SUB, :]


def factor_kernel(
    rows_total, packed_ref, both_ref, ortho_hbm, upper_hbm,
    upper_ref, inverse_ref, ortho_ref, sent, upper_sent,
):
    states = upper_ref.shape[0]
    factor(unpack(packed_ref) * (1.0 / rows_total), upper_ref, inverse_ref)
    copies = [pltpu.make_async_copy(upper_ref, upper_hbm, upper_sent)]
    copies[0].start()
    high, low = two_parts(inverse_ref[...])
    right = jnp.concatenate(
        [
            jnp.concatenate([high, high], axis=1),
            jnp.concatenate([low, jnp.zeros_like(low)], axis=1),
        ],
        axis=0,
    )
    chunks = sent.shape[0]
    per_chunk = both_ref.shape[0] // chunks
    for chunk in range(chunks):
        rows = pl.ds(chunk * per_chunk, per_chunk)
        product = lax.dot_general(
            both_ref[rows, :], right, (((1,), (1,)), ((), ())),
            preferred_element_type=jnp.float32,
        )
        ortho_ref[rows, :] = product[:, :states] + product[:, states:]
        copies.append(
            pltpu.make_async_copy(ortho_ref.at[rows, :], ortho_hbm.at[rows, :], sent.at[chunk])
        )
        copies[-1].start()
    for copy in copies:
        copy.wait()


def call(kernel, out_shape, in_specs, scratch=(), out_spec=vmem):
    return pl.pallas_call(
        kernel,
        out_shape=out_shape,
        in_specs=in_specs,
        out_specs=jax.tree.map(lambda _: out_spec, out_shape),
        scratch_shapes=list(scratch),
        compiler_params=pltpu.CompilerParams(vmem_limit_bytes=VMEM_LIMIT),
    )


def on_device(hamiltonian, block_columns, potential, trial_slab):
    shard_blocks, _, block_size, _ = hamiltonian.shape
    flat_rows, states = trial_slab.shape
    weights = potential.reshape(-1, LANES)
    rows_total = flat_rows * lax.axis_size("group") * lax.axis_size("blk")
    group, index = lax.axis_index("group"), lax.axis_index("blk")
    cycle_size = lax.axis_size("blk")
    levels = cycle_size.bit_length() - 1
    origins = [index]
    for level in range(levels):
        flip = jnp.left_shift(1, step_bits(group, level))
        origins += [jnp.bitwise_xor(origin, flip) for origin in origins]
    odd = group % 2
    origins += [cycle_size + 1 - odd, cycle_size + odd]
    index_array = jnp.concatenate(
        [block_columns.reshape(-1)] + [origin.reshape(1).astype(jnp.int32) for origin in origins]
    )
    last = cycle_size - 1
    ending = [last]
    middle = [1, cycle_size + 1, cycle_size] + list(range(2, last))
    flat = jax.ShapeDtypeStruct((flat_rows, states), jnp.float32)
    rounded = jax.ShapeDtypeStruct((shard_blocks, block_size, states), jnp.bfloat16)
    packed = jax.ShapeDtypeStruct((states // 2 + SUB, states), jnp.float32)
    square = jax.ShapeDtypeStruct((states, states), jnp.float32)

    def own_part(index_array, value, *terms):
        return call(own_kernel, flat, [smem] + [vmem] * (2 + len(terms)))(
            index_array, hamiltonian, value, *terms
        )

    def coupled(value, index_array, early, *terms):
        arrived = cycle_exchange(value, 0)
        pairs = [pair_exchange(value, 0), pair_exchange(value, 1)]
        others = [cycle_exchange(value, level) for level in range(1, levels)]
        if early:
            partial = own_part(index_array, value, *terms)
            arrived, partial = lax.optimization_barrier((arrived, partial))
        pieces = [value, arrived]
        for level, other in zip(range(1, levels), others):
            pieces += [other] + [cycle_exchange(piece, level) for piece in pieces[1:]]
        pieces += pairs
        if not early:
            partial = own_part(index_array, value, *terms)
        partial = call(
            functools.partial(middle_kernel, middle), flat, [smem] + [vmem] * (2 + len(middle)),
        )(index_array, hamiltonian, partial, *[pieces[number] for number in middle])
        return [partial] + [pieces[number] for number in ending]

    parts = coupled(trial_slab.reshape(rounded.shape).astype(jnp.bfloat16), index_array, False)
    once, once_round = call(
        functools.partial(first_kernel, ending), (flat, rounded), [smem] + [vmem] * (4 + len(ending))
    )(index_array, hamiltonian, weights, trial_slab, *parts)
    parts = coupled(once_round, index_array, True, weights, once, trial_slab)
    both = jax.ShapeDtypeStruct((flat_rows, 2 * states), jnp.bfloat16)
    filtered, gram = call(
        functools.partial(second_kernel, ending), (both, packed), [smem] + [vmem] * (2 + len(ending))
    )(index_array, hamiltonian, *parts)
    gram = summed(gram)
    return call(
        functools.partial(factor_kernel, rows_total),
        (flat, square),
        [vmem, vmem],
        [
            pltpu.VMEM((states, states), jnp.float32),
            pltpu.VMEM((states, states), jnp.float32),
            pltpu.VMEM((flat_rows, states), jnp.float32),
            pltpu.SemaphoreType.DMA((4,)),
            pltpu.SemaphoreType.DMA,
        ],
        hbm,
    )(gram, filtered)


def solution(mesh):
    placed = (
        P(("group", "blk"), None, None, None),
        P(("group", "blk"), None, None),
        P(("group", "blk")),
        P(("group", "blk"), None),
    )
    return jax.shard_map(
        on_device,
        mesh=mesh,
        in_specs=placed,
        out_specs=(P(("group", "blk"), None), P()),
        check_vma=False,
    )
```
